32 devices in a mesh: gx: 4 (over y, x), gy: 4 (over z), gz: 2 (over core).
Axes of the slice: x: 2, y: 2, z: 4, core: 2. Of those that a mesh axis runs over, the one named last changes fastest.
Arguments:
- u_now: float32 [3, 64, 64, 256], P(None, 'gx', 'gy', 'gz'), may hold values from -6 to 6
- u_prev: float32 [3, 64, 64, 256], P(None, 'gx', 'gy', 'gz'), may hold values from -6 to 6
- panels: bfloat16 [4, 2, 64, 48, 256], P('gx', 'gz', 'gy'), may hold values from -6 to 6
- panel_owner: int32 [4, 2, 64, 1], P('gx', 'gz'), may hold values from 0 to 3; in each aligned block of 16 rows (0 to 15, 16 to 31, ..., all dimensions but the last counted through in order) at most 8 rows name the same one
- panel_block: int32 [4, 2, 64], P('gx', 'gz'), may hold values from 0 to 2047
- coupling: float32 [3, 16, 16], replicated, may hold values from -1.5 to 1.5
- layer_depth: int32 [256], P('gz'), may hold values from 0 to 7, never falling along the last dimension, each value on 1 to 64 neighbouring positions
- layer_speed: float32 [8], replicated, may hold values from 0.04 to 0.3
- lateral: float32 [64, 64, 256], P('gx', 'gy', 'gz'), may hold values from 0.5 to 1
Outputs:
- u_final: float32 [3, 64, 64, 256], P(None, 'gx', 'gy', 'gz')
- u_before: float32 [3, 64, 64, 256], P(None, 'gx', 'gy', 'gz')
The draws below stay inside these ranges and needn't reach their ends.
Inputs may be any that keep to these rules, and one draw needn't show every extreme that they name: `panel_owner`: among the 16 panels of one device (an aligned block of rows) at most 8 have the same owner; in each draw some owner receives exactly 8 from some device. `layer_depth`: layers never decrease with depth; each layer spans 1 to 64 depths.
All inputs are finite; a program needn't handle non-finite values.
Results may differ from the reference program's by a relative error of at most 0.00038.
Values may be sent and summed in bfloat16 or wider, within the bound.
No kernel may reach another device: no remote copies, remote signals or barrier semaphores. Data moves between devices by JAX's collectives and lax.ppermute only.
A program may use at most 64 MiB of HBM per device.

```python
import math
import jax
import jax.numpy as jnp
import numpy as np
from jax import lax

CX = 16
CY = 16
CZ = 128
PB = 16
NT = 256
PD = 16
NSTEP = 4
NL = 8
CAP = 8
NZB = 8
NBLK = 2048
NX = 64
NY = 64
NZ = 256
N_GX = 4
N_GY = 4
N_GZ = 2


def set_ends(values, key, smallest, top_value):
    spot = [jax.random.randint(jax.random.fold_in(key, axis), (), 0, length) for axis, length in enumerate(values.shape)]
    main_axis = values.shape.index(max(values.shape))
    next_to = spot[:main_axis] + [(spot[main_axis] + 1) % values.shape[main_axis]] + spot[main_axis + 1:]
    return values.at[tuple(spot)].set(smallest).at[tuple(next_to)].set(top_value)


def shard_levels(stream_key, extent, split, least, top_value):
    level, own = 1.0, jax.random.fold_in(stream_key, 6)
    for axis_at, shards_of in split:
        steps = jnp.exp(jax.random.uniform(jax.random.fold_in(own, axis_at), (shards_of,), jnp.float32, least / len(split), top_value / len(split)))
        level = level * jnp.repeat(steps, extent[axis_at] // shards_of).reshape([-1 if axis == axis_at else 1 for axis in range(len(extent))])
    return level


def profile(number_of, total, limit, slope):
    portions = [(1 << 20) // math.isqrt(standing ** slope) + 1 for standing in range(2, number_of + 1)]
    rest, given = total - limit - (number_of - 1), [1] * (number_of - 1)
    while rest > 0:
        movable = [i for i in range(number_of - 1) if given[i] < limit]
        whole, remaining = sum([portions[i] for i in movable]), rest
        for i in movable:
            more = min(limit - given[i], max(1, remaining * portions[i] // whole), rest)
            given[i] = given[i] + more
            rest = rest - more
    return np.array([limit] + given)


def uneven(own_key, number_of, total, limit, skew):
    if number_of == 2:
        one = jax.random.randint(own_key, (), max(1, total - limit), min(limit, total - 1) + 1)
        return jnp.stack([one, total - one])
    lengths = jnp.asarray(profile(number_of, total, limit, skew), jnp.int32)
    couples = (number_of - 1) // 2
    giver, receiver = lengths[1:1 + 2 * couples:2], lengths[2:2 + 2 * couples:2]
    margin = jnp.minimum(giver - 1, limit - receiver)
    shifted = jax.random.randint(jax.random.fold_in(own_key, 1), (couples,), 0, 1 << 20) % (margin + 1)
    lengths = lengths.at[1:1 + 2 * couples:2].set(giver - shifted).at[2:2 + 2 * couples:2].set(receiver + shifted)
    return lengths[jax.random.permutation(jax.random.fold_in(own_key, 2), number_of)]


def assign_block(key, own, number, rows, count, top, bound, lean):
    order = jax.random.permutation(key, count)
    packed, ordinary = load_shares(count, rows * top, bound, lean, True), load_shares(count, rows * top, bound, lean, False)
    places = jnp.arange(count)

    def named(lengths, turn):
        used = int((lengths > 0).sum())
        fixed = max(1, used // 4)
        shifted = fixed + (places - fixed + turn * (used - fixed)) % max(1, count - fixed)
        return jnp.zeros((count,), jnp.int32).at[order[jnp.where(places < fixed, places, shifted)]].set(jnp.asarray(lengths, jnp.int32))

    lengths = jnp.where(number % 4 == 0, named(packed, number // 4), named(ordinary, number - number // 4 - 1))
    mixed = jax.random.permutation(jax.random.fold_in(own, 3), count)
    giver, taker = mixed[0:count // 2 * 2:2], mixed[1:count // 2 * 2:2]
    margin = jnp.minimum(lengths[giver] - 1, bound - lengths[taker]) // 2
    margin = jnp.where((giver == order[0]) | (taker == order[0]) | (lengths[taker] == 0), 0, jnp.maximum(margin, 0))
    shifted = jax.random.randint(jax.random.fold_in(own, 4), (count // 2,), 0, 1 << 20) % (margin + 1)
    lengths = lengths.at[giver].add(-shifted).at[taker].add(shifted)
    labels = jnp.searchsorted(jnp.cumsum(lengths), jnp.arange(rows * top), side="right").astype(jnp.int32)
    table = labels.reshape(top, rows).T
    table = table[jax.random.permutation(jax.random.fold_in(own, 1), rows)]
    turn = jax.random.randint(jax.random.fold_in(own, 2), (rows, 1), 0, top)
    return jnp.take_along_axis(table, (jnp.arange(top)[None, :] + turn) % top, axis=1)


def load_shares(amount, total, reach, slope, full):
    loads = [(1 << 20) // math.isqrt(grade ** slope) + 1 for grade in range(1, amount + 1)]
    largest = reach if full else min(reach, max(-(-total // amount), total * loads[0] // sum(loads)))
    least = 1 if total - largest >= amount - 1 else 0
    counts, surplus = [largest] + [least] * (amount - 1), total - largest - least * (amount - 1)
    while surplus > 0:
        candidates = [i for i in range(1, amount) if counts[i] < largest] or [i for i in range(1, amount) if counts[i] < reach]
        pool, budget = sum([loads[i] for i in candidates]), surplus
        for i in candidates:
            more = min(reach - counts[i], max(1, budget * loads[i] // pool), surplus)
            counts[i] = counts[i] + more
            surplus = surplus - more
    return np.array(counts)


def centred(key, extent, spread, most, shards=(), kind=jnp.bfloat16):
    values = jax.random.normal(key, extent, jnp.float32) * spread
    if len(shards) > 0:
        values = shard_levels(key, extent, shards, -0.22, 0.18) * values
    return jnp.clip(values, min=-most, max=most).astype(kind)


def setup_inputs(seed: int = 0) -> dict:
    arg_keys = jax.random.split(jax.random.key(seed), 10)
    u_now = centred(arg_keys[0], (3, NX, NY, NZ), 1.0, 6.0, ((1, 4), (2, 4), (3, 2)), jnp.float32)
    u_prev = centred(arg_keys[1], (3, NX, NY, NZ), 1.0, 6.0, ((1, 4), (2, 4), (3, 2)), jnp.float32)
    panels = centred(arg_keys[2], (N_GX, N_GZ, N_GY * PD, 3 * PB, NT), 1.0, 6.0, ((0, 4), (1, 2), (2, 4)))
    panel_owner_keys = jax.random.split(jax.random.fold_in(arg_keys[3], 1), N_GX * N_GZ * (N_GY * PD) // PD)
    panel_owner_turns = jax.random.permutation(jax.random.fold_in(arg_keys[3], 3), N_GX * N_GZ * (N_GY * PD) // PD)
    panel_owner = jax.vmap(lambda own, number: assign_block(jax.random.fold_in(arg_keys[3], 2), own, number, PD, N_GY, 1, CAP, 2))(panel_owner_keys, panel_owner_turns).reshape((N_GX, N_GZ, N_GY * PD, 1))
    panel_block = set_ends(jax.random.randint(arg_keys[4], (N_GX, N_GZ, N_GY * PD), 0, NBLK), jax.random.fold_in(arg_keys[4], 1), 0, NBLK - 1).astype(jnp.int32)
    coupling = centred(arg_keys[5], (3, PB, PB), PB ** -0.5, 1.5, (), jnp.float32)
    layer_depth = jnp.searchsorted(jnp.cumsum(uneven(arg_keys[6], NL, NZ, NZ // 4, 0)), jnp.arange(NZ), side="right").astype(jnp.int32)
    layer_speed = jnp.clip(jnp.exp(jax.random.uniform(arg_keys[7], (NL,), jnp.float32, math.log(0.04), math.log(0.3))), 0.04, 0.3)
    lateral = jnp.clip(0.5 + 0.5 * jax.random.uniform(arg_keys[8], (NX, NY, NZ), jnp.float32) ** shard_levels(arg_keys[8], (NX, NY, NZ), ((0, 4), (1, 4), (2, 2)), -0.2, 0.2), 0.5, 1.0)
    return dict(u_now=u_now, u_prev=u_prev, panels=panels, panel_owner=panel_owner, panel_block=panel_block, coupling=coupling, layer_depth=layer_depth, layer_speed=layer_speed, lateral=lateral)


def wave_table():
    half = NT // 2
    freq = 2.0 * jnp.pi * (jnp.arange(half, dtype=jnp.float32) + 0.5) / NT
    times = 37.0 + jnp.arange(NSTEP, dtype=jnp.float32)
    phase = freq[:, None] * times[None, :]
    table = jnp.concatenate([jnp.cos(phase), jnp.sin(phase)], axis=0) / jnp.sqrt(jnp.float32(half))
    return table.astype(jnp.bfloat16)

def laplace(field):
    padded = jnp.pad(field, ((0, 0), (1, 1), (1, 1), (1, 1)))
    beside = padded[:, 2:, 1:-1, 1:-1] + padded[:, :-2, 1:-1, 1:-1]
    beside = beside + padded[:, 1:-1, 2:, 1:-1] + padded[:, 1:-1, :-2, 1:-1]
    beside = beside + padded[:, 1:-1, 1:-1, 2:] + padded[:, 1:-1, 1:-1, :-2]
    return beside - 6.0 * field

def reference(u_now, u_prev, panels, panel_owner, panel_block, coupling, layer_depth, layer_speed, lateral):
    table = wave_table()
    count = N_GX * N_GZ * N_GY * PD
    free = jnp.dot(panels.reshape(-1, NT), table, preferred_element_type=jnp.float32)
    free = free.reshape(count, 3, PB, NSTEP)
    force = jnp.einsum('cij,pcjn->pcin', coupling, free, precision=lax.Precision.HIGHEST)
    owner = panel_owner[..., 0]
    shape = owner.shape
    first = lax.broadcasted_iota(jnp.int32, shape, 0)
    depth = lax.broadcasted_iota(jnp.int32, shape, 1)
    xpos = (first * CX + panel_block // (CY * NZB)).reshape(-1).astype(jnp.int32)
    ypos = (owner * CY + panel_block // NZB % CY).reshape(-1).astype(jnp.int32)
    zbase = (depth * CZ + panel_block % NZB * PB).reshape(-1).astype(jnp.int32)
    zpos = zbase[:, None] + jnp.arange(PB, dtype=jnp.int32)[None, :]
    rate = lateral * layer_speed[layer_depth][None, None, :]
    for step in range(NSTEP):
        values = jnp.transpose(force[:, :, :, step], (1, 0, 2))
        drive = jnp.zeros((3, NX, NY, NZ), jnp.float32).at[:, xpos[:, None], ypos[:, None], zpos].add(values)
        u_next = 2.0 * u_now - u_prev + rate[None] * laplace(u_now) + drive
        u_prev = u_now
        u_now = u_next
    return (u_now, u_prev)
```

```python
import functools

import jax
import jax.numpy as jnp
import ml_dtypes
import numpy as np
from jax import lax
from jax.experimental import pallas as pl
from jax.experimental.pallas import tpu as pltpu
from jax.sharding import PartitionSpec as P

NSTEP = 4
HALO = 8
F32 = jnp.float32
BF16 = jnp.bfloat16


def wave_table(count, per_step):
    half = count // 2
    freq = np.float32(2.0 * np.pi) * (np.arange(half, dtype=np.float32) + np.float32(0.5)) / np.float32(count)
    times = np.float32(37.0) + np.arange(NSTEP, dtype=np.float32)
    phase = freq[:, None] * times[None, :]
    table = np.concatenate([np.cos(phase), np.sin(phase)], axis=0) / np.sqrt(np.float32(half))
    wide = np.repeat(table.astype(ml_dtypes.bfloat16), per_step, axis=1)
    return np.pad(wide, ((0, 0), (0, -wide.shape[1] % 128)))


def shift_of(size):
    assert size & (size - 1) == 0
    return size.bit_length() - 1


def iota(shape, dim):
    return lax.broadcasted_iota(jnp.int32, shape, dim)


def spin(value, amount, axis):
    return pltpu.roll(value, amount % value.shape[axis], axis)


def across(z0, z1):
    lanes = z0.shape[-1]
    lane = iota(z0.shape, z0.ndim - 1)
    first, last = lane == 0, lane == lanes - 1
    ax = z0.ndim - 1
    down0, down1 = spin(z0, 1, ax), spin(z1, 1, ax)
    up0, up1 = spin(z0, -1, ax), spin(z1, -1, ax)
    sum0 = jnp.where(first, 0.0, down0) + jnp.where(last, up1, up0)
    sum1 = jnp.where(first, down0, down1) + jnp.where(last, 0.0, up1)
    return sum0, sum1


def inplane(z0, z1):
    ax = z0.ndim - 2
    sum0, sum1 = across(z0, z1)
    sum0 = sum0 + (spin(z0, 1, ax) + spin(z0, -1, ax)) - 6.0 * z0
    sum1 = sum1 + (spin(z1, 1, ax) + spin(z1, -1, ax)) - 6.0 * z1
    return sum0, sum1


def speed_row(ints_ref, speed_ref):
    depth = ints_ref[0:1, :]
    row = jnp.zeros(depth.shape, F32)
    for layer in range(speed_ref.shape[0]):
        row = jnp.where(depth == layer, speed_ref[layer], row)
    return row


def force_kernel(panels_ref, coupling_ref, table_ref, force_ref):
    count, rows, spectral = panels_ref.shape
    comps, block = 3, rows // 3
    lanes = table_ref.shape[1]
    free = jnp.dot(
        panels_ref[...].reshape(count * rows, spectral), table_ref[...], preferred_element_type=F32
    )
    weights = coupling_ref[...].reshape(rows, block)
    stacked = jnp.concatenate([weights] * NSTEP + [jnp.zeros((lanes - NSTEP * rows, block), F32)], axis=0)
    pick = ((iota((rows, block), 0) & (block - 1)) == iota((rows, block), 1)).astype(F32)
    spread = lax.dot_general(
        pick, stacked, (((1,), (1,)), ((), ())), precision=lax.Precision.HIGHEST, preferred_element_type=F32
    )
    comp_row = iota((rows, lanes), 0) >> shift_of(block)
    comp_lane = iota((rows, lanes), 1) >> shift_of(block)
    same = comp_lane == comp_row
    for step in range(1, NSTEP):
        same = same | (comp_lane == comp_row + step * comps)
    spread = jnp.where(same, spread, 0.0)
    force_ref[...] = jnp.sum(free.reshape(count, rows, lanes) * spread[None], axis=1)


def pack_kernel(
    scal_ref, speed_ref, un_ref, up_ref, lat_ref, uno_ref, upo_ref, lato_ref, ints_ref, intso_ref,
    force_ref, forceo_ref, out_ref, pair_ref,
):
    mine = scal_ref[2]
    high = lax.rem(scal_ref[1] + mine, 2) == 0
    comps, size_x, size_y, size_z = un_ref.shape
    tiles = comps * size_x
    shape = (size_x, HALO, size_z)
    sub = iota(shape, 1)

    def fill(side):
        base = size_y - HALO if side else 0
        for z_at, un, up, lat, ints in (
            (mine, un_ref, up_ref, lat_ref, ints_ref),
            (1 - mine, uno_ref, upo_ref, lato_ref, intso_ref),
        ):
            rate = lat[:, base:base + HALO, :] * speed_row(ints, speed_ref)[None]
            for c in range(comps):
                now = un[c, :, base:base + HALO, :]
                old = spin(up[c, :, base:base + HALO, :], HALO // 2, 1)
                keep = sub >= HALO // 2 if side else sub < HALO // 2
                row = HALO - 1 - c if side else c
                tile = jnp.where(keep, now, old)
                tile = jnp.where(sub == (0 if side else HALO - 1), rate[:, row:row + 1, :], tile)
                out_ref[pl.ds(z_at * tiles + c * size_x, size_x)] = tile

    @pl.when(high)
    def _():
        fill(True)

    @pl.when(jnp.logical_not(high))
    def _():
        fill(False)

    count, lanes = force_ref.shape
    for z_at, force in ((mine, force_ref), (1 - mine, forceo_ref)):
        pair_ref[z_at] = force[...]
        for part in range(lanes // size_z):
            for piece in range(count // HALO):
                at = 2 * tiles + (z_at * (lanes // size_z) + part) * (count // HALO) + piece
                out_ref[at] = force[piece * HALO:(piece + 1) * HALO, part * size_z:(part + 1) * size_z]


def place_forces(scal_ref, sets, all_ref):
    if len(sets) == 1:
        return sets[0]
    own_ref, side_ref, sideo_ref, far_ref, faro_ref = sets
    o, mine = scal_ref[1], scal_ref[2]
    count, lanes = own_ref.shape[1:]
    beside, opposite, mirror = o + 1 - 2 * lax.rem(o, 2), lax.rem(o + 2, 4), 3 - o
    size_z = side_ref.shape[-1]
    tiles = side_ref.shape[0] - 2 * (lanes // size_z) * (count // HALO)
    here = mine == 0

    def spot(j):
        return pl.ds(pl.multiple_of(j * count, count), count)

    for ref, j in ((side_ref, jnp.where(here, beside, mirror)), (sideo_ref, jnp.where(here, mirror, beside))):
        for z in range(2):
            for part in range(lanes // size_z):
                at = tiles + (z * (lanes // size_z) + part) * (count // HALO)
                all_ref[z, spot(j), part * size_z:(part + 1) * size_z] = ref[
                    at:at + count // HALO
                ].reshape(count, size_z)
    for ref, j in (
        (far_ref, jnp.where(here, opposite, mirror)),
        (faro_ref, jnp.where(here, mirror, opposite)),
        (own_ref, o),
    ):
        for z in range(2):
            all_ref[z, spot(j), :] = ref[z]
    return all_ref


def panel_keys(ints_ref, o, panels, rows, size_x, size_y, zblocks):
    owner = jnp.concatenate([ints_ref[1 + i:2 + i, :] for i in range(-(-2 * panels // 128))], axis=1)
    half = 1 + owner.shape[1] // 128
    block = jnp.concatenate([ints_ref[half + i:half + 1 + i, :] for i in range(-(-2 * panels // 128))], axis=1)
    depth = block & (zblocks - 1)
    y = (block >> shift_of(zblocks)) & (size_y - 1)
    x = block >> (shift_of(zblocks) + shift_of(size_y))
    key = x * rows
    reach = NSTEP - 1
    row = jnp.where(owner == o, y, -1)
    row = jnp.where((owner == o + 1) & (y < reach), y + size_y, row)
    row = jnp.where((owner == o - 1) & (y >= size_y - reach), y + rows - size_y, row)
    return jnp.where(row < 0, -1, key + row), depth


def spread_forces(force, depth, size_z, block, steps):
    high = force.astype(BF16).astype(F32)
    both = jnp.concatenate([high, force - high], axis=0)
    rows = both.shape[0]
    lane = iota((rows, size_z), 1) >> shift_of(block)
    base = (
        (iota((size_z, size_z), 0) & (block - 1)) == (iota((size_z, size_z), 1) & (block - 1))
    ).astype(BF16)
    at = (iota((size_z, rows), 0) >> shift_of(block)) == depth
    at = jnp.transpose(at.astype(F32))
    per_tile = size_z // block
    out = []
    for q in range(steps * 3):
        part = both[:, (q // per_tile) * size_z:(q // per_tile + 1) * size_z]
        part = jnp.where(lane == q % per_tile, part, 0.0).astype(BF16)
        wide = jnp.dot(part, base, preferred_element_type=F32)
        out.append((wide * at).astype(BF16))
    return jnp.concatenate(out, axis=1)


def halo_tiles(high, low):
    sub = iota(high.shape, high.ndim - 2)
    upper = sub < HALO // 2
    now = jnp.where(upper, high, low)
    old = spin(jnp.where(upper, low, high), HALO // 2, high.ndim - 2)
    return now, old


def halo_rate(highs, lows):
    sub = iota(highs[0].shape, highs[0].ndim - 2)
    tile = jnp.zeros(highs[0].shape, F32)
    ends = slice(HALO - 1, HALO), slice(0, 1)
    for c in range(3):
        tile = jnp.where(sub == c, highs[c][..., ends[0], :], tile)
        tile = jnp.where(sub == HALO - 1 - c, lows[c][..., ends[1], :], tile)
    return tile


def sides(scal_ref, side_ref, sideo_ref, at):
    o, mine = scal_ref[1], scal_ref[2]
    high = lax.rem(o + mine, 2) == 0
    one, two = side_ref[at], sideo_ref[at]
    upper = jnp.where(o < scal_ref[4] - 1, jnp.where(high, one, two), 0.0)
    lower = jnp.where(o > 0, jnp.where(high, two, one), 0.0)
    return upper, lower


def face_kernel(
    scal_ref, speed_ref, un_ref, up_ref, lat_ref, uno_ref, upo_ref, lato_ref, ints_ref, intso_ref,
    side_ref, sideo_ref, *rest,
):
    *sets, out_ref, all_ref = rest
    comps, size_x, size_y, size_z = un_ref.shape
    rows = size_y + HALO
    tiles = comps * size_x
    a, o, mine = scal_ref[0], scal_ref[1], scal_ref[2]
    high = lax.rem(a + mine, 2) == 0
    forces = place_forces(scal_ref, sets, all_ref)
    panels = forces.shape[1]
    own = mine == 0
    now, old, rate, drive = {}, {}, {}, {}
    for z in range(2):
        keys, depth = panel_keys_of(z, own, ints_ref, intso_ref, o, panels, rows, size_x, size_y, size_z)
        wide = spread_forces(forces[z], depth, size_z, size_z // (size_z // 16), NSTEP - 1)
        first = jnp.where(high, size_x - NSTEP + 1, 0)
        node = iota(((NSTEP - 1) * rows, keys.shape[1]), 0) + first * rows
        hit = (node == keys).astype(F32).astype(BF16)
        got = jnp.dot(hit, wide, preferred_element_type=F32)
        got = got.reshape(NSTEP - 1, rows, wide.shape[1])
        for d in range(1, NSTEP):
            for n in range(NSTEP - d):
                for c in range(comps):
                    q = (n * comps + c) * size_z
                    drive[z, n, d, c] = jnp.where(
                        high, got[NSTEP - 1 - d, :, q:q + size_z], got[d - 1, :, q:q + size_z]
                    )
        speed = jnp.where(
            own if z == 0 else jnp.logical_not(own),
            speed_row(ints_ref, speed_ref),
            speed_row(intso_ref, speed_ref),
        )
        near = own if z == 0 else jnp.logical_not(own)
        for d in range(1, NSTEP + 1):
            x = jnp.where(high, size_x - d, d - 1)
            ups, lows = [], []
            for c in range(comps):
                upper, lower = sides(scal_ref, side_ref, sideo_ref, z * tiles + c * size_x + x)
                ups.append(upper)
                lows.append(lower)
                tile_now, tile_old = halo_tiles(upper, lower)
                centre = jnp.where(near, un_ref[c, x], uno_ref[c, x])
                now[z, d, c] = jnp.concatenate([centre, tile_now], axis=0)
                if d < NSTEP:
                    centre = jnp.where(near, up_ref[c, x], upo_ref[c, x])
                    old[z, d, c] = jnp.concatenate([centre, tile_old], axis=0)
            if d < NSTEP:
                centre = jnp.where(near, lat_ref[x], lato_ref[x]) * speed
                rate[z, d] = jnp.concatenate([centre, halo_rate(ups, lows)], axis=0)
    for z in range(2):
        for c in range(comps):
            out_ref[z, c] = now[z, 1, c]
        for d in (1, 2):
            out_ref[z, NSTEP * comps + d - 1] = rate[z, d]
    for n in range(1, NSTEP):
        later = {}
        for d in range(1, NSTEP - n + 1):
            for c in range(comps):
                sums = inplane(now[0, d, c], now[1, d, c])
                for z in range(2):
                    lap = sums[z] + now[z, d + 1, c]
                    if d > 1:
                        lap = lap + now[z, d - 1, c]
                    later[z, d, c] = (
                        2.0 * now[z, d, c] - old[z, d, c] + rate[z, d] * lap + drive[z, n - 1, d, c]
                    )
        old, now = now, later
        for z in range(2):
            for c in range(comps):
                out_ref[z, n * comps + c] = now[z, 1, c]


def panel_keys_of(z, own, ints_ref, intso_ref, o, panels, rows, size_x, size_y, size_z):
    near = own if z == 0 else jnp.logical_not(own)
    zblocks = size_z // 16
    mine = panel_keys(ints_ref, o, panels, rows, size_x, size_y, zblocks)
    theirs = panel_keys(intso_ref, o, panels, rows, size_x, size_y, zblocks)
    return tuple(jnp.where(near, one, two) for one, two in zip(mine, theirs))


def local_kernel(
    scal_ref, speed_ref, un_ref, up_ref, lat_ref, uno_ref, upo_ref, lato_ref, ints_ref, intso_ref,
    side_ref, sideo_ref, *rest,
):
    *sets, final_ref, before_ref, face_ref, ratef_ref, all_ref, now_ref, old_ref, rate_ref, drive_ref = rest
    comps, size_x, size_y, size_z = un_ref.shape
    rows = size_y + HALO
    tiles = comps * size_x
    o, mine = scal_ref[1], scal_ref[2]
    forces = place_forces(scal_ref, sets, all_ref)
    panels = forces.shape[1]
    own = mine == 0
    for z in range(2):
        keys, depth = panel_keys_of(z, own, ints_ref, intso_ref, o, panels, rows, size_x, size_y, size_z)
        wide = spread_forces(forces[z], depth, size_z, 16, NSTEP)
        node = iota((size_x * rows, keys.shape[1]), 0)
        hit = (node == keys).astype(F32).astype(BF16)
        for n in range(NSTEP):
            span = comps * size_z
            got = jnp.dot(hit, wide[:, n * span:(n + 1) * span], preferred_element_type=F32)
            for c in range(comps):
                drive_ref[n, z, c] = got[:, c * size_z:(c + 1) * size_z].reshape(size_x, rows, size_z)
    edge = jnp.zeros((rows, size_z), F32)
    for z in range(2):
        for c in range(comps):
            for ref in (now_ref, old_ref):
                ref[z, c, 0] = edge
                ref[z, c, size_x + 1] = edge
    for z_at, un, up, lat, ints in (
        (mine, un_ref, up_ref, lat_ref, ints_ref),
        (1 - mine, uno_ref, upo_ref, lato_ref, intso_ref),
    ):
        speed = speed_row(ints, speed_ref)
        ups, lows = [], []
        for c in range(comps):
            upper, lower = sides(scal_ref, side_ref, sideo_ref, pl.ds(z_at * tiles + c * size_x, size_x))
            ups.append(upper)
            lows.append(lower)
            tile_now, tile_old = halo_tiles(upper, lower)
            now_ref[z_at, c, 1:size_x + 1, 0:size_y] = un[c]
            now_ref[z_at, c, 1:size_x + 1, size_y:rows] = tile_now
            old_ref[z_at, c, 1:size_x + 1, 0:size_y] = up[c]
            old_ref[z_at, c, 1:size_x + 1, size_y:rows] = tile_old
        rate_ref[z_at, :, 0:size_y] = lat[...] * speed[None]
        rate_ref[z_at, :, size_y:rows] = halo_rate(ups, lows)
    for side in range(2):
        for z in range(2):
            for d in range(NSTEP):
                ratef_ref[side, z, d] = rate_ref[z, d if side else size_x - 1 - d]
    refs = [now_ref, old_ref]
    for n in range(NSTEP):
        now, old = refs[n % 2], refs[(n + 1) % 2]
        for side in range(2):
            for z in range(2):
                for c in range(comps):
                    face_ref[side, z, n * comps + c] = now[z, c, 1 if side else size_x]

        def step(x, carry):
            for c in range(comps):
                centre = now[0, c, x + 1], now[1, c, x + 1]
                sums = inplane(*centre)
                for z in range(2):
                    lap = sums[z] + (now[z, c, x] + now[z, c, x + 2])
                    old[z, c, x + 1] = (
                        2.0 * centre[z] - old[z, c, x + 1] + rate_ref[z, x] * lap + drive_ref[n, z, c, x]
                    )
            return carry

        lax.fori_loop(0, size_x, step, 0)
    now, old = refs[NSTEP % 2], refs[(NSTEP + 1) % 2]
    for c in range(comps):
        final_ref[c] = now[mine, c, 1:size_x + 1, 0:size_y]
        before_ref[c] = old[mine, c, 1:size_x + 1, 0:size_y]


def join_kernel(
    scal_ref, final_in, before_in, face_ref, ratef_ref, recv_ref, recvo_ref, final_ref, before_ref
):
    comps, size_x, size_y, size_z = final_in.shape
    a, mine = scal_ref[0], scal_ref[2]
    own = mine == 0
    high = lax.rem(a + mine, 2) == 0
    final_ref[...] = final_in[...]
    before_ref[...] = before_in[...]
    for side in range(2):
        is_high = side == 0
        here = high if is_high else jnp.logical_not(high)
        inside = a < scal_ref[3] - 1 if is_high else a > 0

        def theirs(z, at):
            return jnp.where(inside, jnp.where(here, recv_ref[z, at], recvo_ref[z, at]), 0.0)

        rate = {}
        for z in range(2):
            for m in range(NSTEP):
                rate[z, -m] = ratef_ref[side, z, m]
            for m in (1, 2):
                rate[z, m] = theirs(z, NSTEP * comps + m - 1)
        for c in range(comps):
            last, now = {}, {}
            for n in range(NSTEP):
                later = {}
                top = min(n + 1, NSTEP - 1 - n)
                for m in range(-n, top + 1):
                    centre = [now.get((z, m)) for z in range(2)]
                    sums = inplane(*centre) if centre[0] is not None else (None, None)
                    for z in range(2):
                        terms = [sums[z], now.get((z, m - 1)), now.get((z, m + 1))]
                        if m == 0:
                            terms.append(theirs(z, n * comps + c))
                        if m == 1:
                            terms.append(face_ref[side, z, n * comps + c])
                        terms = [t for t in terms if t is not None]
                        lap = functools.reduce(lambda p, q: p + q, terms)
                        value = rate[z, m] * lap
                        if centre[z] is not None:
                            value = value + 2.0 * centre[z]
                        if (z, m) in last:
                            value = value - last[z, m]
                        later[z, m] = value
                last, now = now, later
            for target, values in ((final_ref, now), (before_ref, last)):
                for m in range(0, -NSTEP, -1):
                    if (0, m) not in values:
                        continue
                    x = size_x - 1 + m if is_high else -m
                    add = jnp.where(own, values[0, m], values[1, m])[0:size_y]
                    target[c, x] = target[c, x] + add


def send(value, mesh_sizes, route):
    nx, ny, nz = mesh_sizes
    number = lambda i, j, k: (i * ny + j) * nz + k
    pairs = [
        (number(i, j, k), number(*route(i, j, k))) for i in range(nx) for j in range(ny) for k in range(nz)
    ]
    return lax.ppermute(value, ("gx", "gy", "gz"), pairs)


def partner(i, core, count):
    step = 1 if (i + core) % 2 == 0 else -1
    return (i + step) % count


def per_device(
    u_now, u_prev, panels, panel_owner, panel_block, coupling, layer_depth, layer_speed, lateral
):
    sizes = tuple(lax.axis_size(axis) for axis in ("gx", "gy", "gz"))
    nx, ny, nz = sizes
    assert nx % 2 == 0 and ny % 2 == 0 and nz == 2
    comps, size_x, size_y, size_z = u_now.shape
    rows = size_y + HALO
    per_dev, spectral = panels.shape[2], panels.shape[4]
    npanels = ny * per_dev
    scal = jnp.stack(
        [lax.axis_index("gx"), lax.axis_index("gy"), lax.axis_index("gz"), jnp.int32(nx), jnp.int32(ny)]
    ).astype(jnp.int32)

    def swap(value):
        return send(value, sizes, lambda i, j, k: (i, j, 1 - k))

    def route_x(i, j, k):
        return partner(i, k, nx), j, k

    def route_y(i, j, k):
        to = partner(j, k, ny)
        if abs(to - j) != 1 or (ny == 2 and k == 1):
            return i ^ 1, j, k
        return i, to, k

    owner, block = panel_owner.reshape(-1), panel_block.reshape(-1)
    both = jnp.concatenate([layer_depth, owner, owner, block, block])
    ints = jnp.pad(both, (0, -both.shape[0] % 1024)).reshape(-1, size_z)
    un_o, up_o, lat_o, ints_o = swap(u_now), swap(u_prev), swap(lateral), swap(ints)

    vmem = pl.BlockSpec(memory_space=pltpu.VMEM)
    smem = pl.BlockSpec(memory_space=pltpu.SMEM)
    params = pltpu.CompilerParams(vmem_limit_bytes=48 * 1024 * 1024)
    table = jnp.asarray(wave_table(spectral, panels.shape[3]))
    force = pl.pallas_call(
        force_kernel,
        out_shape=jax.ShapeDtypeStruct((per_dev, table.shape[1]), F32),
        in_specs=[vmem] * 3,
        out_specs=vmem,
        compiler_params=params,
        name="force",
    )(panels.reshape(per_dev, panels.shape[3], spectral), coupling, table)
    force_o = swap(force)
    tiles = comps * size_x
    extra = 2 * (force.shape[1] // size_z) * (per_dev // HALO)
    state = (scal, layer_speed, u_now, u_prev, lateral, un_o, up_o, lat_o, ints, ints_o)
    state_specs = [smem] * 2 + [vmem] * 8
    packed, pair = pl.pallas_call(
        pack_kernel,
        out_shape=(
            jax.ShapeDtypeStruct((2 * tiles + extra, HALO, size_z), F32),
            jax.ShapeDtypeStruct((2,) + force.shape, F32),
        ),
        in_specs=state_specs + [vmem] * 2,
        out_specs=(vmem, vmem),
        compiler_params=params,
        name="pack",
    )(*state, force, force_o)
    side = send(packed, sizes, route_y)
    if ny == 4:
        far = send(pair, sizes, lambda i, j, k: (i, j ^ 2 if k == 0 else 3 - j, k))
        side_o, far_o = swap(side), swap(far)
        sets = (pair, side, side_o, far, far_o)
    else:
        side_o = swap(side)
        sets = (jnp.moveaxis(lax.all_gather(pair, "gy"), 0, 1).reshape(2, npanels, -1),)
    shared = state + (side, side_o) + sets
    shared_specs = state_specs + [vmem] * (2 + len(sets))
    all_scratch = pltpu.VMEM((2, npanels, force.shape[1]), F32)
    planes = NSTEP * comps
    sent = pl.pallas_call(
        face_kernel,
        out_shape=jax.ShapeDtypeStruct((2, planes + 2, rows, size_z), F32),
        in_specs=shared_specs,
        out_specs=vmem,
        scratch_shapes=[all_scratch],
        compiler_params=params,
        name="face",
    )(*shared)
    recv = send(sent, sizes, route_x)
    final, before, face, ratef = pl.pallas_call(
        local_kernel,
        out_shape=(
            jax.ShapeDtypeStruct(u_now.shape, F32),
            jax.ShapeDtypeStruct(u_now.shape, F32),
            jax.ShapeDtypeStruct((2, 2, planes, rows, size_z), F32),
            jax.ShapeDtypeStruct((2, 2, NSTEP, rows, size_z), F32),
        ),
        in_specs=shared_specs,
        out_specs=(vmem,) * 4,
        scratch_shapes=[
            all_scratch,
            pltpu.VMEM((2, comps, size_x + 2, rows, size_z), F32),
            pltpu.VMEM((2, comps, size_x + 2, rows, size_z), F32),
            pltpu.VMEM((2, size_x, rows, size_z), F32),
            pltpu.VMEM((NSTEP, 2, comps, size_x, rows, size_z), F32),
        ],
        compiler_params=params,
        name="local",
    )(*shared)
    recv_o = swap(recv)
    return pl.pallas_call(
        join_kernel,
        out_shape=(
            jax.ShapeDtypeStruct(u_now.shape, F32),
            jax.ShapeDtypeStruct(u_now.shape, F32),
        ),
        in_specs=[smem] + [vmem] * 6,
        out_specs=(vmem, vmem),
        compiler_params=params,
        name="join",
    )(scal, final, before, face, ratef, recv, recv_o)


def solution(mesh):
    in_specs = (
        P(None, "gx", "gy", "gz"),
        P(None, "gx", "gy", "gz"),
        P("gx", "gz", "gy", None, None),
        P("gx", "gz", None, None),
        P("gx", "gz", None),
        P(),
        P("gz"),
        P(),
        P("gx", "gy", "gz"),
    )
    out_specs = (P(None, "gx", "gy", "gz"), P(None, "gx", "gy", "gz"))
    return jax.shard_map(
        per_device, mesh=mesh, in_specs=in_specs, out_specs=out_specs, check_vma=False
    )
```

```python
import functools

import jax
import jax.numpy as jnp
import ml_dtypes
import numpy as np
from jax import lax
from jax.experimental import pallas as pl
from jax.experimental.pallas import tpu as pltpu
from jax.sharding import PartitionSpec as P

NSTEP = 4
HALO = 8
LANES = 128
PANELS = 16
F32 = jnp.float32
BF16 = jnp.bfloat16


def wave_table(count, per_step):
    half = count // 2
    freq = np.float32(2.0 * np.pi) * (np.arange(half, dtype=np.float32) + np.float32(0.5)) / np.float32(count)
    times = np.float32(37.0) + np.arange(NSTEP, dtype=np.float32)
    phase = freq[:, None] * times[None, :]
    table = np.concatenate([np.cos(phase), np.sin(phase)], axis=0) / np.sqrt(np.float32(half))
    wide = np.repeat(table.astype(ml_dtypes.bfloat16), per_step, axis=1)
    return np.pad(wide, ((0, 0), (0, -wide.shape[1] % 128)))


def shift_of(size):
    assert size & (size - 1) == 0
    return size.bit_length() - 1


def iota(shape, dim):
    return lax.broadcasted_iota(jnp.int32, shape, dim)


def spin(value, amount, axis):
    return pltpu.roll(value, amount % value.shape[axis], axis)


def across(z0, z1):
    lanes = z0.shape[-1]
    lane = iota(z0.shape, z0.ndim - 1)
    first, last = lane == 0, lane == lanes - 1
    ax = z0.ndim - 1
    down0, down1 = spin(z0, 1, ax), spin(z1, 1, ax)
    up0, up1 = spin(z0, -1, ax), spin(z1, -1, ax)
    sum0 = jnp.where(first, 0.0, down0) + jnp.where(last, up1, up0)
    sum1 = jnp.where(first, down0, down1) + jnp.where(last, 0.0, up1)
    return sum0, sum1


def inplane(z0, z1):
    ax = z0.ndim - 2
    sum0, sum1 = across(z0, z1)
    sum0 = sum0 + (spin(z0, 1, ax) + spin(z0, -1, ax)) - 6.0 * z0
    sum1 = sum1 + (spin(z1, 1, ax) + spin(z1, -1, ax)) - 6.0 * z1
    return sum0, sum1


def speed_row(ints_ref, speed_ref):
    depth = integers(ints_ref, LANES, 0)
    row = jnp.zeros(depth.shape, F32)
    for layer in range(speed_ref.shape[0]):
        row = jnp.where(depth == layer, speed_ref[layer], row)
    return row


def prepare_kernel(
    panels_hbm, coupling_hbm, table_hbm, depth_hbm, owner_hbm, block_hbm, un_hbm, up_hbm, lat_hbm,
    out_ref, un_ref, up_ref, lat_ref,
    panels_ref, coupling_ref, table_ref, depth_ref, owner_ref, block_ref, sems,
):
    pairs = (
        (panels_hbm, panels_ref), (table_hbm, table_ref), (coupling_hbm, coupling_ref),
        (depth_hbm, depth_ref), (owner_hbm, owner_ref), (block_hbm, block_ref),
        (un_hbm, un_ref), (up_hbm, up_ref), (lat_hbm, lat_ref),
    )
    copies = [pltpu.make_async_copy(src, dst, sems.at[i]) for i, (src, dst) in enumerate(pairs)]
    for copy in copies:
        copy.start()
    for copy in copies[:6]:
        copy.wait()
    count, rows, spectral = panels_ref.shape
    comps, block = 3, rows // 3
    lanes = table_ref.shape[1]
    free = jnp.dot(
        panels_ref[...].reshape(count * rows, spectral), table_ref[...], preferred_element_type=F32
    )
    weights = coupling_ref[...].reshape(rows, block)
    stacked = jnp.concatenate([weights] * NSTEP + [jnp.zeros((lanes - NSTEP * rows, block), F32)], axis=0)
    pick = ((iota((rows, block), 0) & (block - 1)) == iota((rows, block), 1)).astype(F32)
    spread = lax.dot_general(
        pick, stacked, (((1,), (1,)), ((), ())), precision=lax.Precision.HIGHEST, preferred_element_type=F32
    )
    comp_row = iota((rows, lanes), 0) >> shift_of(block)
    comp_lane = iota((rows, lanes), 1) >> shift_of(block)
    same = comp_lane == comp_row
    for step in range(1, NSTEP):
        same = same | (comp_lane == comp_row + step * comps)
    spread = jnp.where(same, spread, 0.0)
    out_ref[0:count] = jnp.sum(free.reshape(count, rows, lanes) * spread[None], axis=1)
    out_ref[count:] = jnp.zeros((out_ref.shape[0] - count, lanes), F32)
    pieces = [depth_ref[...]]
    for ref in (owner_ref, block_ref):
        twice = jnp.concatenate([ref[...], ref[...]], axis=1)
        pieces += [twice[:, i:i + LANES] for i in range(0, twice.shape[1], LANES)]
    for i, piece in enumerate(pieces):
        row, at = count + i * LANES // lanes, i * LANES % lanes
        out_ref[row:row + 1, at:at + LANES] = piece.astype(F32)
    for copy in copies[6:]:
        copy.wait()


def integers(ref, panels, which):
    lanes = ref.shape[1]
    width = -(-2 * panels // LANES)
    first, number = ((0, 1), (1, width), (1 + width, width))[which]
    out = []
    for i in range(first, first + number):
        row, at = PANELS + i * LANES // lanes, i * LANES % lanes
        out.append(ref[row:row + 1, at:at + LANES].astype(jnp.int32))
    return jnp.concatenate(out, axis=1)


def pack_kernel(
    scal_ref, speed_ref, un_ref, up_ref, lat_ref, uno_ref, upo_ref, lato_ref, ints_ref, intso_ref,
    out_ref, pair_ref,
):
    mine = scal_ref[2]
    high = lax.rem(scal_ref[1] + mine, 2) == 0
    comps, size_x, size_y, size_z = un_ref.shape
    tiles = comps * size_x
    shape = (size_x, HALO, size_z)
    sub = iota(shape, 1)

    def fill(side):
        base = size_y - HALO if side else 0
        for z_at, un, up, lat, ints in (
            (mine, un_ref, up_ref, lat_ref, ints_ref),
            (1 - mine, uno_ref, upo_ref, lato_ref, intso_ref),
        ):
            rate = lat[:, base:base + HALO, :] * speed_row(ints, speed_ref)[None]
            for c in range(comps):
                now = un[c, :, base:base + HALO, :]
                old = spin(up[c, :, base:base + HALO, :], HALO // 2, 1)
                keep = sub >= HALO // 2 if side else sub < HALO // 2
                row = HALO - 1 - c if side else c
                tile = jnp.where(keep, now, old)
                tile = jnp.where(sub == (0 if side else HALO - 1), rate[:, row:row + 1, :], tile)
                out_ref[pl.ds(z_at * tiles + c * size_x, size_x)] = tile

    @pl.when(high)
    def _():
        fill(True)

    @pl.when(jnp.logical_not(high))
    def _():
        fill(False)

    count, lanes = PANELS, ints_ref.shape[1]
    for z_at, force in ((mine, ints_ref), (1 - mine, intso_ref)):
        pair_ref[z_at] = force[0:count]
        for part in range(lanes // size_z):
            for piece in range(count // HALO):
                at = 2 * tiles + (z_at * (lanes // size_z) + part) * (count // HALO) + piece
                out_ref[at] = force[piece * HALO:(piece + 1) * HALO, part * size_z:(part + 1) * size_z]


def place_forces(scal_ref, sets, all_ref):
    if len(sets) == 1:
        return sets[0]
    own_ref, side_ref, sideo_ref, far_ref, faro_ref = sets
    o, mine = scal_ref[1], scal_ref[2]
    count, lanes = own_ref.shape[1:]
    beside, opposite, mirror = o + 1 - 2 * lax.rem(o, 2), lax.rem(o + 2, 4), 3 - o
    size_z = side_ref.shape[-1]
    tiles = side_ref.shape[0] - 2 * (lanes // size_z) * (count // HALO)
    here = mine == 0

    def spot(j):
        return pl.ds(pl.multiple_of(j * count, count), count)

    for ref, j in ((side_ref, jnp.where(here, beside, mirror)), (sideo_ref, jnp.where(here, mirror, beside))):
        for z in range(2):
            for part in range(lanes // size_z):
                at = tiles + (z * (lanes // size_z) + part) * (count // HALO)
                all_ref[z, spot(j), part * size_z:(part + 1) * size_z] = ref[
                    at:at + count // HALO
                ].reshape(count, size_z)
    for ref, j in (
        (far_ref, jnp.where(here, opposite, mirror)),
        (faro_ref, jnp.where(here, mirror, opposite)),
        (own_ref, o),
    ):
        for z in range(2):
            all_ref[z, spot(j), :] = ref[z]
    return all_ref


def panel_keys(ints_ref, o, panels, rows, size_x, size_y, zblocks):
    owner = integers(ints_ref, panels, 1)
    block = integers(ints_ref, panels, 2)
    depth = block & (zblocks - 1)
    y = (block >> shift_of(zblocks)) & (size_y - 1)
    x = block >> (shift_of(zblocks) + shift_of(size_y))
    key = x * rows
    reach = NSTEP - 1
    row = jnp.where(owner == o, y, -1)
    row = jnp.where((owner == o + 1) & (y < reach), y + size_y, row)
    row = jnp.where((owner == o - 1) & (y >= size_y - reach), y + rows - size_y, row)
    return jnp.where(row < 0, -1, key + row), depth


def spread_forces(force, depth, size_z, block, steps):
    high = force.astype(BF16).astype(F32)
    both = jnp.concatenate([high, force - high], axis=0)
    rows = both.shape[0]
    lane = iota((rows, size_z), 1) >> shift_of(block)
    base = (
        (iota((size_z, size_z), 0) & (block - 1)) == (iota((size_z, size_z), 1) & (block - 1))
    ).astype(BF16)
    at = (iota((size_z, rows), 0) >> shift_of(block)) == depth
    at = jnp.transpose(at.astype(F32))
    per_tile = size_z // block
    out = []
    for q in range(steps * 3):
        part = both[:, (q // per_tile) * size_z:(q // per_tile + 1) * size_z]
        part = jnp.where(lane == q % per_tile, part, 0.0).astype(BF16)
        wide = jnp.dot(part, base, preferred_element_type=F32)
        out.append((wide * at).astype(BF16))
    return jnp.concatenate(out, axis=1)


def halo_tiles(high, low):
    sub = iota(high.shape, high.ndim - 2)
    upper = sub < HALO // 2
    now = jnp.where(upper, high, low)
    old = spin(jnp.where(upper, low, high), HALO // 2, high.ndim - 2)
    return now, old


def halo_rate(highs, lows):
    sub = iota(highs[0].shape, highs[0].ndim - 2)
    tile = jnp.zeros(highs[0].shape, F32)
    ends = slice(HALO - 1, HALO), slice(0, 1)
    for c in range(3):
        tile = jnp.where(sub == c, highs[c][..., ends[0], :], tile)
        tile = jnp.where(sub == HALO - 1 - c, lows[c][..., ends[1], :], tile)
    return tile


def sides(scal_ref, side_ref, sideo_ref, at):
    o, mine = scal_ref[1], scal_ref[2]
    high = lax.rem(o + mine, 2) == 0
    one, two = side_ref[at], sideo_ref[at]
    upper = jnp.where(o < scal_ref[4] - 1, jnp.where(high, one, two), 0.0)
    lower = jnp.where(o > 0, jnp.where(high, two, one), 0.0)
    return upper, lower


def face_kernel(
    scal_ref, speed_ref, un_ref, up_ref, lat_ref, uno_ref, upo_ref, lato_ref, ints_ref, intso_ref,
    side_ref, sideo_ref, *rest,
):
    *sets, out_ref, all_ref = rest
    comps, size_x, size_y, size_z = un_ref.shape
    rows = size_y + HALO
    tiles = comps * size_x
    a, o, mine = scal_ref[0], scal_ref[1], scal_ref[2]
    high = lax.rem(a + mine, 2) == 0
    forces = place_forces(scal_ref, sets, all_ref)
    panels = forces.shape[1]
    own = mine == 0
    now, old, rate, drive = {}, {}, {}, {}
    for z in range(2):
        keys, depth = panel_keys_of(z, own, ints_ref, intso_ref, o, panels, rows, size_x, size_y, size_z)
        wide = spread_forces(forces[z], depth, size_z, size_z // (size_z // 16), NSTEP - 1)
        first = jnp.where(high, size_x - NSTEP + 1, 0)
        node = iota(((NSTEP - 1) * rows, keys.shape[1]), 0) + first * rows
        hit = (node == keys).astype(F32).astype(BF16)
        got = jnp.dot(hit, wide, preferred_element_type=F32)
        got = got.reshape(NSTEP - 1, rows, wide.shape[1])
        for d in range(1, NSTEP):
            for n in range(NSTEP - d):
                for c in range(comps):
                    q = (n * comps + c) * size_z
                    drive[z, n, d, c] = jnp.where(
                        high, got[NSTEP - 1 - d, :, q:q + size_z], got[d - 1, :, q:q + size_z]
                    )
        speed = jnp.where(
            own if z == 0 else jnp.logical_not(own),
            speed_row(ints_ref, speed_ref),
            speed_row(intso_ref, speed_ref),
        )
        near = own if z == 0 else jnp.logical_not(own)
        for d in range(1, NSTEP + 1):
            x = jnp.where(high, size_x - d, d - 1)
            ups, lows = [], []
            for c in range(comps):
                upper, lower = sides(scal_ref, side_ref, sideo_ref, z * tiles + c * size_x + x)
                ups.append(upper)
                lows.append(lower)
                tile_now, tile_old = halo_tiles(upper, lower)
                centre = jnp.where(near, un_ref[c, x], uno_ref[c, x])
                now[z, d, c] = jnp.concatenate([centre, tile_now], axis=0)
                if d < NSTEP:
                    centre = jnp.where(near, up_ref[c, x], upo_ref[c, x])
                    old[z, d, c] = jnp.concatenate([centre, tile_old], axis=0)
            if d < NSTEP:
                centre = jnp.where(near, lat_ref[x], lato_ref[x]) * speed
                rate[z, d] = jnp.concatenate([centre, halo_rate(ups, lows)], axis=0)
    for z in range(2):
        for c in range(comps):
            out_ref[z, c] = now[z, 1, c]
        for d in (1, 2):
            out_ref[z, NSTEP * comps + d - 1] = rate[z, d]
    for n in range(1, NSTEP):
        later = {}
        for d in range(1, NSTEP - n + 1):
            for c in range(comps):
                sums = inplane(now[0, d, c], now[1, d, c])
                for z in range(2):
                    lap = sums[z] + now[z, d + 1, c]
                    if d > 1:
                        lap = lap + now[z, d - 1, c]
                    later[z, d, c] = (
                        2.0 * now[z, d, c] - old[z, d, c] + rate[z, d] * lap + drive[z, n - 1, d, c]
                    )
        old, now = now, later
        for z in range(2):
            for c in range(comps):
                out_ref[z, n * comps + c] = now[z, 1, c]


def panel_keys_of(z, own, ints_ref, intso_ref, o, panels, rows, size_x, size_y, size_z):
    near = own if z == 0 else jnp.logical_not(own)
    zblocks = size_z // 16
    mine = panel_keys(ints_ref, o, panels, rows, size_x, size_y, zblocks)
    theirs = panel_keys(intso_ref, o, panels, rows, size_x, size_y, zblocks)
    return tuple(jnp.where(near, one, two) for one, two in zip(mine, theirs))


def local_kernel(
    scal_ref, speed_ref, un_ref, up_ref, lat_ref, uno_ref, upo_ref, lato_ref, ints_ref, intso_ref,
    side_ref, sideo_ref, *rest,
):
    *sets, final_ref, before_ref, face_ref, ratef_ref, all_ref, now_ref, old_ref, rate_ref, drive_ref = rest
    comps, size_x, size_y, size_z = un_ref.shape
    rows = size_y + HALO
    tiles = comps * size_x
    o, mine = scal_ref[1], scal_ref[2]
    forces = place_forces(scal_ref, sets, all_ref)
    panels = forces.shape[1]
    own = mine == 0
    for z in range(2):
        keys, depth = panel_keys_of(z, own, ints_ref, intso_ref, o, panels, rows, size_x, size_y, size_z)
        wide = spread_forces(forces[z], depth, size_z, 16, NSTEP)
        node = iota((size_x * rows, keys.shape[1]), 0)
        hit = (node == keys).astype(F32).astype(BF16)
        for n in range(NSTEP):
            span = comps * size_z
            got = jnp.dot(hit, wide[:, n * span:(n + 1) * span], preferred_element_type=F32)
            for c in range(comps):
                drive_ref[n, z, c] = got[:, c * size_z:(c + 1) * size_z].reshape(size_x, rows, size_z)
    edge = jnp.zeros((rows, size_z), F32)
    for z in range(2):
        for c in range(comps):
            for ref in (now_ref, old_ref):
                ref[z, c, 0] = edge
                ref[z, c, size_x + 1] = edge
    for z_at, un, up, lat, ints in (
        (mine, un_ref, up_ref, lat_ref, ints_ref),
        (1 - mine, uno_ref, upo_ref, lato_ref, intso_ref),
    ):
        speed = speed_row(ints, speed_ref)
        ups, lows = [], []
        for c in range(comps):
            upper, lower = sides(scal_ref, side_ref, sideo_ref, pl.ds(z_at * tiles + c * size_x, size_x))
            ups.append(upper)
            lows.append(lower)
            tile_now, tile_old = halo_tiles(upper, lower)
            now_ref[z_at, c, 1:size_x + 1, 0:size_y] = un[c]
            now_ref[z_at, c, 1:size_x + 1, size_y:rows] = tile_now
            old_ref[z_at, c, 1:size_x + 1, 0:size_y] = up[c]
            old_ref[z_at, c, 1:size_x + 1, size_y:rows] = tile_old
        rate_ref[z_at, :, 0:size_y] = lat[...] * speed[None]
        rate_ref[z_at, :, size_y:rows] = halo_rate(ups, lows)
    for side in range(2):
        for z in range(2):
            for d in range(NSTEP):
                ratef_ref[side, z, d] = rate_ref[z, d if side else size_x - 1 - d]
    refs = [now_ref, old_ref]
    for n in range(NSTEP):
        now, old = refs[n % 2], refs[(n + 1) % 2]
        for side in range(2):
            for z in range(2):
                for c in range(comps):
                    face_ref[side, z, n * comps + c] = now[z, c, 1 if side else size_x]

        def step(x, carry):
            for c in range(comps):
                centre = now[0, c, x + 1], now[1, c, x + 1]
                sums = inplane(*centre)
                for z in range(2):
                    lap = sums[z] + (now[z, c, x] + now[z, c, x + 2])
                    old[z, c, x + 1] = (
                        2.0 * centre[z] - old[z, c, x + 1] + rate_ref[z, x] * lap + drive_ref[n, z, c, x]
                    )
            return carry

        lax.fori_loop(0, size_x, step, 0)
    now, old = refs[NSTEP % 2], refs[(NSTEP + 1) % 2]
    for c in range(comps):
        final_ref[c] = now[mine, c, 1:size_x + 1, 0:size_y]
        before_ref[c] = old[mine, c, 1:size_x + 1, 0:size_y]


def join_kernel(
    scal_ref, final_in, before_in, face_ref, ratef_ref, recv_ref, recvo_ref, final_ref, before_ref
):
    comps, size_x, size_y, size_z = final_in.shape
    a, mine = scal_ref[0], scal_ref[2]
    own = mine == 0
    high = lax.rem(a + mine, 2) == 0
    final_ref[...] = final_in[...]
    before_ref[...] = before_in[...]
    for side in range(2):
        is_high = side == 0
        here = high if is_high else jnp.logical_not(high)
        inside = a < scal_ref[3] - 1 if is_high else a > 0

        def theirs(z, at):
            return jnp.where(inside, jnp.where(here, recv_ref[z, at], recvo_ref[z, at]), 0.0)

        rate = {}
        for z in range(2):
            for m in range(NSTEP):
                rate[z, -m] = ratef_ref[side, z, m]
            for m in (1, 2):
                rate[z, m] = theirs(z, NSTEP * comps + m - 1)
        for c in range(comps):
            last, now = {}, {}
            for n in range(NSTEP):
                later = {}
                top = min(n + 1, NSTEP - 1 - n)
                for m in range(-n, top + 1):
                    centre = [now.get((z, m)) for z in range(2)]
                    sums = inplane(*centre) if centre[0] is not None else (None, None)
                    for z in range(2):
                        terms = [sums[z], now.get((z, m - 1)), now.get((z, m + 1))]
                        if m == 0:
                            terms.append(theirs(z, n * comps + c))
                        if m == 1:
                            terms.append(face_ref[side, z, n * comps + c])
                        terms = [t for t in terms if t is not None]
                        lap = functools.reduce(lambda p, q: p + q, terms)
                        value = rate[z, m] * lap
                        if centre[z] is not None:
                            value = value + 2.0 * centre[z]
                        if (z, m) in last:
                            value = value - last[z, m]
                        later[z, m] = value
                last, now = now, later
            for target, values in ((final_ref, now), (before_ref, last)):
                for m in range(0, -NSTEP, -1):
                    if (0, m) not in values:
                        continue
                    x = size_x - 1 + m if is_high else -m
                    add = jnp.where(own, values[0, m], values[1, m])[0:size_y]
                    target[c, x] = target[c, x] + add


def send(value, mesh_sizes, route):
    nx, ny, nz = mesh_sizes
    number = lambda i, j, k: (i * ny + j) * nz + k
    pairs = [
        (number(i, j, k), number(*route(i, j, k))) for i in range(nx) for j in range(ny) for k in range(nz)
    ]
    return lax.ppermute(value, ("gx", "gy", "gz"), pairs)


def partner(i, core, count):
    step = 1 if (i + core) % 2 == 0 else -1
    return (i + step) % count


def per_device(
    u_now, u_prev, panels, panel_owner, panel_block, coupling, layer_depth, layer_speed, lateral
):
    sizes = tuple(lax.axis_size(axis) for axis in ("gx", "gy", "gz"))
    nx, ny, nz = sizes
    assert nx % 2 == 0 and ny % 2 == 0 and nz == 2
    comps, size_x, size_y, size_z = u_now.shape
    rows = size_y + HALO
    per_dev, spectral = panels.shape[2], panels.shape[4]
    npanels = ny * per_dev
    scal = jnp.stack(
        [lax.axis_index("gx"), lax.axis_index("gy"), lax.axis_index("gz"), jnp.int32(nx), jnp.int32(ny)]
    ).astype(jnp.int32)

    def swap(value):
        return send(value, sizes, lambda i, j, k: (i, j, 1 - k))

    def route_x(i, j, k):
        return partner(i, k, nx), j, k

    def route_y(i, j, k):
        to = partner(j, k, ny)
        if abs(to - j) != 1 or (ny == 2 and k == 1):
            return i ^ 1, j, k
        return i, to, k

    assert per_dev == PANELS and size_z == LANES
    un_o, up_o, lat_o = swap(u_now), swap(u_prev), swap(lateral)

    vmem = pl.BlockSpec(memory_space=pltpu.VMEM)
    smem = pl.BlockSpec(memory_space=pltpu.SMEM)
    params = pltpu.CompilerParams(vmem_limit_bytes=48 * 1024 * 1024)
    table = jnp.asarray(wave_table(spectral, panels.shape[3]))
    width = table.shape[1]
    number = LANES + 4 * npanels
    extra_rows = -(-(-(-number // width)) // 8) * 8
    ints, un_v, up_v, lat_v = pl.pallas_call(
        prepare_kernel,
        out_shape=(
            jax.ShapeDtypeStruct((per_dev + extra_rows, width), F32),
            jax.ShapeDtypeStruct(u_now.shape, F32),
            jax.ShapeDtypeStruct(u_prev.shape, F32),
            jax.ShapeDtypeStruct(lateral.shape, F32),
        ),
        in_specs=[pl.BlockSpec(memory_space=pl.ANY)] * 9,
        out_specs=(vmem,) * 4,
        scratch_shapes=[
            pltpu.VMEM((per_dev,) + panels.shape[3:], BF16),
            pltpu.VMEM(coupling.shape, F32),
            pltpu.VMEM(table.shape, BF16),
            pltpu.VMEM((1, size_z), jnp.int32),
            pltpu.VMEM((1, npanels), jnp.int32),
            pltpu.VMEM((1, npanels), jnp.int32),
            pltpu.SemaphoreType.DMA((9,)),
        ],
        compiler_params=params,
        name="prepare",
    )(*(
        pltpu.with_memory_space_constraint(value, pltpu.HBM)
        for value in (
            panels.reshape((per_dev,) + panels.shape[3:]), coupling, table, layer_depth.reshape(1, -1),
            panel_owner.reshape(1, -1), panel_block.reshape(1, -1), u_now, u_prev, lateral,
        )
    ))
    ints_o = swap(ints)
    tiles = comps * size_x
    extra = 2 * (width // size_z) * (per_dev // HALO)
    state = (scal, layer_speed, un_v, up_v, lat_v, un_o, up_o, lat_o, ints, ints_o)
    state_specs = [smem] * 2 + [vmem] * 8
    packed, pair = pl.pallas_call(
        pack_kernel,
        out_shape=(
            jax.ShapeDtypeStruct((2 * tiles + extra, HALO, size_z), F32),
            jax.ShapeDtypeStruct((2, per_dev, width), F32),
        ),
        in_specs=state_specs,
        out_specs=(vmem, vmem),
        compiler_params=params,
        name="pack",
    )(*state)
    side = send(packed, sizes, route_y)
    if ny == 4:
        far = send(pair, sizes, lambda i, j, k: (i, j ^ 2 if k == 0 else 3 - j, k))
        side, far = lax.optimization_barrier((side, far))
        side_o, far_o = swap(side), swap(far)
        sets = (pair, side, side_o, far, far_o)
    else:
        side_o = swap(side)
        sets = (jnp.moveaxis(lax.all_gather(pair, "gy"), 0, 1).reshape(2, npanels, -1),)
    shared = state + (side, side_o) + sets
    shared_specs = state_specs + [vmem] * (2 + len(sets))
    all_scratch = pltpu.VMEM((2, npanels, width), F32)
    planes = NSTEP * comps
    sent = pl.pallas_call(
        face_kernel,
        out_shape=jax.ShapeDtypeStruct((2, planes + 2, rows, size_z), F32),
        in_specs=shared_specs,
        out_specs=vmem,
        scratch_shapes=[all_scratch],
        compiler_params=params,
        name="face",
    )(*shared)
    recv = send(sent, sizes, route_x)
    final, before, face, ratef = pl.pallas_call(
        local_kernel,
        out_shape=(
            jax.ShapeDtypeStruct(u_now.shape, F32),
            jax.ShapeDtypeStruct(u_now.shape, F32),
            jax.ShapeDtypeStruct((2, 2, planes, rows, size_z), F32),
            jax.ShapeDtypeStruct((2, 2, NSTEP, rows, size_z), F32),
        ),
        in_specs=shared_specs,
        out_specs=(vmem,) * 4,
        scratch_shapes=[
            all_scratch,
            pltpu.VMEM((2, comps, size_x + 2, rows, size_z), F32),
            pltpu.VMEM((2, comps, size_x + 2, rows, size_z), F32),
            pltpu.VMEM((2, size_x, rows, size_z), F32),
            pltpu.VMEM((NSTEP, 2, comps, size_x, rows, size_z), F32),
        ],
        compiler_params=params,
        name="local",
    )(*shared)
    final, before, face, ratef, recv = lax.optimization_barrier((final, before, face, ratef, recv))
    recv_o = swap(recv)
    return pl.pallas_call(
        join_kernel,
        out_shape=(
            jax.ShapeDtypeStruct(u_now.shape, F32),
            jax.ShapeDtypeStruct(u_now.shape, F32),
        ),
        in_specs=[smem] + [vmem] * 6,
        out_specs=(vmem, vmem),
        compiler_params=params,
        name="join",
    )(scal, final, before, face, ratef, recv, recv_o)


def solution(mesh):
    in_specs = (
        P(None, "gx", "gy", "gz"),
        P(None, "gx", "gy", "gz"),
        P("gx", "gz", "gy", None, None),
        P("gx", "gz", None, None),
        P("gx", "gz", None),
        P(),
        P("gz"),
        P(),
        P("gx", "gy", "gz"),
    )
    out_specs = (P(None, "gx", "gy", "gz"), P(None, "gx", "gy", "gz"))
    return jax.shard_map(
        per_device, mesh=mesh, in_specs=in_specs, out_specs=out_specs, check_vma=False
    )
```

```python
import functools

import jax
import jax.numpy as jnp
import ml_dtypes
import numpy as np
from jax import lax
from jax.experimental import pallas as pl
from jax.experimental.pallas import tpu as pltpu
from jax.sharding import PartitionSpec as P

NSTEP = 4
HALO = 8
LANES = 128
PANELS = 16
TOP = 32767.0
F32 = jnp.float32
BF16 = jnp.bfloat16


def wave_table(count, per_step):
    half = count // 2
    freq = np.float32(2.0 * np.pi) * (np.arange(half, dtype=np.float32) + np.float32(0.5)) / np.float32(count)
    times = np.float32(37.0) + np.arange(NSTEP, dtype=np.float32)
    phase = freq[:, None] * times[None, :]
    table = np.concatenate([np.cos(phase), np.sin(phase)], axis=0) / np.sqrt(np.float32(half))
    wide = np.repeat(table.astype(ml_dtypes.bfloat16), per_step, axis=1)
    return np.pad(wide, ((0, 0), (0, -wide.shape[1] % 128)))


def shift_of(size):
    assert size & (size - 1) == 0
    return size.bit_length() - 1


def iota(shape, dim):
    return lax.broadcasted_iota(jnp.int32, shape, dim)


def spin(value, amount, axis):
    return pltpu.roll(value, amount % value.shape[axis], axis)


def across(z0, z1):
    lanes = z0.shape[-1]
    lane = iota(z0.shape, z0.ndim - 1)
    first, last = lane == 0, lane == lanes - 1
    ax = z0.ndim - 1
    down0, down1 = spin(z0, 1, ax), spin(z1, 1, ax)
    up0, up1 = spin(z0, -1, ax), spin(z1, -1, ax)
    sum0 = jnp.where(first, 0.0, down0) + jnp.where(last, up1, up0)
    sum1 = jnp.where(first, down0, down1) + jnp.where(last, 0.0, up1)
    return sum0, sum1


def inplane(z0, z1):
    ax = z0.ndim - 2
    sum0, sum1 = across(z0, z1)
    sum0 = sum0 + (spin(z0, 1, ax) + spin(z0, -1, ax)) - 6.0 * z0
    sum1 = sum1 + (spin(z1, 1, ax) + spin(z1, -1, ax)) - 6.0 * z1
    return sum0, sum1


def row_scales(exponents):
    return jnp.exp2(exponents) * (1.0 / TOP)


def quantize(tiles_ref, out_ref):
    number = tiles_ref.shape[0]
    lane = iota(tiles_ref.shape[1:], 1)
    peak = jnp.zeros(tiles_ref.shape[1:], F32)
    for t in range(number):
        peak = jnp.where(lane == t, jnp.max(jnp.abs(tiles_ref[t]), axis=1, keepdims=True), peak)
    exponents = jnp.ceil(jnp.log2(jnp.maximum(peak, 1e-30)))
    factor = jnp.exp2(-exponents) * TOP

    def coded(t):
        scaled = jnp.round(tiles_ref[t] * factor[:, t:t + 1])
        return jnp.clip(scaled, -TOP, TOP).astype(jnp.int32)

    zero = jnp.zeros(tiles_ref.shape[1:], jnp.int32)
    parts = [coded(t) for t in range(number)] + [zero] * (number % 2)
    parts += [exponents.astype(jnp.int32), zero]
    for i in range(out_ref.shape[0]):
        out_ref[i] = jnp.concatenate(parts[2 * i:2 * i + 2], axis=0).astype(jnp.int16)


def coded_shape(number):
    return ((number + 1) // 2 + 1, 2 * HALO, LANES)


def scales_of(ref):
    return row_scales(ref[ref.shape[0] - 1].astype(jnp.int32)[0:HALO].astype(F32))


def expand(ref, tiles_ref, blocks):
    for at, scale in blocks:
        pair = ref[at].astype(jnp.int32).astype(F32)
        tiles_ref[2 * at] = pair[0:HALO] * scale[0]
        tiles_ref[2 * at + 1] = pair[HALO:] * scale[1]


def expand_all(ref, tiles_ref):
    scale = scales_of(ref)
    expand(ref, tiles_ref, [
        (i, (scale[:, 2 * i:2 * i + 1], scale[:, 2 * i + 1:2 * i + 2])) for i in range(tiles_ref.shape[0] // 2)
    ])


def prepare_kernel(
    panels_hbm, coupling_hbm, table_hbm, depth_hbm, owner_hbm, block_hbm, speed_hbm, un_hbm, up_hbm, lat_hbm,
    out_ref, un_ref, up_ref, lat_ref,
    panels_ref, coupling_ref, table_ref, depth_ref, owner_ref, block_ref, speed_ref, sems,
):
    pairs = (
        (panels_hbm, panels_ref), (table_hbm, table_ref), (coupling_hbm, coupling_ref),
        (depth_hbm, depth_ref), (owner_hbm, owner_ref), (block_hbm, block_ref), (speed_hbm, speed_ref),
        (un_hbm, un_ref), (up_hbm, up_ref), (lat_hbm, lat_ref),
    )
    copies = [pltpu.make_async_copy(src, dst, sems.at[i]) for i, (src, dst) in enumerate(pairs)]
    for copy in copies:
        copy.start()
    for copy in copies[:7]:
        copy.wait()
    count, rows, spectral = panels_ref.shape
    comps, block = 3, rows // 3
    lanes = table_ref.shape[1]
    free = jnp.dot(
        panels_ref[...].reshape(count * rows, spectral), table_ref[...], preferred_element_type=F32
    )
    weights = coupling_ref[...].reshape(rows, block)
    stacked = jnp.concatenate([weights] * NSTEP + [jnp.zeros((lanes - NSTEP * rows, block), F32)], axis=0)
    pick = ((iota((rows, block), 0) & (block - 1)) == iota((rows, block), 1)).astype(F32)
    spread = lax.dot_general(
        pick, stacked, (((1,), (1,)), ((), ())), precision=lax.Precision.HIGHEST, preferred_element_type=F32
    )
    comp_row = iota((rows, lanes), 0) >> shift_of(block)
    comp_lane = iota((rows, lanes), 1) >> shift_of(block)
    same = comp_lane == comp_row
    for step in range(1, NSTEP):
        same = same | (comp_lane == comp_row + step * comps)
    spread = jnp.where(same, spread, 0.0)
    out_ref[0:count] = jnp.sum(free.reshape(count, rows, lanes) * spread[None], axis=1)
    out_ref[count:] = jnp.zeros((out_ref.shape[0] - count, lanes), F32)
    speed = jnp.zeros(depth_ref.shape, F32)
    for layer in range(speed_ref.shape[0]):
        speed = jnp.where(depth_ref[...] == layer, speed_ref[layer], speed)
    pieces = [speed]
    for ref in (owner_ref, block_ref):
        twice = jnp.concatenate([ref[...], ref[...]], axis=1)
        pieces += [twice[:, i:i + LANES] for i in range(0, twice.shape[1], LANES)]
    for i, piece in enumerate(pieces):
        row, at = count + i * LANES // lanes, i * LANES % lanes
        out_ref[row:row + 1, at:at + LANES] = piece.astype(F32)
    for copy in copies[7:]:
        copy.wait()


def listed(ref, panels, which):
    lanes = ref.shape[1]
    width = -(-2 * panels // LANES)
    first, number = ((0, 1), (1, width), (1 + width, width))[which]
    out = []
    for i in range(first, first + number):
        row, at = PANELS + i * LANES // lanes, i * LANES % lanes
        out.append(ref[row:row + 1, at:at + LANES])
    return jnp.concatenate(out, axis=1)


def pack_kernel(
    scal_ref, un_ref, up_ref, lat_ref, uno_ref, upo_ref, lato_ref, ints_ref, intso_ref,
    coded_ref, pair_ref, out_ref,
):
    mine = scal_ref[2]
    high = lax.rem(scal_ref[1] + mine, 2) == 0
    comps, size_x, size_y, size_z = un_ref.shape
    tiles = comps * size_x
    shape = (size_x, HALO, size_z)
    sub = iota(shape, 1)

    def fill(side):
        base = size_y - HALO if side else 0
        for z_at, un, up, lat, ints in (
            (mine, un_ref, up_ref, lat_ref, ints_ref),
            (1 - mine, uno_ref, upo_ref, lato_ref, intso_ref),
        ):
            rate = lat[:, base:base + HALO, :] * listed(ints, LANES, 0)[None]
            for c in range(comps):
                now = un[c, :, base:base + HALO, :]
                old = spin(up[c, :, base:base + HALO, :], HALO // 2, 1)
                keep = sub >= HALO // 2 if side else sub < HALO // 2
                row = HALO - 1 - c if side else c
                tile = jnp.where(keep, now, old)
                tile = jnp.where(sub == (0 if side else HALO - 1), rate[:, row:row + 1, :], tile)
                out_ref[pl.ds(z_at * tiles + c * size_x, size_x)] = tile

    @pl.when(high)
    def _():
        fill(True)

    @pl.when(jnp.logical_not(high))
    def _():
        fill(False)

    count, lanes = PANELS, ints_ref.shape[1]
    for z_at, force in ((mine, ints_ref), (1 - mine, intso_ref)):
        pair_ref[z_at] = force[0:count]
        for part in range(lanes // size_z):
            for piece in range(count // HALO):
                at = 2 * tiles + (z_at * (lanes // size_z) + part) * (count // HALO) + piece
                out_ref[at] = force[piece * HALO:(piece + 1) * HALO, part * size_z:(part + 1) * size_z]
    quantize(out_ref, coded_ref)


def place_forces(scal_ref, sets, all_ref):
    if len(sets) == 1:
        return sets[0]
    own_ref, side_ref, sideo_ref, far_ref, faro_ref = sets
    o, mine = scal_ref[1], scal_ref[2]
    count, lanes = own_ref.shape[1:]
    beside, opposite, mirror = o + 1 - 2 * lax.rem(o, 2), lax.rem(o + 2, 4), 3 - o
    size_z = side_ref.shape[-1]
    tiles = side_ref.shape[0] - 2 * (lanes // size_z) * (count // HALO)
    here = mine == 0

    def spot(j):
        return pl.ds(pl.multiple_of(j * count, count), count)

    for ref, j in ((side_ref, jnp.where(here, beside, mirror)), (sideo_ref, jnp.where(here, mirror, beside))):
        for z in range(2):
            for part in range(lanes // size_z):
                at = tiles + (z * (lanes // size_z) + part) * (count // HALO)
                all_ref[z, spot(j), part * size_z:(part + 1) * size_z] = ref[
                    at:at + count // HALO
                ].reshape(count, size_z)
    for ref, j in (
        (far_ref, jnp.where(here, opposite, mirror)),
        (faro_ref, jnp.where(here, mirror, opposite)),
        (own_ref, o),
    ):
        for z in range(2):
            all_ref[z, spot(j), :] = ref[z]
    return all_ref


def panel_keys(ints_ref, o, panels, rows, size_x, size_y, zblocks):
    owner = listed(ints_ref, panels, 1).astype(jnp.int32)
    block = listed(ints_ref, panels, 2).astype(jnp.int32)
    depth = block & (zblocks - 1)
    y = (block >> shift_of(zblocks)) & (size_y - 1)
    x = block >> (shift_of(zblocks) + shift_of(size_y))
    key = x * rows
    reach = NSTEP - 1
    row = jnp.where(owner == o, y, -1)
    row = jnp.where((owner == o + 1) & (y < reach), y + size_y, row)
    row = jnp.where((owner == o - 1) & (y >= size_y - reach), y + rows - size_y, row)
    return jnp.where(row < 0, -1, key + row), depth


def spread_forces(force, depth, size_z, block, steps):
    high = force.astype(BF16).astype(F32)
    both = jnp.concatenate([high, force - high], axis=0)
    rows = both.shape[0]
    lane = iota((rows, size_z), 1) >> shift_of(block)
    base = (
        (iota((size_z, size_z), 0) & (block - 1)) == (iota((size_z, size_z), 1) & (block - 1))
    ).astype(BF16)
    at = (iota((size_z, rows), 0) >> shift_of(block)) == depth
    at = jnp.transpose(at.astype(F32))
    per_tile = size_z // block
    out = []
    for q in range(steps * 3):
        part = both[:, (q // per_tile) * size_z:(q // per_tile + 1) * size_z]
        part = jnp.where(lane == q % per_tile, part, 0.0).astype(BF16)
        wide = jnp.dot(part, base, preferred_element_type=F32)
        out.append((wide * at).astype(BF16))
    return jnp.concatenate(out, axis=1)


def halo_tiles(high, low):
    sub = iota(high.shape, high.ndim - 2)
    upper = sub < HALO // 2
    now = jnp.where(upper, high, low)
    old = spin(jnp.where(upper, low, high), HALO // 2, high.ndim - 2)
    return now, old


def halo_rate(highs, lows):
    sub = iota(highs[0].shape, highs[0].ndim - 2)
    tile = jnp.zeros(highs[0].shape, F32)
    ends = slice(HALO - 1, HALO), slice(0, 1)
    for c in range(3):
        tile = jnp.where(sub == c, highs[c][..., ends[0], :], tile)
        tile = jnp.where(sub == HALO - 1 - c, lows[c][..., ends[1], :], tile)
    return tile


def sides(scal_ref, side_ref, sideo_ref, at):
    o, mine = scal_ref[1], scal_ref[2]
    high = lax.rem(o + mine, 2) == 0
    one, two = side_ref[at], sideo_ref[at]
    upper = jnp.where(o < scal_ref[4] - 1, jnp.where(high, one, two), 0.0)
    lower = jnp.where(o > 0, jnp.where(high, two, one), 0.0)
    return upper, lower


def face_kernel(
    scal_ref, un_ref, up_ref, lat_ref, uno_ref, upo_ref, lato_ref, ints_ref, intso_ref,
    coded_ref, codedo_ref, *rest,
):
    *sets, out_ref, all_ref, side_ref, sideo_ref, faces_ref = rest
    comps, size_x, size_y, size_z = un_ref.shape
    rows = size_y + HALO
    tiles = comps * size_x
    a, o, mine = scal_ref[0], scal_ref[1], scal_ref[2]
    high = lax.rem(a + mine, 2) == 0
    skip = jnp.where(high, size_x - NSTEP, 0)
    for ref, tiles_ref in ((coded_ref, side_ref), (codedo_ref, sideo_ref)):
        scale = scales_of(ref)
        moved = pltpu.roll(scale, lax.rem(LANES - skip, LANES), 1)
        blocks = []
        for first in range(0, 2 * tiles, size_x):
            for i in range(first, first + NSTEP, 2):
                at = i // 2 + lax.div(skip, 2)
                blocks.append((at, (moved[:, i:i + 1], moved[:, i + 1:i + 2])))
        for i in range(2 * tiles, tiles_ref.shape[0], 2):
            blocks.append((i // 2, (scale[:, i:i + 1], scale[:, i + 1:i + 2])))
        expand(ref, tiles_ref, blocks)
    forces = place_forces(scal_ref, with_sides(sets, side_ref, sideo_ref), all_ref)
    panels = forces.shape[1]
    own = mine == 0
    now, old, rate, drive = {}, {}, {}, {}
    for z in range(2):
        keys, depth = panel_keys_of(z, own, ints_ref, intso_ref, o, panels, rows, size_x, size_y, size_z)
        wide = spread_forces(forces[z], depth, size_z, size_z // (size_z // 16), NSTEP - 1)
        first = jnp.where(high, size_x - NSTEP + 1, 0)
        node = iota(((NSTEP - 1) * rows, keys.shape[1]), 0) + first * rows
        hit = (node == keys).astype(F32).astype(BF16)
        got = jnp.dot(hit, wide, preferred_element_type=F32)
        got = got.reshape(NSTEP - 1, rows, wide.shape[1])
        for d in range(1, NSTEP):
            for n in range(NSTEP - d):
                for c in range(comps):
                    q = (n * comps + c) * size_z
                    drive[z, n, d, c] = jnp.where(
                        high, got[NSTEP - 1 - d, :, q:q + size_z], got[d - 1, :, q:q + size_z]
                    )
        speed = jnp.where(
            own if z == 0 else jnp.logical_not(own),
            listed(ints_ref, LANES, 0),
            listed(intso_ref, LANES, 0),
        )
        near = own if z == 0 else jnp.logical_not(own)
        for d in range(1, NSTEP + 1):
            x = jnp.where(high, size_x - d, d - 1)
            ups, lows = [], []
            for c in range(comps):
                upper, lower = sides(scal_ref, side_ref, sideo_ref, z * tiles + c * size_x + x)
                ups.append(upper)
                lows.append(lower)
                tile_now, tile_old = halo_tiles(upper, lower)
                centre = jnp.where(near, un_ref[c, x], uno_ref[c, x])
                now[z, d, c] = jnp.concatenate([centre, tile_now], axis=0)
                if d < NSTEP:
                    centre = jnp.where(near, up_ref[c, x], upo_ref[c, x])
                    old[z, d, c] = jnp.concatenate([centre, tile_old], axis=0)
            if d < NSTEP:
                centre = jnp.where(near, lat_ref[x], lato_ref[x]) * speed
                rate[z, d] = jnp.concatenate([centre, halo_rate(ups, lows)], axis=0)
    series = {(z, 0, c): now[z, 1, c] for z in range(2) for c in range(comps)}
    for n in range(1, NSTEP):
        later = {}
        for d in range(1, NSTEP - n + 1):
            for c in range(comps):
                sums = inplane(now[0, d, c], now[1, d, c])
                for z in range(2):
                    lap = sums[z] + now[z, d + 1, c]
                    if d > 1:
                        lap = lap + now[z, d - 1, c]
                    later[z, d, c] = (
                        2.0 * now[z, d, c] - old[z, d, c] + rate[z, d] * lap + drive[z, n - 1, d, c]
                    )
        old, now = now, later
        for z in range(2):
            for c in range(comps):
                series[z, n, c] = now[z, 1, c]
    sub = iota((HALO, size_z), 0)
    middle = (sub == HALO // 2 - 1) | (sub == HALO // 2)
    ends = (sub < 2) | (sub >= HALO - 2)
    for z in range(2):
        planes = [series[z, n, c] for n in range(NSTEP) for c in range(comps)] + [rate[z, 1], rate[z, 2]]
        rims = [plane[size_y:rows] for plane in planes]
        tails = [jnp.where(middle, spin(rims[2 * comps + c], HALO // 2, 0), rims[c]) for c in range(comps)]
        tails.append(jnp.where(ends, rims[comps], spin(rims[comps + 1], HALO // 2, 0)))
        tails.append(jnp.where(ends, rims[comps + 2], spin(rims[NSTEP * comps], HALO // 2, 0)))
        base = z * face_tiles(comps)
        for i, plane in enumerate(planes):
            for half in range(2):
                faces_ref[base + 2 * i + half] = plane[half * HALO:(half + 1) * HALO]
        for i, tail in enumerate(tails):
            faces_ref[base + 2 * len(planes) + i] = tail
    quantize(faces_ref, out_ref)


def face_tiles(comps):
    return 2 * (NSTEP * comps + 2) + comps + 2


def face_plane(tiles_ref, z, i, comps):
    count = NSTEP * comps + 2
    base = z * face_tiles(comps)
    tail = base + 2 * count
    parts = [tiles_ref[base + 2 * i], tiles_ref[base + 2 * i + 1]]
    turned = lambda at: spin(tiles_ref[at], HALO // 2, 0)
    if i < comps:
        parts.append(tiles_ref[tail + i])
    elif i < comps + 3:
        at, other = ((tail + comps, False), (tail + comps, True), (tail + comps + 1, False))[i - comps]
        parts.append(turned(at) if other else tiles_ref[at])
    elif 2 * comps <= i < 3 * comps:
        parts.append(turned(tail + i - 2 * comps))
    elif i == NSTEP * comps:
        parts.append(turned(tail + comps + 1))
    else:
        parts.append(jnp.zeros(parts[0].shape, F32))
    return jnp.concatenate(parts, axis=0)


def with_sides(sets, side_ref, sideo_ref):
    if len(sets) == 1:
        return sets
    own_ref, far_ref, faro_ref = sets
    return own_ref, side_ref, sideo_ref, far_ref, faro_ref


def panel_keys_of(z, own, ints_ref, intso_ref, o, panels, rows, size_x, size_y, size_z):
    near = own if z == 0 else jnp.logical_not(own)
    zblocks = size_z // 16
    mine = panel_keys(ints_ref, o, panels, rows, size_x, size_y, zblocks)
    theirs = panel_keys(intso_ref, o, panels, rows, size_x, size_y, zblocks)
    return tuple(jnp.where(near, one, two) for one, two in zip(mine, theirs))


def local_kernel(
    scal_ref, un_ref, up_ref, lat_ref, uno_ref, upo_ref, lato_ref, ints_ref, intso_ref,
    coded_ref, codedo_ref, *rest,
):
    *sets, final_ref, before_ref, face_ref, ratef_ref, all_ref, side_ref, sideo_ref = rest[:-4]
    now_ref, old_ref, rate_ref, drive_ref = rest[-4:]
    comps, size_x, size_y, size_z = un_ref.shape
    rows = size_y + HALO
    tiles = comps * size_x
    o, mine = scal_ref[1], scal_ref[2]
    expand_all(coded_ref, side_ref)
    expand_all(codedo_ref, sideo_ref)
    forces = place_forces(scal_ref, with_sides(sets, side_ref, sideo_ref), all_ref)
    panels = forces.shape[1]
    own = mine == 0
    for z in range(2):
        keys, depth = panel_keys_of(z, own, ints_ref, intso_ref, o, panels, rows, size_x, size_y, size_z)
        wide = spread_forces(forces[z], depth, size_z, 16, NSTEP)
        node = iota((size_x * rows, keys.shape[1]), 0)
        hit = (node == keys).astype(F32).astype(BF16)
        for n in range(NSTEP):
            span = comps * size_z
            got = jnp.dot(hit, wide[:, n * span:(n + 1) * span], preferred_element_type=F32)
            for c in range(comps):
                drive_ref[n, z, c] = got[:, c * size_z:(c + 1) * size_z].reshape(size_x, rows, size_z)
    edge = jnp.zeros((rows, size_z), F32)
    for z in range(2):
        for c in range(comps):
            for ref in (now_ref, old_ref):
                ref[z, c, 0] = edge
                ref[z, c, size_x + 1] = edge
    for z_at, un, up, lat, ints in (
        (mine, un_ref, up_ref, lat_ref, ints_ref),
        (1 - mine, uno_ref, upo_ref, lato_ref, intso_ref),
    ):
        speed = listed(ints, LANES, 0)
        ups, lows = [], []
        for c in range(comps):
            upper, lower = sides(scal_ref, side_ref, sideo_ref, pl.ds(z_at * tiles + c * size_x, size_x))
            ups.append(upper)
            lows.append(lower)
            tile_now, tile_old = halo_tiles(upper, lower)
            now_ref[z_at, c, 1:size_x + 1, 0:size_y] = un[c]
            now_ref[z_at, c, 1:size_x + 1, size_y:rows] = tile_now
            old_ref[z_at, c, 1:size_x + 1, 0:size_y] = up[c]
            old_ref[z_at, c, 1:size_x + 1, size_y:rows] = tile_old
        rate_ref[z_at, :, 0:size_y] = lat[...] * speed[None]
        rate_ref[z_at, :, size_y:rows] = halo_rate(ups, lows)
    for side in range(2):
        for z in range(2):
            for d in range(NSTEP):
                ratef_ref[side, z, d] = rate_ref[z, d if side else size_x - 1 - d]
    refs = [now_ref, old_ref]
    for n in range(NSTEP):
        now, old = refs[n % 2], refs[(n + 1) % 2]
        for side in range(2):
            for z in range(2):
                for c in range(comps):
                    face_ref[side, z, n * comps + c] = now[z, c, 1 if side else size_x]

        def step(x, carry):
            for c in range(comps):
                centre = now[0, c, x + 1], now[1, c, x + 1]
                sums = inplane(*centre)
                for z in range(2):
                    lap = sums[z] + (now[z, c, x] + now[z, c, x + 2])
                    old[z, c, x + 1] = (
                        2.0 * centre[z] - old[z, c, x + 1] + rate_ref[z, x] * lap + drive_ref[n, z, c, x]
                    )
            return carry

        lax.fori_loop(0, size_x, step, 0, unroll=4)
    now, old = refs[NSTEP % 2], refs[(NSTEP + 1) % 2]
    for c in range(comps):
        final_ref[c] = now[mine, c, 1:size_x + 1, 0:size_y]
        before_ref[c] = old[mine, c, 1:size_x + 1, 0:size_y]


def join_kernel(
    scal_ref, final_in, before_in, face_ref, ratef_ref, coded_ref, codedo_ref, final_ref, before_ref,
    recv_ref, recvo_ref,
):
    comps, size_x, size_y, size_z = final_in.shape
    a, mine = scal_ref[0], scal_ref[2]
    own = mine == 0
    high = lax.rem(a + mine, 2) == 0
    expand_all(coded_ref, recv_ref)
    expand_all(codedo_ref, recvo_ref)
    final_ref[...] = final_in[...]
    before_ref[...] = before_in[...]
    for side in range(2):
        is_high = side == 0
        here = high if is_high else jnp.logical_not(high)
        inside = a < scal_ref[3] - 1 if is_high else a > 0

        def theirs(z, at):
            return jnp.where(inside, jnp.where(here, face_plane(recv_ref, z, at, comps), face_plane(recvo_ref, z, at, comps)), 0.0)

        rate = {}
        for z in range(2):
            for m in range(NSTEP):
                rate[z, -m] = ratef_ref[side, z, m]
            for m in (1, 2):
                rate[z, m] = theirs(z, NSTEP * comps + m - 1)
        for c in range(comps):
            last, now = {}, {}
            for n in range(NSTEP):
                later = {}
                top = min(n + 1, NSTEP - 1 - n)
                for m in range(-n, top + 1):
                    centre = [now.get((z, m)) for z in range(2)]
                    sums = inplane(*centre) if centre[0] is not None else (None, None)
                    for z in range(2):
                        terms = [sums[z], now.get((z, m - 1)), now.get((z, m + 1))]
                        if m == 0:
                            terms.append(theirs(z, n * comps + c))
                        if m == 1:
                            terms.append(face_ref[side, z, n * comps + c])
                        terms = [t for t in terms if t is not None]
                        lap = functools.reduce(lambda p, q: p + q, terms)
                        value = rate[z, m] * lap
                        if centre[z] is not None:
                            value = value + 2.0 * centre[z]
                        if (z, m) in last:
                            value = value - last[z, m]
                        later[z, m] = value
                last, now = now, later
            for target, values in ((final_ref, now), (before_ref, last)):
                for m in range(0, -NSTEP, -1):
                    if (0, m) not in values:
                        continue
                    x = size_x - 1 + m if is_high else -m
                    add = jnp.where(own, values[0, m], values[1, m])[0:size_y]
                    target[c, x] = target[c, x] + add


def send(value, mesh_sizes, route):
    nx, ny, nz = mesh_sizes
    number = lambda i, j, k: (i * ny + j) * nz + k
    pairs = [
        (number(i, j, k), number(*route(i, j, k))) for i in range(nx) for j in range(ny) for k in range(nz)
    ]
    return lax.ppermute(value, ("gx", "gy", "gz"), pairs)


def partner(i, core, count):
    step = 1 if (i + core) % 2 == 0 else -1
    return (i + step) % count


def per_device(
    u_now, u_prev, panels, panel_owner, panel_block, coupling, layer_depth, layer_speed, lateral
):
    sizes = tuple(lax.axis_size(axis) for axis in ("gx", "gy", "gz"))
    nx, ny, nz = sizes
    assert nx % 2 == 0 and ny % 2 == 0 and nz == 2
    comps, size_x, size_y, size_z = u_now.shape
    rows = size_y + HALO
    per_dev, spectral = panels.shape[2], panels.shape[4]
    npanels = ny * per_dev
    scal = jnp.stack(
        [lax.axis_index("gx"), lax.axis_index("gy"), lax.axis_index("gz"), jnp.int32(nx), jnp.int32(ny)]
    ).astype(jnp.int32)

    def swap(value):
        return send(value, sizes, lambda i, j, k: (i, j, 1 - k))

    def route_x(i, j, k):
        return partner(i, k, nx), j, k

    def route_y(i, j, k):
        to = partner(j, k, ny)
        if abs(to - j) != 1 or (ny == 2 and k == 1):
            return i ^ 1, j, k
        return i, to, k

    assert per_dev == PANELS and size_z == LANES
    un_o, up_o, lat_o = swap(u_now), swap(u_prev), swap(lateral)

    vmem = pl.BlockSpec(memory_space=pltpu.VMEM)
    smem = pl.BlockSpec(memory_space=pltpu.SMEM)
    params = pltpu.CompilerParams(vmem_limit_bytes=48 * 1024 * 1024)
    table = jnp.asarray(wave_table(spectral, panels.shape[3]))
    width = table.shape[1]
    number = LANES + 4 * npanels
    extra_rows = -(-(-(-number // width)) // 8) * 8
    ints, un_v, up_v, lat_v = pl.pallas_call(
        prepare_kernel,
        out_shape=(
            jax.ShapeDtypeStruct((per_dev + extra_rows, width), F32),
            jax.ShapeDtypeStruct(u_now.shape, F32),
            jax.ShapeDtypeStruct(u_prev.shape, F32),
            jax.ShapeDtypeStruct(lateral.shape, F32),
        ),
        in_specs=[pl.BlockSpec(memory_space=pl.ANY)] * 10,
        out_specs=(vmem,) * 4,
        scratch_shapes=[
            pltpu.VMEM((per_dev,) + panels.shape[3:], BF16),
            pltpu.VMEM(coupling.shape, F32),
            pltpu.VMEM(table.shape, BF16),
            pltpu.VMEM((1, size_z), jnp.int32),
            pltpu.VMEM((1, npanels), jnp.int32),
            pltpu.VMEM((1, npanels), jnp.int32),
            pltpu.SMEM(layer_speed.shape, F32),
            pltpu.SemaphoreType.DMA((10,)),
        ],
        compiler_params=params,
        name="prepare",
    )(*(
        pltpu.with_memory_space_constraint(value, pltpu.HBM)
        for value in (
            panels.reshape((per_dev,) + panels.shape[3:]), coupling, table, layer_depth.reshape(1, -1),
            panel_owner.reshape(1, -1), panel_block.reshape(1, -1), layer_speed, u_now, u_prev, lateral,
        )
    ))
    ints_o = swap(ints)
    tiles = comps * size_x
    extra = 2 * (width // size_z) * (per_dev // HALO)
    state = (scal, un_v, up_v, lat_v, un_o, up_o, lat_o, ints, ints_o)
    state_specs = [smem] + [vmem] * 8
    tiles_scratch = pltpu.VMEM((2 * tiles + extra, HALO, size_z), F32)
    packed, pair = pl.pallas_call(
        pack_kernel,
        out_shape=(
            jax.ShapeDtypeStruct(coded_shape(2 * tiles + extra), jnp.int16),
            jax.ShapeDtypeStruct((2, per_dev, width), F32),
        ),
        in_specs=state_specs,
        out_specs=(vmem, vmem),
        scratch_shapes=[tiles_scratch],
        compiler_params=params,
        name="pack",
    )(*state)
    side = send(packed, sizes, route_y)
    if ny == 4:
        far = send(pair, sizes, lambda i, j, k: (i, j ^ 2 if k == 0 else 3 - j, k))
        side, far = lax.optimization_barrier((side, far))
        side_o, far_o = swap(side), swap(far)
        sets = (pair, far, far_o)
    else:
        side_o = swap(side)
        sets = (jnp.moveaxis(lax.all_gather(pair, "gy"), 0, 1).reshape(2, npanels, -1),)
    shared = state + (side, side_o) + sets
    shared_specs = state_specs + [vmem] * (2 + len(sets))
    all_scratch = pltpu.VMEM((2, npanels, width), F32)
    planes = NSTEP * comps
    face_scratch = pltpu.VMEM((2 * face_tiles(comps), HALO, size_z), F32)
    sent = pl.pallas_call(
        face_kernel,
        out_shape=jax.ShapeDtypeStruct(coded_shape(2 * face_tiles(comps)), jnp.int16),
        in_specs=shared_specs,
        out_specs=vmem,
        scratch_shapes=[all_scratch, tiles_scratch, tiles_scratch, face_scratch],
        compiler_params=params,
        name="face",
    )(*shared)
    recv = send(sent, sizes, route_x)
    final, before, face, ratef = pl.pallas_call(
        local_kernel,
        out_shape=(
            jax.ShapeDtypeStruct(u_now.shape, F32),
            jax.ShapeDtypeStruct(u_now.shape, F32),
            jax.ShapeDtypeStruct((2, 2, planes, rows, size_z), F32),
            jax.ShapeDtypeStruct((2, 2, NSTEP, rows, size_z), F32),
        ),
        in_specs=shared_specs,
        out_specs=(vmem,) * 4,
        scratch_shapes=[
            all_scratch,
            tiles_scratch,
            tiles_scratch,
            pltpu.VMEM((2, comps, size_x + 2, rows, size_z), F32),
            pltpu.VMEM((2, comps, size_x + 2, rows, size_z), F32),
            pltpu.VMEM((2, size_x, rows, size_z), F32),
            pltpu.VMEM((NSTEP, 2, comps, size_x, rows, size_z), F32),
        ],
        compiler_params=params,
        name="local",
    )(*shared)
    final, before, face, ratef, recv = lax.optimization_barrier((final, before, face, ratef, recv))
    recv_o = swap(recv)
    return pl.pallas_call(
        join_kernel,
        out_shape=(
            jax.ShapeDtypeStruct(u_now.shape, F32),
            jax.ShapeDtypeStruct(u_now.shape, F32),
        ),
        in_specs=[smem] + [vmem] * 6,
        out_specs=(vmem, vmem),
        scratch_shapes=[face_scratch, face_scratch],
        compiler_params=params,
        name="join",
    )(scal, final, before, face, ratef, recv, recv_o)


def solution(mesh):
    in_specs = (
        P(None, "gx", "gy", "gz"),
        P(None, "gx", "gy", "gz"),
        P("gx", "gz", "gy", None, None),
        P("gx", "gz", None, None),
        P("gx", "gz", None),
        P(),
        P("gz"),
        P(),
        P("gx", "gy", "gz"),
    )
    out_specs = (P(None, "gx", "gy", "gz"), P(None, "gx", "gy", "gz"))
    return jax.shard_map(
        per_device, mesh=mesh, in_specs=in_specs, out_specs=out_specs, check_vma=False
    )
```

```python
import functools

import jax
import jax.numpy as jnp
import ml_dtypes
import numpy as np
from jax import lax
from jax.experimental import pallas as pl
from jax.experimental.pallas import tpu as pltpu
from jax.sharding import PartitionSpec as P

NSTEP = 4
HALO = 8
LANES = 128
PANELS = 16
TOP = 32000.0
F32 = jnp.float32
BF16 = jnp.bfloat16


def wave_table(count, per_step):
    half = count // 2
    freq = np.float32(2.0 * np.pi) * (np.arange(half, dtype=np.float32) + np.float32(0.5)) / np.float32(count)
    times = np.float32(37.0) + np.arange(NSTEP, dtype=np.float32)
    phase = freq[:, None] * times[None, :]
    table = np.concatenate([np.cos(phase), np.sin(phase)], axis=0) / np.sqrt(np.float32(half))
    wide = np.repeat(table.astype(ml_dtypes.bfloat16), per_step, axis=1)
    return np.pad(wide, ((0, 0), (0, -wide.shape[1] % 128)))


def shift_of(size):
    assert size & (size - 1) == 0
    return size.bit_length() - 1


def iota(shape, dim):
    return lax.broadcasted_iota(jnp.int32, shape, dim)


def spin(value, amount, axis):
    return pltpu.roll(value, amount % value.shape[axis], axis)


def across(z0, z1):
    lanes = z0.shape[-1]
    lane = iota(z0.shape, z0.ndim - 1)
    first, last = lane == 0, lane == lanes - 1
    ax = z0.ndim - 1
    down0, down1 = spin(z0, 1, ax), spin(z1, 1, ax)
    up0, up1 = spin(z0, -1, ax), spin(z1, -1, ax)
    sum0 = jnp.where(first, 0.0, down0) + jnp.where(last, up1, up0)
    sum1 = jnp.where(first, down0, down1) + jnp.where(last, 0.0, up1)
    return sum0, sum1


def inplane(z0, z1):
    ax = z0.ndim - 2
    sum0, sum1 = across(z0, z1)
    sum0 = sum0 + (spin(z0, 1, ax) + spin(z0, -1, ax)) - 6.0 * z0
    sum1 = sum1 + (spin(z1, 1, ax) + spin(z1, -1, ax)) - 6.0 * z1
    return sum0, sum1


def row_scales(exponents):
    return jnp.exp2(exponents) * (1.0 / TOP)


def quantize(load, groups, out_ref):
    shape = (HALO, LANES)
    lane = iota(shape, 1)
    peak = jnp.zeros(shape, F32)
    for group in range(max(groups) + 1):
        members = [jnp.abs(load(t)) for t, of in enumerate(groups) if of == group]
        top = functools.reduce(jnp.maximum, members)
        peak = jnp.where(lane == group, jnp.max(top, axis=1, keepdims=True), peak)
    exponents = jnp.ceil(jnp.log2(jnp.maximum(peak, 1e-30)))
    factor = jnp.exp2(-exponents) * TOP
    zero = jnp.zeros(shape, jnp.int32)
    wide = [jnp.broadcast_to(factor[:, g:g + 1], shape) for g in range(max(groups) + 1)]
    parts = [jnp.round(load(t) * wide[of]).astype(jnp.int32) for t, of in enumerate(groups)]
    parts += [zero] * (len(groups) % 2) + [exponents.astype(jnp.int32), zero]
    for i in range(out_ref.shape[0]):
        out_ref[i] = jnp.concatenate(parts[2 * i:2 * i + 2], axis=0).astype(jnp.int16)


def coded_shape(number):
    return ((number + 1) // 2 + 1, 2 * HALO, LANES)


def side_groups(comps, size_x, rest):
    near = [c * (size_x // NSTEP) + x // NSTEP for c in range(comps) for x in range(size_x)]
    return near + [max(near) + 1 + i for i in range(rest)]


def scales_of(coded):
    return row_scales(coded.astype(jnp.int32)[0:HALO].astype(F32))


def expand(load, store, scales, blocks):
    for at, one, two in blocks:
        pair = load(at).astype(jnp.int32).astype(F32)
        store(2 * at, pair[0:HALO] * scales[:, one:one + 1])
        store(2 * at + 1, pair[HALO:] * scales[:, two:two + 1])


def expand_all(ref, tiles_ref, groups):
    def store(t, value):
        tiles_ref[t] = value

    expand(lambda i: ref[i], store, scales_of(ref[ref.shape[0] - 1]), [
        (t // 2, groups[t], groups[t + 1]) for t in range(0, len(groups), 2)
    ])


def expand_sides(ref, tiles_ref, first, choose):
    for half in range(2):
        z = first if half == 0 else 1 - first

        def store(t, value):
            tiles_ref[z, t] = value

        scales = scales_of(ref[half, ref.shape[1] - 1])
        for moved, blocks in choose(scales):
            expand(lambda i: ref[half, i], store, moved, blocks)


def prepare_kernel(
    scal_ref, panels_hbm, coupling_hbm, table_hbm, depth_hbm, owner_hbm, block_hbm, speed_hbm,
    un_hbm, up_hbm, lat_hbm, out_ref, state_ref, mine_ref, theirs_ref, tiles_ref,
    panels_ref, coupling_ref, table_ref, depth_ref, owner_ref, block_ref, speed_ref, sems,
):
    comps = un_hbm.shape[0]
    un_ref, up_ref, lat_ref = state_ref.at[0:comps], state_ref.at[comps:2 * comps], state_ref.at[2 * comps]
    pairs = (
        (panels_hbm, panels_ref), (table_hbm, table_ref), (coupling_hbm, coupling_ref),
        (depth_hbm, depth_ref), (owner_hbm, owner_ref), (block_hbm, block_ref), (speed_hbm, speed_ref),
        (un_hbm, un_ref), (up_hbm, up_ref), (lat_hbm, lat_ref),
    )
    copies = [pltpu.make_async_copy(src, dst, sems.at[i]) for i, (src, dst) in enumerate(pairs)]
    for copy in copies:
        copy.start()
    for copy in copies[:7]:
        copy.wait()
    count, rows, spectral = panels_ref.shape
    block = rows // comps
    lanes = table_ref.shape[1]
    free = jnp.dot(
        panels_ref[...].reshape(count * rows, spectral), table_ref[...], preferred_element_type=F32
    )
    weights = coupling_ref[...].reshape(rows, block)
    stacked = jnp.concatenate([weights] * NSTEP + [jnp.zeros((lanes - NSTEP * rows, block), F32)], axis=0)
    pick = ((iota((rows, block), 0) & (block - 1)) == iota((rows, block), 1)).astype(F32)
    spread = lax.dot_general(
        pick, stacked, (((1,), (1,)), ((), ())), precision=lax.Precision.HIGHEST, preferred_element_type=F32
    )
    comp_row = iota((rows, lanes), 0) >> shift_of(block)
    comp_lane = iota((rows, lanes), 1) >> shift_of(block)
    same = comp_lane == comp_row
    for step in range(1, NSTEP):
        same = same | (comp_lane == comp_row + step * comps)
    spread = jnp.where(same, spread, 0.0)
    out_ref[0:count] = jnp.sum(free.reshape(count, rows, lanes) * spread[None], axis=1)
    out_ref[count:] = jnp.zeros((out_ref.shape[0] - count, lanes), F32)
    speed = jnp.zeros(depth_ref.shape, F32)
    for layer in range(speed_ref.shape[0]):
        speed = jnp.where(depth_ref[...] == layer, speed_ref[layer], speed)
    pieces = [speed]
    for ref in (owner_ref, block_ref):
        twice = jnp.concatenate([ref[...], ref[...]], axis=1)
        pieces += [twice[:, i:i + LANES] for i in range(0, twice.shape[1], LANES)]
    for i, piece in enumerate(pieces):
        row, at = count + i * LANES // lanes, i * LANES % lanes
        out_ref[row:row + 1, at:at + LANES] = piece.astype(F32)
    for copy in copies[7:]:
        copy.wait()
    comps, size_x, size_y, size_z = un_ref.shape
    sub = iota((size_x, HALO, size_z), 1)
    for side in range(2):
        base = 0 if side else size_y - HALO
        rate = lat_ref[:, base:base + HALO, :] * speed[None]
        for c in range(comps):
            now = un_ref[c, :, base:base + HALO, :]
            old = spin(up_ref[c, :, base:base + HALO, :], HALO // 2, 1)
            keep = sub < HALO // 2 if side else sub >= HALO // 2
            row = c if side else HALO - 1 - c
            tile = jnp.where(keep, now, old)
            tile = jnp.where(sub == (HALO - 1 if side else 0), rate[:, row:row + 1, :], tile)
            tiles_ref[side, c * size_x:(c + 1) * size_x] = tile
        for part in range(lanes // size_z):
            for piece in range(count // HALO):
                at = comps * size_x + part * (count // HALO) + piece
                tiles_ref[side, at] = out_ref[piece * HALO:(piece + 1) * HALO, part * size_z:(part + 1) * size_z]
    low = lax.rem(scal_ref[1] + scal_ref[2], 2)
    groups = side_groups(comps, size_x, tiles_ref.shape[1] - comps * size_x)
    quantize(lambda t: tiles_ref[low, t], groups, mine_ref)
    quantize(lambda t: tiles_ref[1 - low, t], groups, theirs_ref)


def listed(ref, panels, which):
    lanes = ref.shape[1]
    width = -(-2 * panels // LANES)
    first, number = ((0, 1), (1, width), (1 + width, width))[which]
    out = []
    for i in range(first, first + number):
        row, at = PANELS + i * LANES // lanes, i * LANES % lanes
        out.append(ref[row:row + 1, at:at + LANES])
    return jnp.concatenate(out, axis=1)


def gather_kernel(mine_ref, theirs_ref, ints_ref, intso_ref, both_ref, pair_ref):
    both_ref[0] = mine_ref[...]
    both_ref[1] = theirs_ref[...]
    pair_ref[0] = ints_ref[0:PANELS]
    pair_ref[1] = intso_ref[0:PANELS]


def place_forces(scal_ref, sets, all_ref):
    if len(sets) == 1:
        return sets[0]
    own_ref, side_ref, sideo_ref, far_ref, faro_ref = sets
    o, mine = scal_ref[1], scal_ref[2]
    count, lanes = own_ref.shape[1:]
    beside, opposite, mirror = o + 1 - 2 * lax.rem(o, 2), lax.rem(o + 2, 4), 3 - o
    size_z = side_ref.shape[-1]
    step = count // HALO
    tiles = side_ref.shape[1] - lanes // size_z * step
    here = mine == 0

    def spot(j):
        return pl.ds(pl.multiple_of(j * count, count), count)

    for ref, j in ((side_ref, jnp.where(here, beside, mirror)), (sideo_ref, jnp.where(here, mirror, beside))):
        for z in range(2):
            for part in range(lanes // size_z):
                at = tiles + part * step
                all_ref[z, spot(j), part * size_z:(part + 1) * size_z] = ref[z, at:at + step].reshape(count, size_z)
    for ref, j, first in (
        (far_ref, jnp.where(here, opposite, mirror), mine),
        (faro_ref, jnp.where(here, mirror, opposite), 1 - mine),
        (own_ref, o, mine),
    ):
        all_ref[first, spot(j), :] = ref[0]
        all_ref[1 - first, spot(j), :] = ref[1]
    return all_ref


def panel_keys(ints_ref, o, panels, rows, size_x, size_y, zblocks):
    owner = listed(ints_ref, panels, 1).astype(jnp.int32)
    block = listed(ints_ref, panels, 2).astype(jnp.int32)
    depth = block & (zblocks - 1)
    y = (block >> shift_of(zblocks)) & (size_y - 1)
    x = block >> (shift_of(zblocks) + shift_of(size_y))
    key = x * rows
    reach = NSTEP - 1
    row = jnp.where(owner == o, y, -1)
    row = jnp.where((owner == o + 1) & (y < reach), y + size_y, row)
    row = jnp.where((owner == o - 1) & (y >= size_y - reach), y + rows - size_y, row)
    return jnp.where(row < 0, -1, key + row), depth


def spread_forces(force, depth, size_z, block, steps):
    high = force.astype(BF16).astype(F32)
    both = jnp.concatenate([high, force - high], axis=0)
    rows = both.shape[0]
    lane = iota((rows, size_z), 1) >> shift_of(block)
    base = (
        (iota((size_z, size_z), 0) & (block - 1)) == (iota((size_z, size_z), 1) & (block - 1))
    ).astype(BF16)
    at = (iota((size_z, rows), 0) >> shift_of(block)) == depth
    at = jnp.transpose(at.astype(F32))
    per_tile = size_z // block
    out = []
    for q in range(steps * 3):
        part = both[:, (q // per_tile) * size_z:(q // per_tile + 1) * size_z]
        part = jnp.where(lane == q % per_tile, part, 0.0).astype(BF16)
        wide = jnp.dot(part, base, preferred_element_type=F32)
        out.append((wide * at).astype(BF16))
    return jnp.concatenate(out, axis=1)


def fields(state_ref):
    comps = state_ref.shape[0] // 2
    return state_ref.at[0:comps], state_ref.at[comps:2 * comps], state_ref.at[2 * comps]


def halo_tiles(high, low):
    sub = iota(high.shape, high.ndim - 2)
    upper = sub < HALO // 2
    now = jnp.where(upper, high, low)
    old = spin(jnp.where(upper, low, high), HALO // 2, high.ndim - 2)
    return now, old


def halo_rate(highs, lows):
    sub = iota(highs[0].shape, highs[0].ndim - 2)
    tile = jnp.zeros(highs[0].shape, F32)
    ends = slice(HALO - 1, HALO), slice(0, 1)
    for c in range(3):
        tile = jnp.where(sub == c, highs[c][..., ends[0], :], tile)
        tile = jnp.where(sub == HALO - 1 - c, lows[c][..., ends[1], :], tile)
    return tile


def sides(scal_ref, side_ref, sideo_ref, at):
    o, mine = scal_ref[1], scal_ref[2]
    high = lax.rem(o + mine, 2) == 0
    one, two = side_ref[at], sideo_ref[at]
    upper = jnp.where(o < scal_ref[4] - 1, jnp.where(high, one, two), 0.0)
    lower = jnp.where(o > 0, jnp.where(high, two, one), 0.0)
    return upper, lower


def face_kernel(
    scal_ref, state_ref, stateo_ref, ints_ref, intso_ref,
    coded_ref, codedo_ref, *rest,
):
    *sets, out_ref, all_ref, side_ref, sideo_ref, faces_ref = rest
    (un_ref, up_ref, lat_ref), (uno_ref, upo_ref, lato_ref) = fields(state_ref), fields(stateo_ref)
    comps, size_x, size_y, size_z = un_ref.shape
    rows = size_y + HALO
    tiles = comps * size_x
    a, o, mine = scal_ref[0], scal_ref[1], scal_ref[2]
    high = lax.rem(a + mine, 2) == 0
    skip = jnp.where(high, size_x - NSTEP, 0)

    groups = side_groups(comps, size_x, side_ref.shape[1] - tiles)

    def choose(scales):
        moved = pltpu.roll(scales, lax.rem(LANES - lax.div(skip, NSTEP), LANES), 1)
        near = [first + i for first in range(0, tiles, size_x) for i in range(0, NSTEP, 2)]
        rest = [(t // 2, groups[t], groups[t + 1]) for t in range(tiles, len(groups), 2)]
        return (moved, [(t // 2 + lax.div(skip, 2), groups[t], groups[t + 1]) for t in near]), (scales, rest)

    expand_sides(coded_ref, side_ref, mine, choose)
    expand_sides(codedo_ref, sideo_ref, 1 - mine, choose)
    forces = place_forces(scal_ref, with_sides(sets, side_ref, sideo_ref), all_ref)
    panels = forces.shape[1]
    own = mine == 0
    now, old, rate, drive = {}, {}, {}, {}
    for z in range(2):
        keys, depth = panel_keys_of(z, own, ints_ref, intso_ref, o, panels, rows, size_x, size_y, size_z)
        wide = spread_forces(forces[z], depth, size_z, size_z // (size_z // 16), NSTEP - 1)
        first = jnp.where(high, size_x - NSTEP + 1, 0)
        node = iota(((NSTEP - 1) * rows, keys.shape[1]), 0) + first * rows
        hit = (node == keys).astype(F32).astype(BF16)
        got = jnp.dot(hit, wide, preferred_element_type=F32)
        got = got.reshape(NSTEP - 1, rows, wide.shape[1])
        for d in range(1, NSTEP):
            for n in range(NSTEP - d):
                for c in range(comps):
                    q = (n * comps + c) * size_z
                    drive[z, n, d, c] = jnp.where(
                        high, got[NSTEP - 1 - d, :, q:q + size_z], got[d - 1, :, q:q + size_z]
                    )
        speed = jnp.where(
            own if z == 0 else jnp.logical_not(own),
            listed(ints_ref, LANES, 0),
            listed(intso_ref, LANES, 0),
        )
        near = own if z == 0 else jnp.logical_not(own)
        for d in range(1, NSTEP + 1):
            x = jnp.where(high, size_x - d, d - 1)
            ups, lows = [], []
            for c in range(comps):
                upper, lower = sides(scal_ref, side_ref, sideo_ref, (z, c * size_x + x))
                ups.append(upper)
                lows.append(lower)
                tile_now, tile_old = halo_tiles(upper, lower)
                centre = jnp.where(near, un_ref[c, x], uno_ref[c, x])
                now[z, d, c] = jnp.concatenate([centre, tile_now], axis=0)
                if d < NSTEP:
                    centre = jnp.where(near, up_ref[c, x], upo_ref[c, x])
                    old[z, d, c] = jnp.concatenate([centre, tile_old], axis=0)
            if d < NSTEP:
                centre = jnp.where(near, lat_ref[x], lato_ref[x]) * speed
                rate[z, d] = jnp.concatenate([centre, halo_rate(ups, lows)], axis=0)
    series = {(z, 0, c): now[z, 1, c] for z in range(2) for c in range(comps)}
    for n in range(1, NSTEP):
        later = {}
        for d in range(1, NSTEP - n + 1):
            for c in range(comps):
                sums = inplane(now[0, d, c], now[1, d, c])
                for z in range(2):
                    lap = sums[z] + now[z, d + 1, c]
                    if d > 1:
                        lap = lap + now[z, d - 1, c]
                    later[z, d, c] = (
                        2.0 * now[z, d, c] - old[z, d, c] + rate[z, d] * lap + drive[z, n - 1, d, c]
                    )
        old, now = now, later
        for z in range(2):
            for c in range(comps):
                series[z, n, c] = now[z, 1, c]
    sub = iota((HALO, size_z), 0)
    middle = (sub == HALO // 2 - 1) | (sub == HALO // 2)
    ends = (sub < 2) | (sub >= HALO - 2)
    for z in range(2):
        planes = [series[z, n, c] for n in range(NSTEP) for c in range(comps)] + [rate[z, 1], rate[z, 2]]
        rims = [plane[size_y:rows] for plane in planes]
        tails = [jnp.where(middle, spin(rims[2 * comps + c], HALO // 2, 0), rims[c]) for c in range(comps)]
        tails.append(jnp.where(ends, rims[comps], spin(rims[comps + 1], HALO // 2, 0)))
        tails.append(jnp.where(ends, rims[comps + 2], spin(rims[NSTEP * comps], HALO // 2, 0)))
        base = z * face_tiles(comps)
        for i, plane in enumerate(planes):
            for half in range(2):
                faces_ref[base + 2 * i + half] = plane[half * HALO:(half + 1) * HALO]
        for i, tail in enumerate(tails):
            faces_ref[base + 2 * len(planes) + i] = tail
    quantize(lambda t: faces_ref[t], face_groups(comps), out_ref)


def face_tiles(comps):
    return 2 * (NSTEP * comps + 2) + comps + 2


def face_groups(comps):
    groups = []
    for z in range(2):
        base = z * (2 * NSTEP + 5)
        groups += [base + 2 * n + half for n in range(NSTEP) for _ in range(comps) for half in range(2)]
        groups += [base + 2 * NSTEP + half for _ in range(2) for half in range(2)]
        groups += [base + 2 * NSTEP + 2] * comps + [base + 2 * NSTEP + 3, base + 2 * NSTEP + 4]
    return groups


def face_plane(tiles_ref, z, i, comps):
    count = NSTEP * comps + 2
    base = z * face_tiles(comps)
    tail = base + 2 * count
    parts = [tiles_ref[base + 2 * i], tiles_ref[base + 2 * i + 1]]
    turned = lambda at: spin(tiles_ref[at], HALO // 2, 0)
    if i < comps:
        parts.append(tiles_ref[tail + i])
    elif i < comps + 3:
        at, other = ((tail + comps, False), (tail + comps, True), (tail + comps + 1, False))[i - comps]
        parts.append(turned(at) if other else tiles_ref[at])
    elif 2 * comps <= i < 3 * comps:
        parts.append(turned(tail + i - 2 * comps))
    elif i == NSTEP * comps:
        parts.append(turned(tail + comps + 1))
    else:
        parts.append(jnp.zeros(parts[0].shape, F32))
    return jnp.concatenate(parts, axis=0)


def with_sides(sets, side_ref, sideo_ref):
    if len(sets) == 1:
        return sets
    own_ref, far_ref, faro_ref = sets
    return own_ref, side_ref, sideo_ref, far_ref, faro_ref


def panel_keys_of(z, own, ints_ref, intso_ref, o, panels, rows, size_x, size_y, size_z):
    near = own if z == 0 else jnp.logical_not(own)
    zblocks = size_z // 16
    mine = panel_keys(ints_ref, o, panels, rows, size_x, size_y, zblocks)
    theirs = panel_keys(intso_ref, o, panels, rows, size_x, size_y, zblocks)
    return tuple(jnp.where(near, one, two) for one, two in zip(mine, theirs))


def local_kernel(
    scal_ref, state_ref, stateo_ref, ints_ref, intso_ref,
    coded_ref, codedo_ref, *rest,
):
    *sets, final_ref, before_ref, face_ref, ratef_ref, all_ref, side_ref, sideo_ref = rest[:-4]
    now_ref, old_ref, rate_ref, drive_ref = rest[-4:]
    (un_ref, up_ref, lat_ref), (uno_ref, upo_ref, lato_ref) = fields(state_ref), fields(stateo_ref)
    comps, size_x, size_y, size_z = un_ref.shape
    rows = size_y + HALO
    tiles = comps * size_x
    o, mine = scal_ref[1], scal_ref[2]
    groups = side_groups(comps, size_x, side_ref.shape[1] - comps * size_x)
    choose = lambda scales: (
        (scales, [(t // 2, groups[t], groups[t + 1]) for t in range(0, len(groups), 2)]),
    )
    expand_sides(coded_ref, side_ref, mine, choose)
    expand_sides(codedo_ref, sideo_ref, 1 - mine, choose)
    forces = place_forces(scal_ref, with_sides(sets, side_ref, sideo_ref), all_ref)
    panels = forces.shape[1]
    own = mine == 0
    for z in range(2):
        keys, depth = panel_keys_of(z, own, ints_ref, intso_ref, o, panels, rows, size_x, size_y, size_z)
        wide = spread_forces(forces[z], depth, size_z, 16, NSTEP)
        node = iota((size_x * rows, keys.shape[1]), 0)
        hit = (node == keys).astype(F32).astype(BF16)
        for n in range(NSTEP):
            span = comps * size_z
            got = jnp.dot(hit, wide[:, n * span:(n + 1) * span], preferred_element_type=F32)
            for c in range(comps):
                drive_ref[n, z, c] = got[:, c * size_z:(c + 1) * size_z].reshape(size_x, rows, size_z)
    edge = jnp.zeros((rows, size_z), F32)
    for z in range(2):
        for c in range(comps):
            for ref in (now_ref, old_ref):
                ref[z, c, 0] = edge
                ref[z, c, size_x + 1] = edge
    for z_at, un, up, lat, ints in (
        (mine, un_ref, up_ref, lat_ref, ints_ref),
        (1 - mine, uno_ref, upo_ref, lato_ref, intso_ref),
    ):
        speed = listed(ints, LANES, 0)
        ups, lows = [], []
        for c in range(comps):
            upper, lower = sides(scal_ref, side_ref, sideo_ref, (z_at, slice(c * size_x, (c + 1) * size_x)))
            ups.append(upper)
            lows.append(lower)
            tile_now, tile_old = halo_tiles(upper, lower)
            now_ref[z_at, c, 1:size_x + 1, 0:size_y] = un[c]
            now_ref[z_at, c, 1:size_x + 1, size_y:rows] = tile_now
            old_ref[z_at, c, 1:size_x + 1, 0:size_y] = up[c]
            old_ref[z_at, c, 1:size_x + 1, size_y:rows] = tile_old
        rate_ref[z_at, :, 0:size_y] = lat[...] * speed[None]
        rate_ref[z_at, :, size_y:rows] = halo_rate(ups, lows)
    for side in range(2):
        for z in range(2):
            for d in range(NSTEP):
                ratef_ref[side, z, d] = rate_ref[z, d if side else size_x - 1 - d]
    refs = [now_ref, old_ref]
    for n in range(NSTEP):
        now, old = refs[n % 2], refs[(n + 1) % 2]
        for side in range(2):
            for z in range(2):
                for c in range(comps):
                    face_ref[side, z, n * comps + c] = now[z, c, 1 if side else size_x]

        def step(x, carry, now=now, old=old, n=n, halves=(0, 1)):
            for c in range(comps):
                centre = now[0, c, x + 1], now[1, c, x + 1]
                sums = inplane(*centre)
                for z in halves:
                    lap = sums[z] + (now[z, c, x] + now[z, c, x + 2])
                    value = (
                        2.0 * centre[z] - old[z, c, x + 1] + rate_ref[z, x] * lap + drive_ref[n, z, c, x]
                    )
                    if len(halves) == 2:
                        old[z, c, x + 1] = value
                    else:
                        final_ref[c, x] = value[0:size_y]
                        before_ref[c, x] = centre[z][0:size_y]
            return carry

        if n < NSTEP - 1:
            lax.fori_loop(0, size_x, step, 0, unroll=size_x)
        else:
            for z in range(2):
                @pl.when(mine == z)
                def _(step=step, z=z):
                    lax.fori_loop(0, size_x, functools.partial(step, halves=(z,)), 0, unroll=size_x)


def corrected(scal_ref, final_in, before_in, face_ref, ratef_ref, coded_ref, recv_ref, high, edges):
    comps, size_x, size_y, size_z = final_in.shape
    a, mine = scal_ref[0], scal_ref[2]
    side = jnp.where(high, 0, 1)
    inside = jnp.where(high, a < scal_ref[3] - 1, a > 0)
    expand_all(coded_ref, recv_ref, face_groups(comps))

    def theirs(z, at):
        return jnp.where(inside, face_plane(recv_ref, z, at, comps), 0.0)

    def correct(own):
        rate = {}
        for z in range(2):
            for m in range(NSTEP):
                rate[z, -m] = ratef_ref[side, z, m]
            for m in (1, 2):
                rate[z, m] = theirs(z, NSTEP * comps + m - 1)
        for c in range(comps):
            last, now = {}, {}
            for n in range(NSTEP):
                later = {}
                for m in range(-n, min(n + 1, NSTEP - 1 - n) + 1):
                    centre = [now.get((z, m)) for z in range(2)]
                    sums = inplane(*centre) if centre[0] is not None else (None, None)
                    for z in range(2) if n < NSTEP - 1 else (own,):
                        terms = [sums[z], now.get((z, m - 1)), now.get((z, m + 1))]
                        if m == 0:
                            terms.append(theirs(z, n * comps + c))
                        if m == 1:
                            terms.append(face_ref[side, z, n * comps + c])
                        value = functools.reduce(lambda p, q: p + q, [t for t in terms if t is not None])
                        value = rate[z, m] * value
                        if centre[z] is not None:
                            value = value + 2.0 * centre[z]
                        if (z, m) in last:
                            value = value - last[z, m]
                        later[z, m] = value
                last, now = now, later
            for values, source, edge in zip((now, last), (final_in, before_in), edges):
                depth = edge.shape[1]
                for m in range(1 - depth, 1):
                    x, at = jnp.where(high, size_x - 1 + m, -m), jnp.where(high, depth - 1 + m, -m)
                    edge[c, at] = source[c, x] + values[own, m][0:size_y]

    for z in range(2):
        pl.when(mine == z)(functools.partial(correct, z))


def near_kernel(
    scal_ref, final_in, before_in, face_ref, ratef_ref, coded_ref, final_edge, before_edge, recv_ref
):
    high = lax.rem(scal_ref[0] + scal_ref[2], 2) == 0
    edges = final_edge, before_edge
    corrected(scal_ref, final_in, before_in, face_ref, ratef_ref, coded_ref, recv_ref, high, edges)


def far_kernel(
    scal_ref, final_in, before_in, face_ref, ratef_ref, coded_ref, final_near, before_near,
    final_ref, before_ref, recv_ref, final_edge, before_edge, sems,
):
    size_x = final_in.shape[1]
    high = lax.rem(scal_ref[0] + scal_ref[2], 2) == 1
    copies = []

    def begin(src, target, first, count):
        copies.append(pltpu.make_async_copy(src, target.at[:, pl.ds(first, count)], sems.at[len(copies)]))
        copies[-1].start()

    outputs = ((final_in, final_near, final_ref, final_edge), (before_in, before_near, before_ref, before_edge))
    for source, near, target, edge in outputs:
        depth = edge.shape[1]
        begin(near, target, jnp.where(high, 0, size_x - depth), depth)
        begin(source.at[:, pl.ds(depth, size_x - 2 * depth)], target, depth, size_x - 2 * depth)
    edges = final_edge, before_edge
    corrected(scal_ref, final_in, before_in, face_ref, ratef_ref, coded_ref, recv_ref, high, edges)
    for source, near, target, edge in outputs:
        depth = edge.shape[1]
        begin(edge, target, jnp.where(high, size_x - depth, 0), depth)
    for copy in copies:
        copy.wait()


def send(value, mesh_sizes, route):
    nx, ny, nz = mesh_sizes
    number = lambda i, j, k: (i * ny + j) * nz + k
    pairs = [
        (number(i, j, k), number(*route(i, j, k))) for i in range(nx) for j in range(ny) for k in range(nz)
    ]
    return lax.ppermute(value, ("gx", "gy", "gz"), pairs)


def partner(i, core, count):
    step = 1 if (i + core) % 2 == 0 else -1
    return (i + step) % count


def per_device(
    u_now, u_prev, panels, panel_owner, panel_block, coupling, layer_depth, layer_speed, lateral
):
    sizes = tuple(lax.axis_size(axis) for axis in ("gx", "gy", "gz"))
    nx, ny, nz = sizes
    assert nx % 2 == 0 and ny % 2 == 0 and nz == 2
    comps, size_x, size_y, size_z = u_now.shape
    rows = size_y + HALO
    per_dev, spectral = panels.shape[2], panels.shape[4]
    npanels = ny * per_dev
    scal = jnp.stack(
        [lax.axis_index("gx"), lax.axis_index("gy"), lax.axis_index("gz"), jnp.int32(nx), jnp.int32(ny)]
    ).astype(jnp.int32)

    def swap(value):
        return send(value, sizes, lambda i, j, k: (i, j, 1 - k))

    def route_x(i, j, k):
        return partner(i, k, nx), j, k

    def route_y(i, j, k):
        to = partner(j, k, ny)
        if abs(to - j) != 1 or (ny == 2 and k == 1):
            return i ^ 1, j, k
        return i, to, k

    assert per_dev == PANELS and size_z == LANES
    vmem = pl.BlockSpec(memory_space=pltpu.VMEM)
    smem = pl.BlockSpec(memory_space=pltpu.SMEM)
    params = pltpu.CompilerParams(vmem_limit_bytes=48 * 1024 * 1024)
    table = jnp.asarray(wave_table(spectral, panels.shape[3]))
    width = table.shape[1]
    extra_rows = -(-(LANES + 4 * npanels) // (8 * width)) * 8
    tiles = comps * size_x
    number = tiles + width // size_z * (per_dev // HALO)
    half = jax.ShapeDtypeStruct(coded_shape(number), jnp.int16)
    ints, fields_own, mine, theirs = pl.pallas_call(
        prepare_kernel,
        out_shape=(
            jax.ShapeDtypeStruct((per_dev + extra_rows, width), F32),
            jax.ShapeDtypeStruct((2 * comps + 1,) + u_now.shape[1:], F32),
            half,
            half,
        ),
        in_specs=[smem] + [pl.BlockSpec(memory_space=pl.ANY)] * 10,
        out_specs=(vmem,) * 4,
        scratch_shapes=[
            pltpu.VMEM((2, number, HALO, size_z), F32),
            pltpu.VMEM((per_dev,) + panels.shape[3:], BF16),
            pltpu.VMEM(coupling.shape, F32),
            pltpu.VMEM(table.shape, BF16),
            pltpu.VMEM((1, size_z), jnp.int32),
            pltpu.VMEM((1, npanels), jnp.int32),
            pltpu.VMEM((1, npanels), jnp.int32),
            pltpu.SMEM(layer_speed.shape, F32),
            pltpu.SemaphoreType.DMA((10,)),
        ],
        compiler_params=params,
        name="prepare",
    )(scal, *(
        pltpu.with_memory_space_constraint(value, pltpu.HBM)
        for value in (
            panels.reshape((per_dev,) + panels.shape[3:]), coupling, table, layer_depth.reshape(1, -1),
            panel_owner.reshape(1, -1), panel_block.reshape(1, -1), layer_speed, u_now, u_prev, lateral,
        )
    ))
    theirs, ints_o = swap(theirs), swap(ints)
    both, pair = pl.pallas_call(
        gather_kernel,
        out_shape=(
            jax.ShapeDtypeStruct((2,) + half.shape, jnp.int16),
            jax.ShapeDtypeStruct((2, per_dev, width), F32),
        ),
        in_specs=[vmem] * 4,
        out_specs=(vmem,) * 2,
        compiler_params=params,
        name="gather",
    )(mine, theirs, ints, ints_o)
    fields_own, both = lax.optimization_barrier((fields_own, both))
    side = send(both, sizes, route_y)
    state = (scal, fields_own, swap(fields_own), ints, ints_o)
    state_specs = [smem] + [vmem] * 4
    tiles_scratch = pltpu.VMEM((2, number, HALO, size_z), F32)
    if ny == 4:
        far = send(pair, sizes, lambda i, j, k: (i, j ^ 2 if k == 0 else 3 - j, k))
        side, far = lax.optimization_barrier((side, far))
        side_o, far_o = swap(side), swap(far)
        sets = (pair, far, far_o)
    else:
        side_o = swap(side)
        pair = jnp.where(lax.axis_index("gz") == 0, pair, pair[::-1])
        sets = (jnp.moveaxis(lax.all_gather(pair, "gy"), 0, 1).reshape(2, npanels, -1),)
    shared = state + (side, side_o) + sets
    shared_specs = state_specs + [vmem] * (2 + len(sets))
    all_scratch = pltpu.VMEM((2, npanels, width), F32)
    planes = NSTEP * comps
    face_scratch = pltpu.VMEM((2 * face_tiles(comps), HALO, size_z), F32)
    sent = pl.pallas_call(
        face_kernel,
        out_shape=jax.ShapeDtypeStruct(coded_shape(2 * face_tiles(comps)), jnp.int16),
        in_specs=shared_specs,
        out_specs=vmem,
        scratch_shapes=[all_scratch, tiles_scratch, tiles_scratch, face_scratch],
        compiler_params=params,
        name="face",
    )(*shared)
    recv = send(sent, sizes, route_x)
    final, before, face, ratef = pl.pallas_call(
        local_kernel,
        out_shape=(
            jax.ShapeDtypeStruct(u_now.shape, F32),
            jax.ShapeDtypeStruct(u_now.shape, F32),
            jax.ShapeDtypeStruct((2, 2, planes, rows, size_z), F32),
            jax.ShapeDtypeStruct((2, 2, NSTEP, rows, size_z), F32),
        ),
        in_specs=shared_specs,
        out_specs=(vmem,) * 4,
        scratch_shapes=[
            all_scratch,
            tiles_scratch,
            tiles_scratch,
            pltpu.VMEM((2, comps, size_x + 2, rows, size_z), F32),
            pltpu.VMEM((2, comps, size_x + 2, rows, size_z), F32),
            pltpu.VMEM((2, size_x, rows, size_z), F32),
            pltpu.VMEM((NSTEP, 2, comps, size_x, rows, size_z), F32),
        ],
        compiler_params=params,
        name="local",
    )(*shared)
    final, before, face, ratef, recv = lax.optimization_barrier((final, before, face, ratef, recv))
    recv_o = swap(recv)
    edges = [jax.ShapeDtypeStruct((comps, depth, size_y, size_z), F32) for depth in (NSTEP, NSTEP - 1)]
    whole = (scal, final, before, face, ratef)
    near = pl.pallas_call(
        near_kernel,
        out_shape=tuple(edges),
        in_specs=[smem] + [vmem] * 5,
        out_specs=(vmem, vmem),
        scratch_shapes=[face_scratch],
        compiler_params=params,
        name="near",
    )(*whole, recv)
    near, recv_o = lax.optimization_barrier((near, recv_o))
    return pl.pallas_call(
        far_kernel,
        out_shape=(
            jax.ShapeDtypeStruct(u_now.shape, F32),
            jax.ShapeDtypeStruct(u_now.shape, F32),
        ),
        in_specs=[smem] + [vmem] * 7,
        out_specs=(pl.BlockSpec(memory_space=pl.ANY),) * 2,
        scratch_shapes=[
            face_scratch,
            pltpu.VMEM(edges[0].shape, F32),
            pltpu.VMEM(edges[1].shape, F32),
            pltpu.SemaphoreType.DMA((6,)),
        ],
        compiler_params=params,
        name="far",
    )(*whole, recv_o, *near)


def solution(mesh):
    in_specs = (
        P(None, "gx", "gy", "gz"),
        P(None, "gx", "gy", "gz"),
        P("gx", "gz", "gy", None, None),
        P("gx", "gz", None, None),
        P("gx", "gz", None),
        P(),
        P("gz"),
        P(),
        P("gx", "gy", "gz"),
    )
    out_specs = (P(None, "gx", "gy", "gz"), P(None, "gx", "gy", "gz"))
    return jax.shard_map(
        per_device, mesh=mesh, in_specs=in_specs, out_specs=out_specs, check_vma=False
    )
```

```python
import functools

import jax
import jax.numpy as jnp
import ml_dtypes
import numpy as np
from jax import lax
from jax.experimental import pallas as pl
from jax.experimental.pallas import tpu as pltpu
from jax.sharding import PartitionSpec as P

NSTEP = 4
HALO = 8
LANES = 128
PANELS = 16
TOP = 32000.0
F32 = jnp.float32
BF16 = jnp.bfloat16


def wave_table(count, per_step):
    half = count // 2
    freq = np.float32(2.0 * np.pi) * (np.arange(half, dtype=np.float32) + np.float32(0.5)) / np.float32(count)
    times = np.float32(37.0) + np.arange(NSTEP, dtype=np.float32)
    phase = freq[:, None] * times[None, :]
    table = np.concatenate([np.cos(phase), np.sin(phase)], axis=0) / np.sqrt(np.float32(half))
    wide = np.repeat(table.astype(ml_dtypes.bfloat16), per_step, axis=1)
    return np.pad(wide, ((0, 0), (0, -wide.shape[1] % 128)))


def shift_of(size):
    assert size & (size - 1) == 0
    return size.bit_length() - 1


def iota(shape, dim):
    return lax.broadcasted_iota(jnp.int32, shape, dim)


def spin(value, amount, axis):
    return pltpu.roll(value, amount % value.shape[axis], axis)


def across(z0, z1):
    lanes = z0.shape[-1]
    lane = iota(z0.shape, z0.ndim - 1)
    first, last = lane == 0, lane == lanes - 1
    ax = z0.ndim - 1
    down0, down1 = spin(z0, 1, ax), spin(z1, 1, ax)
    up0, up1 = spin(z0, -1, ax), spin(z1, -1, ax)
    sum0 = jnp.where(first, 0.0, down0) + jnp.where(last, up1, up0)
    sum1 = jnp.where(first, down0, down1) + jnp.where(last, 0.0, up1)
    return sum0, sum1


def inplane(z0, z1):
    ax = z0.ndim - 2
    sum0, sum1 = across(z0, z1)
    sum0 = sum0 + (spin(z0, 1, ax) + spin(z0, -1, ax)) - 6.0 * z0
    sum1 = sum1 + (spin(z1, 1, ax) + spin(z1, -1, ax)) - 6.0 * z1
    return sum0, sum1


def row_scales(exponents):
    return jnp.exp2(exponents) * (1.0 / TOP)


def quantize(load, groups, out_ref):
    shape = (HALO, LANES)
    lane = iota(shape, 1)
    peak = jnp.zeros(shape, F32)
    for group in range(max(groups) + 1):
        members = [jnp.abs(load(t)) for t, of in enumerate(groups) if of == group]
        top = functools.reduce(jnp.maximum, members)
        peak = jnp.where(lane == group, jnp.max(top, axis=1, keepdims=True), peak)
    exponents = jnp.ceil(jnp.log2(jnp.maximum(peak, 1e-30)))
    factor = jnp.exp2(-exponents) * TOP
    zero = jnp.zeros(shape, jnp.int32)
    wide = [jnp.broadcast_to(factor[:, g:g + 1], shape) for g in range(max(groups) + 1)]
    parts = [jnp.round(load(t) * wide[of]).astype(jnp.int32) for t, of in enumerate(groups)]
    parts += [zero] * (len(groups) % 2) + [exponents.astype(jnp.int32), zero]
    for i in range(out_ref.shape[0]):
        out_ref[i] = jnp.concatenate(parts[2 * i:2 * i + 2], axis=0).astype(jnp.int16)


def coded_shape(number):
    return ((number + 1) // 2 + 1, 2 * HALO, LANES)


def side_groups(comps, size_x, rest):
    near = [c * (size_x // NSTEP) + x // NSTEP for c in range(comps) for x in range(size_x)]
    return near + [max(near) + 1 + i for i in range(rest)]


def scales_of(coded):
    return row_scales(coded.astype(jnp.int32)[0:HALO].astype(F32))


def expand(load, store, scales, blocks):
    for at, one, two in blocks:
        pair = load(at).astype(jnp.int32).astype(F32)
        store(2 * at, pair[0:HALO] * scales[:, one:one + 1])
        store(2 * at + 1, pair[HALO:] * scales[:, two:two + 1])


def expand_all(ref, tiles_ref, groups):
    def store(t, value):
        tiles_ref[t] = value

    expand(lambda i: ref[i], store, scales_of(ref[ref.shape[0] - 1]), [
        (t // 2, groups[t], groups[t + 1]) for t in range(0, len(groups), 2)
    ])


def expand_sides(ref, tiles_ref, far_ref, first, groups, choose):
    last = len(groups) // 2
    forces = len(groups) - far_ref.shape[1]
    for half in range(2):
        z = first if half == 0 else 1 - first

        def store(t, value):
            tiles_ref[z, t] = value

        def store_far(t, value):
            far_ref[z, t] = value

        scales = scales_of(ref[half, last])
        for moved, blocks in choose(scales):
            expand(lambda i: ref[half, i], store, moved, blocks)
        if ref.shape[1] > last + 1:
            expand(lambda i: ref[half, last + 1 + i], store_far, scales_of(ref[half, ref.shape[1] - 1]), [
                ((t - forces) // 2, groups[t], groups[t + 1]) for t in range(forces, len(groups), 2)
            ])


def prepare_kernel(
    scal_ref, panels_hbm, coupling_hbm, table_hbm, depth_hbm, owner_hbm, block_hbm, speed_hbm,
    un_hbm, up_hbm, lat_hbm, out_ref, state_ref, mine_ref, theirs_ref, tiles_ref,
    panels_ref, coupling_ref, table_ref, depth_ref, owner_ref, block_ref, speed_ref, sems,
):
    comps = un_hbm.shape[0]
    un_ref, up_ref, lat_ref = state_ref.at[0:comps], state_ref.at[comps:2 * comps], state_ref.at[2 * comps]
    pairs = (
        (panels_hbm, panels_ref), (table_hbm, table_ref), (coupling_hbm, coupling_ref),
        (depth_hbm, depth_ref), (owner_hbm, owner_ref), (block_hbm, block_ref), (speed_hbm, speed_ref),
        (un_hbm, un_ref), (up_hbm, up_ref), (lat_hbm, lat_ref),
    )
    copies = [pltpu.make_async_copy(src, dst, sems.at[i]) for i, (src, dst) in enumerate(pairs)]
    for copy in copies:
        copy.start()
    for copy in copies[:7]:
        copy.wait()
    count, rows, spectral = panels_ref.shape
    block = rows // comps
    lanes = table_ref.shape[1]
    free = jnp.dot(
        panels_ref[...].reshape(count * rows, spectral), table_ref[...], preferred_element_type=F32
    )
    weights = coupling_ref[...].reshape(rows, block)
    stacked = jnp.concatenate([weights] * NSTEP + [jnp.zeros((lanes - NSTEP * rows, block), F32)], axis=0)
    pick = ((iota((rows, block), 0) & (block - 1)) == iota((rows, block), 1)).astype(F32)
    spread = lax.dot_general(
        pick, stacked, (((1,), (1,)), ((), ())), precision=lax.Precision.HIGHEST, preferred_element_type=F32
    )
    comp_row = iota((rows, lanes), 0) >> shift_of(block)
    comp_lane = iota((rows, lanes), 1) >> shift_of(block)
    same = comp_lane == comp_row
    for step in range(1, NSTEP):
        same = same | (comp_lane == comp_row + step * comps)
    spread = jnp.where(same, spread, 0.0)
    out_ref[0:count] = jnp.sum(free.reshape(count, rows, lanes) * spread[None], axis=1)
    out_ref[count:] = jnp.zeros((out_ref.shape[0] - count, lanes), F32)
    speed = jnp.zeros(depth_ref.shape, F32)
    for layer in range(speed_ref.shape[0]):
        speed = jnp.where(depth_ref[...] == layer, speed_ref[layer], speed)
    pieces = [speed]
    for ref in (owner_ref, block_ref):
        twice = jnp.concatenate([ref[...], ref[...]], axis=1)
        pieces += [twice[:, i:i + LANES] for i in range(0, twice.shape[1], LANES)]
    for i, piece in enumerate(pieces):
        row, at = count + i * LANES // lanes, i * LANES % lanes
        out_ref[row:row + 1, at:at + LANES] = piece.astype(F32)
    for copy in copies[7:]:
        copy.wait()
    comps, size_x, size_y, size_z = un_ref.shape
    sub = iota((size_x, HALO, size_z), 1)
    for side in range(2):
        base = 0 if side else size_y - HALO
        rate = lat_ref[:, base:base + HALO, :] * speed[None]
        for c in range(comps):
            now = un_ref[c, :, base:base + HALO, :]
            old = spin(up_ref[c, :, base:base + HALO, :], HALO // 2, 1)
            keep = sub < HALO // 2 if side else sub >= HALO // 2
            row = c if side else HALO - 1 - c
            tile = jnp.where(keep, now, old)
            tile = jnp.where(sub == (HALO - 1 if side else 0), rate[:, row:row + 1, :], tile)
            tiles_ref[side, c * size_x:(c + 1) * size_x] = tile
        for part in range(lanes // size_z):
            for piece in range(count // HALO):
                at = comps * size_x + part * (count // HALO) + piece
                tiles_ref[side, at] = out_ref[piece * HALO:(piece + 1) * HALO, part * size_z:(part + 1) * size_z]
    low = lax.rem(scal_ref[1] + scal_ref[2], 2)
    groups = side_groups(comps, size_x, tiles_ref.shape[1] - comps * size_x)
    quantize(lambda t: tiles_ref[low, t], groups, mine_ref)
    quantize(lambda t: tiles_ref[1 - low, t], groups, theirs_ref)


def listed(ref, panels, which):
    lanes = ref.shape[1]
    width = -(-2 * panels // LANES)
    first, number = ((0, 1), (1, width), (1 + width, width))[which]
    out = []
    for i in range(first, first + number):
        row, at = PANELS + i * LANES // lanes, i * LANES % lanes
        out.append(ref[row:row + 1, at:at + LANES])
    return jnp.concatenate(out, axis=1)


def place_forces(scal_ref, ints_ref, intso_ref, sets, all_ref):
    o, mine = scal_ref[1], scal_ref[2]
    side_ref, sideo_ref, far_ref, faro_ref = sets
    count, lanes = PANELS, ints_ref.shape[1]
    beside, opposite, mirror = o + 1 - 2 * lax.rem(o, 2), lax.rem(o + 2, 4), 3 - o
    size_z = side_ref.shape[-1]
    step = count // HALO
    here = mine == 0

    def spot(j):
        return pl.ds(pl.multiple_of(j * count, count), count)

    for ref, j in (
        (side_ref, jnp.where(here, beside, mirror)),
        (sideo_ref, jnp.where(here, mirror, beside)),
        (far_ref, jnp.where(here, opposite, mirror)),
        (faro_ref, jnp.where(here, mirror, opposite)),
    ):
        first = ref.shape[1] - lanes // size_z * step
        for z in range(2):
            for part in range(lanes // size_z):
                at = first + part * step
                all_ref[z, spot(j), part * size_z:(part + 1) * size_z] = ref[z, at:at + step].reshape(count, size_z)
    all_ref[mine, spot(o), :] = ints_ref[0:count]
    all_ref[1 - mine, spot(o), :] = intso_ref[0:count]
    return all_ref


def index_kernel(scal_ref, ints_ref, intso_ref, at_ref, hit_ref, *, sizes, block, panels):
    size_x, size_y, size_z = sizes
    rows = size_y + HALO
    for z, ints in ((scal_ref[2], ints_ref), (1 - scal_ref[2], intso_ref)):
        keys, depth = panel_keys(ints, scal_ref[1], panels, rows, size_x, size_y, size_z // block)
        at = (iota((size_z, depth.shape[1]), 0) >> shift_of(block)) == depth
        at_ref[z] = jnp.transpose(at.astype(F32))
        hit = iota((size_x * rows, keys.shape[1]), 0) == keys
        hit_ref[z] = hit.astype(F32).astype(BF16)


def panel_keys(ints_ref, o, panels, rows, size_x, size_y, zblocks):
    owner = listed(ints_ref, panels, 1).astype(jnp.int32)
    block = listed(ints_ref, panels, 2).astype(jnp.int32)
    depth = block & (zblocks - 1)
    y = (block >> shift_of(zblocks)) & (size_y - 1)
    x = block >> (shift_of(zblocks) + shift_of(size_y))
    key = x * rows
    reach = NSTEP - 1
    row = jnp.where(owner == o, y, -1)
    row = jnp.where((owner == o + 1) & (y < reach), y + size_y, row)
    row = jnp.where((owner == o - 1) & (y >= size_y - reach), y + rows - size_y, row)
    return jnp.where(row < 0, -1, key + row), depth


def spread_forces(force, at, block, steps):
    high = force.astype(BF16).astype(F32)
    both = jnp.concatenate([high, force - high], axis=0)
    rows, size_z = at.shape
    lane = iota((rows, size_z), 1) >> shift_of(block)
    base = (
        (iota((size_z, size_z), 0) & (block - 1)) == (iota((size_z, size_z), 1) & (block - 1))
    ).astype(BF16)
    per_tile = size_z // block
    out = []
    for q in range(steps * 3):
        part = both[:, (q // per_tile) * size_z:(q // per_tile + 1) * size_z]
        part = jnp.where(lane == q % per_tile, part, 0.0).astype(BF16)
        wide = jnp.dot(part, base, preferred_element_type=F32)
        out.append((wide * at).astype(BF16))
    return jnp.concatenate(out, axis=1)


def fields(state_ref):
    comps = state_ref.shape[0] // 2
    return state_ref.at[0:comps], state_ref.at[comps:2 * comps], state_ref.at[2 * comps]


def halo_tiles(high, low):
    sub = iota(high.shape, high.ndim - 2)
    upper = sub < HALO // 2
    now = jnp.where(upper, high, low)
    old = spin(jnp.where(upper, low, high), HALO // 2, high.ndim - 2)
    return now, old


def halo_rate(highs, lows):
    sub = iota(highs[0].shape, highs[0].ndim - 2)
    tile = jnp.zeros(highs[0].shape, F32)
    ends = slice(HALO - 1, HALO), slice(0, 1)
    for c in range(3):
        tile = jnp.where(sub == c, highs[c][..., ends[0], :], tile)
        tile = jnp.where(sub == HALO - 1 - c, lows[c][..., ends[1], :], tile)
    return tile


def sides(scal_ref, side_ref, sideo_ref, at):
    o, mine = scal_ref[1], scal_ref[2]
    high = lax.rem(o + mine, 2) == 0
    one, two = side_ref[at], sideo_ref[at]
    upper = jnp.where(o < scal_ref[4] - 1, jnp.where(high, one, two), 0.0)
    lower = jnp.where(o > 0, jnp.where(high, two, one), 0.0)
    return upper, lower


def forces_of(scal_ref, ints_ref, intso_ref, rest, all_ref, scratch):
    if rest:
        return rest[0]
    return place_forces(scal_ref, ints_ref, intso_ref, scratch, all_ref)


def face_kernel(
    scal_ref, state_ref, stateo_ref, ints_ref, intso_ref, at_ref, hit_ref, coded_ref, codedo_ref, *rest,
):
    *rest, out_ref, all_ref, side_ref, sideo_ref, far_ref, faro_ref, faces_ref = rest
    scratch = side_ref, sideo_ref, far_ref, faro_ref
    (un_ref, up_ref, lat_ref), (uno_ref, upo_ref, lato_ref) = fields(state_ref), fields(stateo_ref)
    comps, size_x, size_y, size_z = un_ref.shape
    rows = size_y + HALO
    tiles = comps * size_x
    a, o, mine = scal_ref[0], scal_ref[1], scal_ref[2]
    high = lax.rem(a + mine, 2) == 0
    skip = jnp.where(high, size_x - NSTEP, 0)

    groups = side_groups(comps, size_x, side_ref.shape[1] - tiles)

    def choose(scales):
        moved = pltpu.roll(scales, lax.rem(LANES - lax.div(skip, NSTEP), LANES), 1)
        near = [first + i for first in range(0, tiles, size_x) for i in range(0, NSTEP, 2)]
        rest = [(t // 2, groups[t], groups[t + 1]) for t in range(tiles, len(groups), 2)]
        return (moved, [(t // 2 + lax.div(skip, 2), groups[t], groups[t + 1]) for t in near]), (scales, rest)

    expand_sides(coded_ref, side_ref, far_ref, mine, groups, choose)
    expand_sides(codedo_ref, sideo_ref, faro_ref, 1 - mine, groups, choose)
    forces = forces_of(scal_ref, ints_ref, intso_ref, rest, all_ref, scratch)
    own = mine == 0
    now, old, rate, drive = {}, {}, {}, {}
    for z in range(2):
        wide = spread_forces(forces[z], at_ref[z], 16, NSTEP - 1)
        first = pl.multiple_of(jnp.where(high, size_x - NSTEP, 0) * rows, 2 * HALO)
        hit = hit_ref[z, pl.ds(first, NSTEP * rows)]
        got = jnp.dot(hit, wide, preferred_element_type=F32)
        got = got.reshape(NSTEP, rows, wide.shape[1])
        for d in range(1, NSTEP):
            for n in range(NSTEP - d):
                for c in range(comps):
                    q = (n * comps + c) * size_z
                    drive[z, n, d, c] = jnp.where(
                        high, got[NSTEP - d, :, q:q + size_z], got[d - 1, :, q:q + size_z]
                    )
        speed = jnp.where(
            own if z == 0 else jnp.logical_not(own),
            listed(ints_ref, LANES, 0),
            listed(intso_ref, LANES, 0),
        )
        near = own if z == 0 else jnp.logical_not(own)
        for d in range(1, NSTEP + 1):
            x = jnp.where(high, size_x - d, d - 1)
            ups, lows = [], []
            for c in range(comps):
                upper, lower = sides(scal_ref, side_ref, sideo_ref, (z, c * size_x + x))
                ups.append(upper)
                lows.append(lower)
                tile_now, tile_old = halo_tiles(upper, lower)
                centre = jnp.where(near, un_ref[c, x], uno_ref[c, x])
                now[z, d, c] = jnp.concatenate([centre, tile_now], axis=0)
                if d < NSTEP:
                    centre = jnp.where(near, up_ref[c, x], upo_ref[c, x])
                    old[z, d, c] = jnp.concatenate([centre, tile_old], axis=0)
            if d < NSTEP:
                centre = jnp.where(near, lat_ref[x], lato_ref[x]) * speed
                rate[z, d] = jnp.concatenate([centre, halo_rate(ups, lows)], axis=0)
    series = {(z, 0, c): now[z, 1, c] for z in range(2) for c in range(comps)}
    for n in range(1, NSTEP):
        later = {}
        for d in range(1, NSTEP - n + 1):
            for c in range(comps):
                sums = inplane(now[0, d, c], now[1, d, c])
                for z in range(2):
                    lap = sums[z] + now[z, d + 1, c]
                    if d > 1:
                        lap = lap + now[z, d - 1, c]
                    later[z, d, c] = (
                        2.0 * now[z, d, c] - old[z, d, c] + rate[z, d] * lap + drive[z, n - 1, d, c]
                    )
        old, now = now, later
        for z in range(2):
            for c in range(comps):
                series[z, n, c] = now[z, 1, c]
    sub = iota((HALO, size_z), 0)
    middle = (sub == HALO // 2 - 1) | (sub == HALO // 2)
    ends = (sub < 2) | (sub >= HALO - 2)
    for z in range(2):
        planes = [series[z, n, c] for n in range(NSTEP) for c in range(comps)] + [rate[z, 1], rate[z, 2]]
        rims = [plane[size_y:rows] for plane in planes]
        tails = [jnp.where(middle, spin(rims[2 * comps + c], HALO // 2, 0), rims[c]) for c in range(comps)]
        tails.append(jnp.where(ends, rims[comps], spin(rims[comps + 1], HALO // 2, 0)))
        tails.append(jnp.where(ends, rims[comps + 2], spin(rims[NSTEP * comps], HALO // 2, 0)))
        base = z * face_tiles(comps)
        for i, plane in enumerate(planes):
            for half in range(2):
                faces_ref[base + 2 * i + half] = plane[half * HALO:(half + 1) * HALO]
        for i, tail in enumerate(tails):
            faces_ref[base + 2 * len(planes) + i] = tail
    quantize(lambda t: faces_ref[t], face_groups(comps), out_ref)


def face_tiles(comps):
    return 2 * (NSTEP * comps + 2) + comps + 2


def face_groups(comps):
    groups = []
    for z in range(2):
        base = z * (2 * NSTEP + 5)
        groups += [base + 2 * n + half for n in range(NSTEP) for _ in range(comps) for half in range(2)]
        groups += [base + 2 * NSTEP + half for _ in range(2) for half in range(2)]
        groups += [base + 2 * NSTEP + 2] * comps + [base + 2 * NSTEP + 3, base + 2 * NSTEP + 4]
    return groups


def face_plane(tiles_ref, z, i, comps):
    count = NSTEP * comps + 2
    base = z * face_tiles(comps)
    tail = base + 2 * count
    parts = [tiles_ref[base + 2 * i], tiles_ref[base + 2 * i + 1]]
    turned = lambda at: spin(tiles_ref[at], HALO // 2, 0)
    if i < comps:
        parts.append(tiles_ref[tail + i])
    elif i < comps + 3:
        at, other = ((tail + comps, False), (tail + comps, True), (tail + comps + 1, False))[i - comps]
        parts.append(turned(at) if other else tiles_ref[at])
    elif 2 * comps <= i < 3 * comps:
        parts.append(turned(tail + i - 2 * comps))
    elif i == NSTEP * comps:
        parts.append(turned(tail + comps + 1))
    else:
        parts.append(jnp.zeros(parts[0].shape, F32))
    return jnp.concatenate(parts, axis=0)


def local_kernel(
    scal_ref, state_ref, stateo_ref, ints_ref, intso_ref, at_ref, hit_ref, coded_ref, codedo_ref, *rest,
):
    now_ref, old_ref, rate_ref, drive_ref = rest[-4:]
    all_ref, side_ref, sideo_ref, far_ref, faro_ref = rest[-9:-4]
    *rest, final_ref, before_ref, face_ref, ratef_ref = rest[:-9]
    scratch = side_ref, sideo_ref, far_ref, faro_ref
    (un_ref, up_ref, lat_ref), (uno_ref, upo_ref, lato_ref) = fields(state_ref), fields(stateo_ref)
    comps, size_x, size_y, size_z = un_ref.shape
    rows = size_y + HALO
    tiles = comps * size_x
    o, mine = scal_ref[1], scal_ref[2]
    groups = side_groups(comps, size_x, side_ref.shape[1] - comps * size_x)
    choose = lambda scales: (
        (scales, [(t // 2, groups[t], groups[t + 1]) for t in range(0, len(groups), 2)]),
    )
    expand_sides(coded_ref, side_ref, far_ref, mine, groups, choose)
    expand_sides(codedo_ref, sideo_ref, faro_ref, 1 - mine, groups, choose)
    forces = forces_of(scal_ref, ints_ref, intso_ref, rest, all_ref, scratch)
    own = mine == 0
    for z in range(2):
        wide = spread_forces(forces[z], at_ref[z], 16, NSTEP)
        hit = hit_ref[z]
        for n in range(NSTEP):
            span = comps * size_z
            got = jnp.dot(hit, wide[:, n * span:(n + 1) * span], preferred_element_type=F32)
            for c in range(comps):
                drive_ref[n, z, c] = got[:, c * size_z:(c + 1) * size_z].reshape(size_x, rows, size_z)
    edge = jnp.zeros((rows, size_z), F32)
    for z in range(2):
        for c in range(comps):
            for ref in (now_ref, old_ref):
                ref[z, c, 0] = edge
                ref[z, c, size_x + 1] = edge
    for z_at, un, up, lat, ints in (
        (mine, un_ref, up_ref, lat_ref, ints_ref),
        (1 - mine, uno_ref, upo_ref, lato_ref, intso_ref),
    ):
        speed = listed(ints, LANES, 0)
        ups, lows = [], []
        for c in range(comps):
            upper, lower = sides(scal_ref, side_ref, sideo_ref, (z_at, slice(c * size_x, (c + 1) * size_x)))
            ups.append(upper)
            lows.append(lower)
            tile_now, tile_old = halo_tiles(upper, lower)
            now_ref[z_at, c, 1:size_x + 1, 0:size_y] = un[c]
            now_ref[z_at, c, 1:size_x + 1, size_y:rows] = tile_now
            old_ref[z_at, c, 1:size_x + 1, 0:size_y] = up[c]
            old_ref[z_at, c, 1:size_x + 1, size_y:rows] = tile_old
        rate_ref[z_at, :, 0:size_y] = lat[...] * speed[None]
        rate_ref[z_at, :, size_y:rows] = halo_rate(ups, lows)
    for side in range(2):
        for z in range(2):
            for d in range(NSTEP):
                ratef_ref[side, z, d] = rate_ref[z, d if side else size_x - 1 - d]
    refs = [now_ref, old_ref]
    for n in range(NSTEP):
        now, old = refs[n % 2], refs[(n + 1) % 2]
        for side in range(2):
            for z in range(2):
                for c in range(comps):
                    face_ref[side, z, n * comps + c] = now[z, c, 1 if side else size_x]

        def step(x, carry, now=now, old=old, n=n, halves=(0, 1)):
            for c in range(comps):
                centre = now[0, c, x + 1], now[1, c, x + 1]
                sums = inplane(*centre)
                for z in halves:
                    lap = sums[z] + (now[z, c, x] + now[z, c, x + 2])
                    value = (
                        2.0 * centre[z] - old[z, c, x + 1] + rate_ref[z, x] * lap + drive_ref[n, z, c, x]
                    )
                    if len(halves) == 2:
                        old[z, c, x + 1] = value
                    else:
                        final_ref[c, x] = value[0:size_y]
                        before_ref[c, x] = centre[z][0:size_y]
            return carry

        if n < NSTEP - 1:
            lax.fori_loop(0, size_x, step, 0, unroll=size_x)
        else:
            for z in range(2):
                @pl.when(mine == z)
                def _(step=step, z=z):
                    lax.fori_loop(0, size_x, functools.partial(step, halves=(z,)), 0, unroll=size_x)


def corrected(scal_ref, final_in, before_in, face_ref, ratef_ref, coded_ref, recv_ref, high, edges):
    comps, size_x, size_y, size_z = final_in.shape
    a, mine = scal_ref[0], scal_ref[2]
    side = jnp.where(high, 0, 1)
    inside = jnp.where(high, a < scal_ref[3] - 1, a > 0)
    expand_all(coded_ref, recv_ref, face_groups(comps))

    def theirs(z, at):
        return jnp.where(inside, face_plane(recv_ref, z, at, comps), 0.0)

    def correct(own):
        rate = {}
        for z in range(2):
            for m in range(NSTEP):
                rate[z, -m] = ratef_ref[side, z, m]
            for m in (1, 2):
                rate[z, m] = theirs(z, NSTEP * comps + m - 1)
        for c in range(comps):
            last, now = {}, {}
            for n in range(NSTEP):
                later = {}
                for m in range(-n, min(n + 1, NSTEP - 1 - n) + 1):
                    centre = [now.get((z, m)) for z in range(2)]
                    sums = inplane(*centre) if centre[0] is not None else (None, None)
                    for z in range(2) if n < NSTEP - 1 else (own,):
                        terms = [sums[z], now.get((z, m - 1)), now.get((z, m + 1))]
                        if m == 0:
                            terms.append(theirs(z, n * comps + c))
                        if m == 1:
                            terms.append(face_ref[side, z, n * comps + c])
                        value = functools.reduce(lambda p, q: p + q, [t for t in terms if t is not None])
                        value = rate[z, m] * value
                        if centre[z] is not None:
                            value = value + 2.0 * centre[z]
                        if (z, m) in last:
                            value = value - last[z, m]
                        later[z, m] = value
                last, now = now, later
            for values, source, edge in zip((now, last), (final_in, before_in), edges):
                depth = edge.shape[1]
                for m in range(1 - depth, 1):
                    x, at = jnp.where(high, size_x - 1 + m, -m), jnp.where(high, depth - 1 + m, -m)
                    edge[c, at] = source[c, x] + values[own, m][0:size_y]

    for z in range(2):
        pl.when(mine == z)(functools.partial(correct, z))


def near_kernel(
    scal_ref, final_in, before_in, face_ref, ratef_ref, coded_ref, final_edge, before_edge, recv_ref
):
    high = lax.rem(scal_ref[0] + scal_ref[2], 2) == 0
    edges = final_edge, before_edge
    corrected(scal_ref, final_in, before_in, face_ref, ratef_ref, coded_ref, recv_ref, high, edges)


def far_kernel(
    scal_ref, final_in, before_in, face_ref, ratef_ref, coded_ref, final_near, before_near,
    final_ref, before_ref, recv_ref, final_edge, before_edge, sems,
):
    size_x = final_in.shape[1]
    high = lax.rem(scal_ref[0] + scal_ref[2], 2) == 1
    copies = []

    def begin(src, target, first, count):
        copies.append(pltpu.make_async_copy(src, target.at[:, pl.ds(first, count)], sems.at[len(copies)]))
        copies[-1].start()

    outputs = ((final_in, final_near, final_ref, final_edge), (before_in, before_near, before_ref, before_edge))
    for source, near, target, edge in outputs:
        depth = edge.shape[1]
        begin(near, target, jnp.where(high, 0, size_x - depth), depth)
        begin(source.at[:, pl.ds(depth, size_x - 2 * depth)], target, depth, size_x - 2 * depth)
    edges = final_edge, before_edge
    corrected(scal_ref, final_in, before_in, face_ref, ratef_ref, coded_ref, recv_ref, high, edges)
    for source, near, target, edge in outputs:
        depth = edge.shape[1]
        begin(edge, target, jnp.where(high, size_x - depth, 0), depth)
    for copy in copies:
        copy.wait()


def send(value, mesh_sizes, route):
    nx, ny, nz = mesh_sizes
    number = lambda i, j, k: (i * ny + j) * nz + k
    pairs = [
        (number(i, j, k), number(*route(i, j, k))) for i in range(nx) for j in range(ny) for k in range(nz)
    ]
    return lax.ppermute(value, ("gx", "gy", "gz"), pairs)


def partner(i, core, count):
    step = 1 if (i + core) % 2 == 0 else -1
    return (i + step) % count


def per_device(
    u_now, u_prev, panels, panel_owner, panel_block, coupling, layer_depth, layer_speed, lateral
):
    sizes = tuple(lax.axis_size(axis) for axis in ("gx", "gy", "gz"))
    nx, ny, nz = sizes
    assert nx % 2 == 0 and ny % 2 == 0 and nz == 2
    comps, size_x, size_y, size_z = u_now.shape
    rows = size_y + HALO
    per_dev, spectral = panels.shape[2], panels.shape[4]
    npanels = ny * per_dev
    scal = jnp.stack(
        [lax.axis_index("gx"), lax.axis_index("gy"), lax.axis_index("gz"), jnp.int32(nx), jnp.int32(ny)]
    ).astype(jnp.int32)

    def swap(value):
        return send(value, sizes, lambda i, j, k: (i, j, 1 - k))

    def route_x(i, j, k):
        return partner(i, k, nx), j, k

    def route_y(i, j, k):
        to = partner(j, k, ny)
        if abs(to - j) != 1 or (ny == 2 and k == 1):
            return i ^ 1, j, k
        return i, to, k

    assert per_dev == PANELS and size_z == LANES
    vmem = pl.BlockSpec(memory_space=pltpu.VMEM)
    smem = pl.BlockSpec(memory_space=pltpu.SMEM)
    params = pltpu.CompilerParams(vmem_limit_bytes=48 * 1024 * 1024)
    table = jnp.asarray(wave_table(spectral, panels.shape[3]))
    width = table.shape[1]
    extra_rows = -(-(LANES + 4 * npanels) // (8 * width)) * 8
    tiles = comps * size_x
    number = tiles + width // size_z * (per_dev // HALO)
    half = jax.ShapeDtypeStruct(coded_shape(number), jnp.int16)
    ints, fields_own, mine, theirs = pl.pallas_call(
        prepare_kernel,
        out_shape=(
            jax.ShapeDtypeStruct((per_dev + extra_rows, width), F32),
            jax.ShapeDtypeStruct((2 * comps + 1,) + u_now.shape[1:], F32),
            half,
            half,
        ),
        in_specs=[smem] + [pl.BlockSpec(memory_space=pl.ANY)] * 10,
        out_specs=(vmem,) * 4,
        scratch_shapes=[
            pltpu.VMEM((2, number, HALO, size_z), F32),
            pltpu.VMEM((per_dev,) + panels.shape[3:], BF16),
            pltpu.VMEM(coupling.shape, F32),
            pltpu.VMEM(table.shape, BF16),
            pltpu.VMEM((1, size_z), jnp.int32),
            pltpu.VMEM((1, npanels), jnp.int32),
            pltpu.VMEM((1, npanels), jnp.int32),
            pltpu.SMEM(layer_speed.shape, F32),
            pltpu.SemaphoreType.DMA((10,)),
        ],
        compiler_params=params,
        name="prepare",
    )(scal, *(
        pltpu.with_memory_space_constraint(value, pltpu.HBM)
        for value in (
            panels.reshape((per_dev,) + panels.shape[3:]), coupling, table, layer_depth.reshape(1, -1),
            panel_owner.reshape(1, -1), panel_block.reshape(1, -1), layer_speed, u_now, u_prev, lateral,
        )
    ))
    both = jnp.stack([mine, swap(theirs)])
    ints, fields_own, both = lax.optimization_barrier((ints, fields_own, both))
    side = send(both, sizes, route_y)
    ints_o, fields_o = swap(ints), swap(fields_own)
    index = pl.pallas_call(
        functools.partial(
            index_kernel, sizes=u_now.shape[1:], block=coupling.shape[1], panels=npanels
        ),
        out_shape=(
            jax.ShapeDtypeStruct((2, 2 * npanels, size_z), F32),
            jax.ShapeDtypeStruct((2, size_x * rows, 2 * npanels), BF16),
        ),
        in_specs=[smem] + [vmem] * 2,
        out_specs=(vmem,) * 2,
        compiler_params=params,
        name="index",
    )(scal, ints, ints_o)
    sets = ()
    if ny == 4:
        forces = both[:, tiles // 2:]
        far = send(forces, sizes, lambda i, j, k: (i, j ^ 2 if k == 0 else 3 - j, k))
        side = jnp.concatenate([side, far], axis=1)
    else:
        pair = jnp.stack([ints[0:per_dev], ints_o[0:per_dev]])
        pair = jnp.where(lax.axis_index("gz") == 0, pair, pair[::-1])
        sets = (jnp.moveaxis(lax.all_gather(pair, "gy"), 0, 1).reshape(2, npanels, -1),)
    side, index, ints_o, fields_o = lax.optimization_barrier((side, index, ints_o, fields_o))
    shared = (scal, fields_own, fields_o, ints, ints_o, *index, side, swap(side)) + sets
    shared_specs = [smem] + [vmem] * (8 + len(sets))
    tiles_scratch = pltpu.VMEM((2, number, HALO, size_z), F32)
    far_scratch = pltpu.VMEM((2, number - tiles, HALO, size_z), F32)
    all_scratch = pltpu.VMEM((2, npanels, width), F32)
    planes = NSTEP * comps
    face_scratch = pltpu.VMEM((2 * face_tiles(comps), HALO, size_z), F32)
    sent = pl.pallas_call(
        face_kernel,
        out_shape=jax.ShapeDtypeStruct(coded_shape(2 * face_tiles(comps)), jnp.int16),
        in_specs=shared_specs,
        out_specs=vmem,
        scratch_shapes=[all_scratch, tiles_scratch, tiles_scratch, far_scratch, far_scratch, face_scratch],
        compiler_params=params,
        name="face",
    )(*shared)
    recv = send(sent, sizes, route_x)
    final, before, face, ratef = pl.pallas_call(
        local_kernel,
        out_shape=(
            jax.ShapeDtypeStruct(u_now.shape, F32),
            jax.ShapeDtypeStruct(u_now.shape, F32),
            jax.ShapeDtypeStruct((2, 2, planes, rows, size_z), F32),
            jax.ShapeDtypeStruct((2, 2, NSTEP, rows, size_z), F32),
        ),
        in_specs=shared_specs,
        out_specs=(vmem,) * 4,
        scratch_shapes=[
            all_scratch,
            tiles_scratch,
            tiles_scratch,
            far_scratch,
            far_scratch,
            pltpu.VMEM((2, comps, size_x + 2, rows, size_z), F32),
            pltpu.VMEM((2, comps, size_x + 2, rows, size_z), F32),
            pltpu.VMEM((2, size_x, rows, size_z), F32),
            pltpu.VMEM((NSTEP, 2, comps, size_x, rows, size_z), F32),
        ],
        compiler_params=params,
        name="local",
    )(*shared)
    final, before, face, ratef, recv = lax.optimization_barrier((final, before, face, ratef, recv))
    recv_o = swap(recv)
    edges = [jax.ShapeDtypeStruct((comps, depth, size_y, size_z), F32) for depth in (NSTEP, NSTEP - 1)]
    whole = (scal, final, before, face, ratef)
    near = pl.pallas_call(
        near_kernel,
        out_shape=tuple(edges),
        in_specs=[smem] + [vmem] * 5,
        out_specs=(vmem, vmem),
        scratch_shapes=[face_scratch],
        compiler_params=params,
        name="near",
    )(*whole, recv)
    near, recv_o = lax.optimization_barrier((near, recv_o))
    return pl.pallas_call(
        far_kernel,
        out_shape=(
            jax.ShapeDtypeStruct(u_now.shape, F32),
            jax.ShapeDtypeStruct(u_now.shape, F32),
        ),
        in_specs=[smem] + [vmem] * 7,
        out_specs=(pl.BlockSpec(memory_space=pl.ANY),) * 2,
        scratch_shapes=[
            face_scratch,
            pltpu.VMEM(edges[0].shape, F32),
            pltpu.VMEM(edges[1].shape, F32),
            pltpu.SemaphoreType.DMA((6,)),
        ],
        compiler_params=params,
        name="far",
    )(*whole, recv_o, *near)


def solution(mesh):
    in_specs = (
        P(None, "gx", "gy", "gz"),
        P(None, "gx", "gy", "gz"),
        P("gx", "gz", "gy", None, None),
        P("gx", "gz", None, None),
        P("gx", "gz", None),
        P(),
        P("gz"),
        P(),
        P("gx", "gy", "gz"),
    )
    out_specs = (P(None, "gx", "gy", "gz"), P(None, "gx", "gy", "gz"))
    return jax.shard_map(
        per_device, mesh=mesh, in_specs=in_specs, out_specs=out_specs, check_vma=False
    )
```

```python
import functools

import jax
import jax.numpy as jnp
import ml_dtypes
import numpy as np
from jax import lax
from jax.experimental import pallas as pl
from jax.experimental.pallas import tpu as pltpu
from jax.sharding import PartitionSpec as P

NSTEP = 4
HALO = 8
LANES = 128
PANELS = 16
TOP = 32000.0
F32 = jnp.float32
BF16 = jnp.bfloat16


def wave_table(count, per_step):
    half = count // 2
    freq = np.float32(2.0 * np.pi) * (np.arange(half, dtype=np.float32) + np.float32(0.5)) / np.float32(count)
    times = np.float32(37.0) + np.arange(NSTEP, dtype=np.float32)
    phase = freq[:, None] * times[None, :]
    table = np.concatenate([np.cos(phase), np.sin(phase)], axis=0) / np.sqrt(np.float32(half))
    wide = np.repeat(table.astype(ml_dtypes.bfloat16), per_step, axis=1)
    return np.pad(wide, ((0, 0), (0, -wide.shape[1] % 128)))


def shift_of(size):
    assert size & (size - 1) == 0
    return size.bit_length() - 1


def iota(shape, dim):
    return lax.broadcasted_iota(jnp.int32, shape, dim)


def spin(value, amount, axis):
    return pltpu.roll(value, amount % value.shape[axis], axis)


def across(z0, z1):
    lanes = z0.shape[-1]
    lane = iota(z0.shape, z0.ndim - 1)
    first, last = lane == 0, lane == lanes - 1
    ax = z0.ndim - 1
    down0, down1 = spin(z0, 1, ax), spin(z1, 1, ax)
    up0, up1 = spin(z0, -1, ax), spin(z1, -1, ax)
    sum0 = jnp.where(first, 0.0, down0) + jnp.where(last, up1, up0)
    sum1 = jnp.where(first, down0, down1) + jnp.where(last, 0.0, up1)
    return sum0, sum1


def inplane(z0, z1):
    ax = z0.ndim - 2
    sum0, sum1 = across(z0, z1)
    sum0 = sum0 + (spin(z0, 1, ax) + spin(z0, -1, ax)) - 6.0 * z0
    sum1 = sum1 + (spin(z1, 1, ax) + spin(z1, -1, ax)) - 6.0 * z1
    return sum0, sum1


def row_scales(exponents):
    return jnp.exp2(exponents) * (1.0 / TOP)


def quantize(load, groups, out_ref):
    shape = (HALO, LANES)
    lane = iota(shape, 1)
    peak = jnp.zeros(shape, F32)
    for group in range(max(groups) + 1):
        members = [jnp.abs(load(t)) for t, of in enumerate(groups) if of == group]
        top = functools.reduce(jnp.maximum, members)
        peak = jnp.where(lane == group, jnp.max(top, axis=1, keepdims=True), peak)
    exponents = jnp.ceil(jnp.log2(jnp.maximum(peak, 1e-30)))
    factor = jnp.exp2(-exponents) * TOP
    zero = jnp.zeros(shape, jnp.int32)
    wide = [jnp.broadcast_to(factor[:, g:g + 1], shape) for g in range(max(groups) + 1)]
    parts = [jnp.round(load(t) * wide[of]).astype(jnp.int32) for t, of in enumerate(groups)]
    parts += [zero] * (len(groups) % 2) + [exponents.astype(jnp.int32), zero]
    for i in range(out_ref.shape[0]):
        out_ref[i] = jnp.concatenate(parts[2 * i:2 * i + 2], axis=0).astype(jnp.int16)


def coded_shape(number):
    return ((number + 1) // 2 + 1, 2 * HALO, LANES)


def side_groups(comps, size_x, rest):
    near = [c * (size_x // NSTEP) + x // NSTEP for c in range(comps) for x in range(size_x)]
    return near + [max(near) + 1 + i for i in range(rest)]


def scales_of(coded):
    return row_scales(coded.astype(jnp.int32)[0:HALO].astype(F32))


def expand(load, store, scales, blocks):
    for at, one, two in blocks:
        pair = load(at).astype(jnp.int32).astype(F32)
        store(2 * at, pair[0:HALO] * scales[:, one:one + 1])
        store(2 * at + 1, pair[HALO:] * scales[:, two:two + 1])


def expand_all(ref, tiles_ref, groups):
    def store(t, value):
        tiles_ref[t] = value

    expand(lambda i: ref[i], store, scales_of(ref[ref.shape[0] - 1]), [
        (t // 2, groups[t], groups[t + 1]) for t in range(0, len(groups), 2)
    ])


def expand_sides(ref, tiles_ref, far_ref, first, groups, choose):
    last = len(groups) // 2
    forces = len(groups) - far_ref.shape[1]
    for half in range(2):
        z = first if half == 0 else 1 - first

        def store(t, value):
            tiles_ref[z, t] = value

        def store_far(t, value):
            far_ref[z, t] = value

        scales = scales_of(ref[half, last])
        for moved, blocks in choose(scales):
            expand(lambda i: ref[half, i], store, moved, blocks)
        if ref.shape[1] > last + 1:
            expand(lambda i: ref[half, last + 1 + i], store_far, scales_of(ref[half, ref.shape[1] - 1]), [
                ((t - forces) // 2, groups[t], groups[t + 1]) for t in range(forces, len(groups), 2)
            ])


def position():
    return [lax.axis_index(axis) for axis in ("gx", "gy", "gz")] + [lax.axis_size("gx"), lax.axis_size("gy")]


def prepare_kernel(
    panels_hbm, coupling_hbm, table_hbm, depth_hbm, owner_hbm, block_hbm, speed_hbm,
    un_hbm, up_hbm, lat_hbm, out_ref, state_ref, theirs_ref, tiles_ref,
    panels_ref, coupling_ref, table_ref, depth_ref, owner_ref, block_ref, speed_ref, sems,
):
    scal_ref = position()
    comps = un_hbm.shape[0]
    un_ref, up_ref, lat_ref = state_ref.at[0:comps], state_ref.at[comps:2 * comps], state_ref.at[2 * comps]
    pairs = (
        (panels_hbm, panels_ref), (table_hbm, table_ref), (coupling_hbm, coupling_ref),
        (depth_hbm, depth_ref), (owner_hbm, owner_ref), (block_hbm, block_ref), (speed_hbm, speed_ref),
        (un_hbm, un_ref), (up_hbm, up_ref), (lat_hbm, lat_ref),
    )
    copies = [pltpu.make_async_copy(src, dst, sems.at[i]) for i, (src, dst) in enumerate(pairs)]
    for copy in copies:
        copy.start()
    for copy in copies[:7]:
        copy.wait()
    count, rows, spectral = panels_ref.shape
    block = rows // comps
    lanes = table_ref.shape[1]
    free = jnp.dot(
        panels_ref[...].reshape(count * rows, spectral), table_ref[...], preferred_element_type=F32
    )
    weights = coupling_ref[...].reshape(rows, block)
    stacked = jnp.concatenate([weights] * NSTEP + [jnp.zeros((lanes - NSTEP * rows, block), F32)], axis=0)
    pick = ((iota((rows, block), 0) & (block - 1)) == iota((rows, block), 1)).astype(F32)
    spread = lax.dot_general(
        pick, stacked, (((1,), (1,)), ((), ())), precision=lax.Precision.HIGHEST, preferred_element_type=F32
    )
    comp_row = iota((rows, lanes), 0) >> shift_of(block)
    comp_lane = iota((rows, lanes), 1) >> shift_of(block)
    same = comp_lane == comp_row
    for step in range(1, NSTEP):
        same = same | (comp_lane == comp_row + step * comps)
    spread = jnp.where(same, spread, 0.0)
    out_ref[0:count] = jnp.sum(free.reshape(count, rows, lanes) * spread[None], axis=1)
    out_ref[count:] = jnp.zeros((out_ref.shape[0] - count, lanes), F32)
    speed = jnp.zeros(depth_ref.shape, F32)
    for layer in range(speed_ref.shape[0]):
        speed = jnp.where(depth_ref[...] == layer, speed_ref[layer], speed)
    pieces = [speed]
    for ref in (owner_ref, block_ref):
        twice = jnp.concatenate([ref[...], ref[...]], axis=1)
        pieces += [twice[:, i:i + LANES] for i in range(0, twice.shape[1], LANES)]
    for i, piece in enumerate(pieces):
        row, at = count + i * LANES // lanes, i * LANES % lanes
        out_ref[row:row + 1, at:at + LANES] = piece.astype(F32)
    for copy in copies[7:]:
        copy.wait()
    code_side(state_ref, out_ref, 1 - lax.rem(scal_ref[1] + scal_ref[2], 2), tiles_ref, theirs_ref)


def mine_kernel(state_ref, force_ref, mine_ref, tiles_ref):
    scal_ref = position()
    code_side(state_ref, force_ref, lax.rem(scal_ref[1] + scal_ref[2], 2), tiles_ref, mine_ref)


def code_side(state_ref, force_ref, which, tiles_ref, coded_ref):
    un_ref, up_ref, lat_ref = fields(state_ref)
    comps, size_x, size_y, size_z = un_ref.shape
    count, lanes = PANELS, force_ref.shape[1]
    speed = listed(force_ref, LANES, 0)
    sub = iota((size_x, HALO, size_z), 1)

    def fill(side):
        base = 0 if side else size_y - HALO
        rate = lat_ref[:, base:base + HALO, :] * speed[None]
        for c in range(comps):
            now = un_ref[c, :, base:base + HALO, :]
            old = spin(up_ref[c, :, base:base + HALO, :], HALO // 2, 1)
            keep = sub < HALO // 2 if side else sub >= HALO // 2
            row = c if side else HALO - 1 - c
            tile = jnp.where(keep, now, old)
            tile = jnp.where(sub == (HALO - 1 if side else 0), rate[:, row:row + 1, :], tile)
            tiles_ref[c * size_x:(c + 1) * size_x] = tile

    for side in range(2):
        pl.when(which == side)(functools.partial(fill, side))
    for part in range(lanes // size_z):
        for piece in range(count // HALO):
            at = comps * size_x + part * (count // HALO) + piece
            tiles_ref[at] = force_ref[piece * HALO:(piece + 1) * HALO, part * size_z:(part + 1) * size_z]
    groups = side_groups(comps, size_x, tiles_ref.shape[0] - comps * size_x)
    quantize(lambda t: tiles_ref[t], groups, coded_ref)


def listed(ref, panels, which):
    lanes = ref.shape[1]
    width = -(-2 * panels // LANES)
    first, number = ((0, 1), (1, width), (1 + width, width))[which]
    out = []
    for i in range(first, first + number):
        row, at = PANELS + i * LANES // lanes, i * LANES % lanes
        out.append(ref[row:row + 1, at:at + LANES])
    return jnp.concatenate(out, axis=1)


def place_forces(scal_ref, ints_ref, intso_ref, sets, all_ref):
    o, mine = scal_ref[1], scal_ref[2]
    side_ref, sideo_ref, far_ref, faro_ref = sets
    count, lanes = PANELS, ints_ref.shape[1]
    beside, opposite, mirror = o + 1 - 2 * lax.rem(o, 2), lax.rem(o + 2, 4), 3 - o
    size_z = side_ref.shape[-1]
    step = count // HALO
    here = mine == 0

    def spot(j):
        return pl.ds(pl.multiple_of(j * count, count), count)

    for ref, j in (
        (side_ref, jnp.where(here, beside, mirror)),
        (sideo_ref, jnp.where(here, mirror, beside)),
        (far_ref, jnp.where(here, opposite, mirror)),
        (faro_ref, jnp.where(here, mirror, opposite)),
    ):
        first = ref.shape[1] - lanes // size_z * step
        for z in range(2):
            for part in range(lanes // size_z):
                at = first + part * step
                all_ref[z, spot(j), part * size_z:(part + 1) * size_z] = ref[z, at:at + step].reshape(count, size_z)
    all_ref[mine, spot(o), :] = ints_ref[0:count]
    all_ref[1 - mine, spot(o), :] = intso_ref[0:count]
    return all_ref


def index_kernel(ints_ref, intso_ref, at_ref, hit_ref, *, sizes, block, panels):
    scal_ref = position()
    size_x, size_y, size_z = sizes
    rows = size_y + HALO
    for z, ints in ((scal_ref[2], ints_ref), (1 - scal_ref[2], intso_ref)):
        keys, depth = panel_keys(ints, scal_ref[1], panels, rows, size_x, size_y, size_z // block)
        at = (iota((size_z, depth.shape[1]), 0) >> shift_of(block)) == depth
        at_ref[z] = jnp.transpose(at.astype(F32))
        hit = iota((size_x * rows, keys.shape[1]), 0) == keys
        hit_ref[z] = hit.astype(F32).astype(BF16)


def panel_keys(ints_ref, o, panels, rows, size_x, size_y, zblocks):
    owner = listed(ints_ref, panels, 1).astype(jnp.int32)
    block = listed(ints_ref, panels, 2).astype(jnp.int32)
    depth = block & (zblocks - 1)
    y = (block >> shift_of(zblocks)) & (size_y - 1)
    x = block >> (shift_of(zblocks) + shift_of(size_y))
    key = x * rows
    reach = NSTEP - 1
    row = jnp.where(owner == o, y, -1)
    row = jnp.where((owner == o + 1) & (y < reach), y + size_y, row)
    row = jnp.where((owner == o - 1) & (y >= size_y - reach), y + rows - size_y, row)
    return jnp.where(row < 0, -1, key + row), depth


def spread_forces(force, at, block, steps):
    high = force.astype(BF16).astype(F32)
    both = jnp.concatenate([high, force - high], axis=0)
    rows, size_z = at.shape
    lane = iota((rows, size_z), 1) >> shift_of(block)
    base = (
        (iota((size_z, size_z), 0) & (block - 1)) == (iota((size_z, size_z), 1) & (block - 1))
    ).astype(BF16)
    per_tile = size_z // block
    out = []
    for q in range(steps * 3):
        part = both[:, (q // per_tile) * size_z:(q // per_tile + 1) * size_z]
        part = jnp.where(lane == q % per_tile, part, 0.0).astype(BF16)
        wide = jnp.dot(part, base, preferred_element_type=F32)
        out.append((wide * at).astype(BF16))
    return jnp.concatenate(out, axis=1)


def fields(state_ref):
    comps = state_ref.shape[0] // 2
    return state_ref.at[0:comps], state_ref.at[comps:2 * comps], state_ref.at[2 * comps]


def halo_tiles(high, low):
    sub = iota(high.shape, high.ndim - 2)
    upper = sub < HALO // 2
    now = jnp.where(upper, high, low)
    old = spin(jnp.where(upper, low, high), HALO // 2, high.ndim - 2)
    return now, old


def halo_rate(highs, lows):
    sub = iota(highs[0].shape, highs[0].ndim - 2)
    tile = jnp.zeros(highs[0].shape, F32)
    ends = slice(HALO - 1, HALO), slice(0, 1)
    for c in range(3):
        tile = jnp.where(sub == c, highs[c][..., ends[0], :], tile)
        tile = jnp.where(sub == HALO - 1 - c, lows[c][..., ends[1], :], tile)
    return tile


def sides(scal_ref, side_ref, sideo_ref, at):
    o, mine = scal_ref[1], scal_ref[2]
    high = lax.rem(o + mine, 2) == 0
    one, two = side_ref[at], sideo_ref[at]
    upper = jnp.where(o < scal_ref[4] - 1, jnp.where(high, one, two), 0.0)
    lower = jnp.where(o > 0, jnp.where(high, two, one), 0.0)
    return upper, lower


def forces_of(scal_ref, ints_ref, intso_ref, rest, all_ref, scratch):
    if rest:
        return rest[0]
    return place_forces(scal_ref, ints_ref, intso_ref, scratch, all_ref)


def face_kernel(
    state_ref, stateo_ref, ints_ref, intso_ref, at_ref, hit_ref, coded_ref, codedo_ref, *rest,
):
    scal_ref = position()
    *rest, out_ref, all_ref, side_ref, sideo_ref, far_ref, faro_ref, faces_ref = rest
    scratch = side_ref, sideo_ref, far_ref, faro_ref
    (un_ref, up_ref, lat_ref), (uno_ref, upo_ref, lato_ref) = fields(state_ref), fields(stateo_ref)
    comps, size_x, size_y, size_z = un_ref.shape
    rows = size_y + HALO
    tiles = comps * size_x
    a, o, mine = scal_ref[0], scal_ref[1], scal_ref[2]
    high = lax.rem(a + mine, 2) == 0
    skip = jnp.where(high, size_x - NSTEP, 0)

    groups = side_groups(comps, size_x, side_ref.shape[1] - tiles)

    def choose(scales):
        moved = pltpu.roll(scales, lax.rem(LANES - lax.div(skip, NSTEP), LANES), 1)
        near = [first + i for first in range(0, tiles, size_x) for i in range(0, NSTEP, 2)]
        rest = [(t // 2, groups[t], groups[t + 1]) for t in range(tiles, len(groups), 2)]
        return (moved, [(t // 2 + lax.div(skip, 2), groups[t], groups[t + 1]) for t in near]), (scales, rest)

    expand_sides(coded_ref, side_ref, far_ref, mine, groups, choose)
    expand_sides(codedo_ref, sideo_ref, faro_ref, 1 - mine, groups, choose)
    forces = forces_of(scal_ref, ints_ref, intso_ref, rest, all_ref, scratch)
    own = mine == 0
    now, old, rate, drive = {}, {}, {}, {}
    for z in range(2):
        wide = spread_forces(forces[z], at_ref[z], 16, NSTEP - 1)
        first = pl.multiple_of(jnp.where(high, size_x - NSTEP, 0) * rows, 2 * HALO)
        hit = hit_ref[z, pl.ds(first, NSTEP * rows)]
        got = jnp.dot(hit, wide, preferred_element_type=F32)
        got = got.reshape(NSTEP, rows, wide.shape[1])
        for d in range(1, NSTEP):
            for n in range(NSTEP - d):
                for c in range(comps):
                    q = (n * comps + c) * size_z
                    drive[z, n, d, c] = jnp.where(
                        high, got[NSTEP - d, :, q:q + size_z], got[d - 1, :, q:q + size_z]
                    )
        speed = jnp.where(
            own if z == 0 else jnp.logical_not(own),
            listed(ints_ref, LANES, 0),
            listed(intso_ref, LANES, 0),
        )
        near = own if z == 0 else jnp.logical_not(own)
        for d in range(1, NSTEP + 1):
            x = jnp.where(high, size_x - d, d - 1)
            ups, lows = [], []
            for c in range(comps):
                upper, lower = sides(scal_ref, side_ref, sideo_ref, (z, c * size_x + x))
                ups.append(upper)
                lows.append(lower)
                tile_now, tile_old = halo_tiles(upper, lower)
                centre = jnp.where(near, un_ref[c, x], uno_ref[c, x])
                now[z, d, c] = jnp.concatenate([centre, tile_now], axis=0)
                if d < NSTEP:
                    centre = jnp.where(near, up_ref[c, x], upo_ref[c, x])
                    old[z, d, c] = jnp.concatenate([centre, tile_old], axis=0)
            if d < NSTEP:
                centre = jnp.where(near, lat_ref[x], lato_ref[x]) * speed
                rate[z, d] = jnp.concatenate([centre, halo_rate(ups, lows)], axis=0)
    series = {(z, 0, c): now[z, 1, c] for z in range(2) for c in range(comps)}
    for n in range(1, NSTEP):
        later = {}
        for d in range(1, NSTEP - n + 1):
            for c in range(comps):
                sums = inplane(now[0, d, c], now[1, d, c])
                for z in range(2):
                    lap = sums[z] + now[z, d + 1, c]
                    if d > 1:
                        lap = lap + now[z, d - 1, c]
                    later[z, d, c] = (
                        2.0 * now[z, d, c] - old[z, d, c] + rate[z, d] * lap + drive[z, n - 1, d, c]
                    )
        old, now = now, later
        for z in range(2):
            for c in range(comps):
                series[z, n, c] = now[z, 1, c]
    sub = iota((HALO, size_z), 0)
    middle = (sub == HALO // 2 - 1) | (sub == HALO // 2)
    ends = (sub < 2) | (sub >= HALO - 2)
    for z in range(2):
        planes = [series[z, n, c] for n in range(NSTEP) for c in range(comps)] + [rate[z, 1], rate[z, 2]]
        rims = [plane[size_y:rows] for plane in planes]
        tails = [jnp.where(middle, spin(rims[2 * comps + c], HALO // 2, 0), rims[c]) for c in range(comps)]
        tails.append(jnp.where(ends, rims[comps], spin(rims[comps + 1], HALO // 2, 0)))
        tails.append(jnp.where(ends, rims[comps + 2], spin(rims[NSTEP * comps], HALO // 2, 0)))
        base = z * face_tiles(comps)
        for i, plane in enumerate(planes):
            for half in range(2):
                faces_ref[base + 2 * i + half] = plane[half * HALO:(half + 1) * HALO]
        for i, tail in enumerate(tails):
            faces_ref[base + 2 * len(planes) + i] = tail
    quantize(lambda t: faces_ref[t], face_groups(comps), out_ref)


def face_tiles(comps):
    return 2 * (NSTEP * comps + 2) + comps + 2


def face_groups(comps):
    groups = []
    for z in range(2):
        base = z * (2 * NSTEP + 5)
        groups += [base + 2 * n + half for n in range(NSTEP) for _ in range(comps) for half in range(2)]
        groups += [base + 2 * NSTEP + half for _ in range(2) for half in range(2)]
        groups += [base + 2 * NSTEP + 2] * comps + [base + 2 * NSTEP + 3, base + 2 * NSTEP + 4]
    return groups


def face_plane(tiles_ref, z, i, comps):
    count = NSTEP * comps + 2
    base = z * face_tiles(comps)
    tail = base + 2 * count
    parts = [tiles_ref[base + 2 * i], tiles_ref[base + 2 * i + 1]]
    turned = lambda at: spin(tiles_ref[at], HALO // 2, 0)
    if i < comps:
        parts.append(tiles_ref[tail + i])
    elif i < comps + 3:
        at, other = ((tail + comps, False), (tail + comps, True), (tail + comps + 1, False))[i - comps]
        parts.append(turned(at) if other else tiles_ref[at])
    elif 2 * comps <= i < 3 * comps:
        parts.append(turned(tail + i - 2 * comps))
    elif i == NSTEP * comps:
        parts.append(turned(tail + comps + 1))
    else:
        parts.append(jnp.zeros(parts[0].shape, F32))
    return jnp.concatenate(parts, axis=0)


def local_kernel(
    state_ref, stateo_ref, ints_ref, intso_ref, at_ref, hit_ref, coded_ref, codedo_ref, *rest,
):
    scal_ref = position()
    now_ref, old_ref, rate_ref, drive_ref = rest[-4:]
    all_ref, side_ref, sideo_ref, far_ref, faro_ref = rest[-9:-4]
    *rest, final_ref, before_ref, face_ref, ratef_ref = rest[:-9]
    scratch = side_ref, sideo_ref, far_ref, faro_ref
    (un_ref, up_ref, lat_ref), (uno_ref, upo_ref, lato_ref) = fields(state_ref), fields(stateo_ref)
    comps, size_x, size_y, size_z = un_ref.shape
    rows = size_y + HALO
    tiles = comps * size_x
    o, mine = scal_ref[1], scal_ref[2]
    groups = side_groups(comps, size_x, side_ref.shape[1] - comps * size_x)
    choose = lambda scales: (
        (scales, [(t // 2, groups[t], groups[t + 1]) for t in range(0, len(groups), 2)]),
    )
    expand_sides(coded_ref, side_ref, far_ref, mine, groups, choose)
    expand_sides(codedo_ref, sideo_ref, faro_ref, 1 - mine, groups, choose)
    forces = forces_of(scal_ref, ints_ref, intso_ref, rest, all_ref, scratch)
    own = mine == 0
    for z in range(2):
        wide = spread_forces(forces[z], at_ref[z], 16, NSTEP)
        hit = hit_ref[z]
        for n in range(NSTEP):
            span = comps * size_z
            got = jnp.dot(hit, wide[:, n * span:(n + 1) * span], preferred_element_type=F32)
            for c in range(comps):
                drive_ref[n, z, c] = got[:, c * size_z:(c + 1) * size_z].reshape(size_x, rows, size_z)
    edge = jnp.zeros((rows, size_z), F32)
    for z in range(2):
        for c in range(comps):
            for ref in (now_ref, old_ref):
                ref[z, c, 0] = edge
                ref[z, c, size_x + 1] = edge
    for z_at, un, up, lat, ints in (
        (mine, un_ref, up_ref, lat_ref, ints_ref),
        (1 - mine, uno_ref, upo_ref, lato_ref, intso_ref),
    ):
        speed = listed(ints, LANES, 0)
        ups, lows = [], []
        for c in range(comps):
            upper, lower = sides(scal_ref, side_ref, sideo_ref, (z_at, slice(c * size_x, (c + 1) * size_x)))
            ups.append(upper)
            lows.append(lower)
            tile_now, tile_old = halo_tiles(upper, lower)
            now_ref[z_at, c, 1:size_x + 1, 0:size_y] = un[c]
            now_ref[z_at, c, 1:size_x + 1, size_y:rows] = tile_now
            old_ref[z_at, c, 1:size_x + 1, 0:size_y] = up[c]
            old_ref[z_at, c, 1:size_x + 1, size_y:rows] = tile_old
        rate_ref[z_at, :, 0:size_y] = lat[...] * speed[None]
        rate_ref[z_at, :, size_y:rows] = halo_rate(ups, lows)
    for side in range(2):
        for z in range(2):
            for d in range(NSTEP):
                ratef_ref[side, z, d] = rate_ref[z, d if side else size_x - 1 - d]
    refs = [now_ref, old_ref]
    for n in range(NSTEP):
        now, old = refs[n % 2], refs[(n + 1) % 2]
        for side in range(2):
            for z in range(2):
                for c in range(comps):
                    face_ref[side, z, n * comps + c] = now[z, c, 1 if side else size_x]

        def step(x, carry, now=now, old=old, n=n, halves=(0, 1)):
            for c in range(comps):
                centre = now[0, c, x + 1], now[1, c, x + 1]
                sums = inplane(*centre)
                for z in halves:
                    lap = sums[z] + (now[z, c, x] + now[z, c, x + 2])
                    value = (
                        2.0 * centre[z] - old[z, c, x + 1] + rate_ref[z, x] * lap + drive_ref[n, z, c, x]
                    )
                    if len(halves) == 2:
                        old[z, c, x + 1] = value
                    else:
                        final_ref[c, x] = value[0:size_y]
                        before_ref[c, x] = centre[z][0:size_y]
            return carry

        if n < NSTEP - 1:
            lax.fori_loop(0, size_x, step, 0, unroll=size_x)
        else:
            for z in range(2):
                @pl.when(mine == z)
                def _(step=step, z=z):
                    lax.fori_loop(0, size_x, functools.partial(step, halves=(z,)), 0, unroll=size_x)


def corrected(scal_ref, final_in, before_in, face_ref, ratef_ref, coded_ref, recv_ref, high, edges):
    comps, size_x, size_y, size_z = final_in.shape
    a, mine = scal_ref[0], scal_ref[2]
    side = jnp.where(high, 0, 1)
    inside = jnp.where(high, a < scal_ref[3] - 1, a > 0)
    expand_all(coded_ref, recv_ref, face_groups(comps))

    def theirs(z, at):
        return jnp.where(inside, face_plane(recv_ref, z, at, comps), 0.0)

    def correct(own):
        rate = {}
        for z in range(2):
            for m in range(NSTEP):
                rate[z, -m] = ratef_ref[side, z, m]
            for m in (1, 2):
                rate[z, m] = theirs(z, NSTEP * comps + m - 1)
        for c in range(comps):
            last, now = {}, {}
            for n in range(NSTEP):
                later = {}
                for m in range(-n, min(n + 1, NSTEP - 1 - n) + 1):
                    centre = [now.get((z, m)) for z in range(2)]
                    sums = inplane(*centre) if centre[0] is not None else (None, None)
                    for z in range(2) if n < NSTEP - 1 else (own,):
                        terms = [sums[z], now.get((z, m - 1)), now.get((z, m + 1))]
                        if m == 0:
                            terms.append(theirs(z, n * comps + c))
                        if m == 1:
                            terms.append(face_ref[side, z, n * comps + c])
                        value = functools.reduce(lambda p, q: p + q, [t for t in terms if t is not None])
                        value = rate[z, m] * value
                        if centre[z] is not None:
                            value = value + 2.0 * centre[z]
                        if (z, m) in last:
                            value = value - last[z, m]
                        later[z, m] = value
                last, now = now, later
            for values, source, edge in zip((now, last), (final_in, before_in), edges):
                depth = edge.shape[1]
                for m in range(1 - depth, 1):
                    x, at = jnp.where(high, size_x - 1 + m, -m), jnp.where(high, depth - 1 + m, -m)
                    edge[c, at] = source[c, x] + values[own, m][0:size_y]

    for z in range(2):
        pl.when(mine == z)(functools.partial(correct, z))


def near_kernel(
    final_in, before_in, face_ref, ratef_ref, coded_ref, final_edge, before_edge, recv_ref
):
    scal_ref = position()
    high = lax.rem(scal_ref[0] + scal_ref[2], 2) == 0
    edges = final_edge, before_edge
    corrected(scal_ref, final_in, before_in, face_ref, ratef_ref, coded_ref, recv_ref, high, edges)


def far_kernel(
    final_in, before_in, face_ref, ratef_ref, coded_ref, final_near, before_near,
    final_ref, before_ref, recv_ref, final_edge, before_edge, sems,
):
    scal_ref = position()
    size_x = final_in.shape[1]
    high = lax.rem(scal_ref[0] + scal_ref[2], 2) == 1
    copies = []

    def begin(src, target, first, count):
        copies.append(pltpu.make_async_copy(src, target.at[:, pl.ds(first, count)], sems.at[len(copies)]))
        copies[-1].start()

    outputs = ((final_in, final_near, final_ref, final_edge), (before_in, before_near, before_ref, before_edge))
    for source, near, target, edge in outputs:
        depth = edge.shape[1]
        begin(near, target, jnp.where(high, 0, size_x - depth), depth)
        begin(source.at[:, pl.ds(depth, size_x - 2 * depth)], target, depth, size_x - 2 * depth)
    edges = final_edge, before_edge
    corrected(scal_ref, final_in, before_in, face_ref, ratef_ref, coded_ref, recv_ref, high, edges)
    for source, near, target, edge in outputs:
        depth = edge.shape[1]
        begin(edge, target, jnp.where(high, size_x - depth, 0), depth)
    for copy in copies:
        copy.wait()


def send(value, mesh_sizes, route):
    nx, ny, nz = mesh_sizes
    number = lambda i, j, k: (i * ny + j) * nz + k
    pairs = [
        (number(i, j, k), number(*route(i, j, k))) for i in range(nx) for j in range(ny) for k in range(nz)
    ]
    return lax.ppermute(value, ("gx", "gy", "gz"), pairs)


def partner(i, core, count):
    step = 1 if (i + core) % 2 == 0 else -1
    return (i + step) % count


def per_device(
    u_now, u_prev, panels, panel_owner, panel_block, coupling, layer_depth, layer_speed, lateral
):
    sizes = tuple(lax.axis_size(axis) for axis in ("gx", "gy", "gz"))
    nx, ny, nz = sizes
    assert nx % 2 == 0 and ny % 2 == 0 and nz == 2
    comps, size_x, size_y, size_z = u_now.shape
    rows = size_y + HALO
    per_dev, spectral = panels.shape[2], panels.shape[4]
    npanels = ny * per_dev

    def swap(value):
        return send(value, sizes, lambda i, j, k: (i, j, 1 - k))

    def route_x(i, j, k):
        return partner(i, k, nx), j, k

    def route_y(i, j, k):
        to = partner(j, k, ny)
        if abs(to - j) != 1 or (ny == 2 and k == 1):
            return i ^ 1, j, k
        return i, to, k

    assert per_dev == PANELS and size_z == LANES
    vmem = pl.BlockSpec(memory_space=pltpu.VMEM)
    params = pltpu.CompilerParams(vmem_limit_bytes=48 * 1024 * 1024)
    table = jnp.asarray(wave_table(spectral, panels.shape[3]))
    width = table.shape[1]
    extra_rows = -(-(LANES + 4 * npanels) // (8 * width)) * 8
    tiles = comps * size_x
    number = tiles + width // size_z * (per_dev // HALO)
    half = jax.ShapeDtypeStruct(coded_shape(number), jnp.int16)
    ints, fields_own, theirs = pl.pallas_call(
        prepare_kernel,
        out_shape=(
            jax.ShapeDtypeStruct((per_dev + extra_rows, width), F32),
            jax.ShapeDtypeStruct((2 * comps + 1,) + u_now.shape[1:], F32),
            half,
        ),
        in_specs=[pl.BlockSpec(memory_space=pl.ANY)] * 10,
        out_specs=(vmem,) * 3,
        scratch_shapes=[
            pltpu.VMEM((number, HALO, size_z), F32),
            pltpu.VMEM((per_dev,) + panels.shape[3:], BF16),
            pltpu.VMEM(coupling.shape, F32),
            pltpu.VMEM(table.shape, BF16),
            pltpu.VMEM((1, size_z), jnp.int32),
            pltpu.VMEM((1, npanels), jnp.int32),
            pltpu.VMEM((1, npanels), jnp.int32),
            pltpu.SMEM(layer_speed.shape, F32),
            pltpu.SemaphoreType.DMA((10,)),
        ],
        compiler_params=params,
        name="prepare",
    )(*(
        pltpu.with_memory_space_constraint(value, pltpu.HBM)
        for value in (
            panels.reshape((per_dev,) + panels.shape[3:]), coupling, table, layer_depth.reshape(1, -1),
            panel_owner.reshape(1, -1), panel_block.reshape(1, -1), layer_speed, u_now, u_prev, lateral,
        )
    ))
    mine = pl.pallas_call(
        mine_kernel,
        out_shape=half,
        in_specs=[vmem] * 2,
        out_specs=vmem,
        scratch_shapes=[pltpu.VMEM((number, HALO, size_z), F32)],
        compiler_params=params,
        name="mine",
    )(fields_own, ints)
    both = jnp.stack([mine, swap(theirs)])
    ints, fields_own, both = lax.optimization_barrier((ints, fields_own, both))
    side = send(both, sizes, route_y)
    ints_o, fields_o = swap(ints), swap(fields_own)
    index = pl.pallas_call(
        functools.partial(
            index_kernel, sizes=u_now.shape[1:], block=coupling.shape[1], panels=npanels
        ),
        out_shape=(
            jax.ShapeDtypeStruct((2, 2 * npanels, size_z), F32),
            jax.ShapeDtypeStruct((2, size_x * rows, 2 * npanels), BF16),
        ),
        in_specs=[vmem] * 2,
        out_specs=(vmem,) * 2,
        compiler_params=params,
        name="index",
    )(ints, ints_o)
    sets = ()
    if ny == 4:
        forces = both[:, tiles // 2:]
        far = send(forces, sizes, lambda i, j, k: (i, j ^ 2 if k == 0 else 3 - j, k))
        side = jnp.concatenate([side, far], axis=1)
    else:
        pair = jnp.stack([ints[0:per_dev], ints_o[0:per_dev]])
        pair = jnp.where(lax.axis_index("gz") == 0, pair, pair[::-1])
        sets = (jnp.moveaxis(lax.all_gather(pair, "gy"), 0, 1).reshape(2, npanels, -1),)
    side, index, ints_o, fields_o = lax.optimization_barrier((side, index, ints_o, fields_o))
    shared = (fields_own, fields_o, ints, ints_o, *index, side, swap(side)) + sets
    shared_specs = [vmem] * (8 + len(sets))
    tiles_scratch = pltpu.VMEM((2, number, HALO, size_z), F32)
    far_scratch = pltpu.VMEM((2, number - tiles, HALO, size_z), F32)
    all_scratch = pltpu.VMEM((2, npanels, width), F32)
    planes = NSTEP * comps
    face_scratch = pltpu.VMEM((2 * face_tiles(comps), HALO, size_z), F32)
    sent = pl.pallas_call(
        face_kernel,
        out_shape=jax.ShapeDtypeStruct(coded_shape(2 * face_tiles(comps)), jnp.int16),
        in_specs=shared_specs,
        out_specs=vmem,
        scratch_shapes=[all_scratch, tiles_scratch, tiles_scratch, far_scratch, far_scratch, face_scratch],
        compiler_params=params,
        name="face",
    )(*shared)
    recv = send(sent, sizes, route_x)
    final, before, face, ratef = pl.pallas_call(
        local_kernel,
        out_shape=(
            jax.ShapeDtypeStruct(u_now.shape, F32),
            jax.ShapeDtypeStruct(u_now.shape, F32),
            jax.ShapeDtypeStruct((2, 2, planes, rows, size_z), F32),
            jax.ShapeDtypeStruct((2, 2, NSTEP, rows, size_z), F32),
        ),
        in_specs=shared_specs,
        out_specs=(vmem,) * 4,
        scratch_shapes=[
            all_scratch,
            tiles_scratch,
            tiles_scratch,
            far_scratch,
            far_scratch,
            pltpu.VMEM((2, comps, size_x + 2, rows, size_z), F32),
            pltpu.VMEM((2, comps, size_x + 2, rows, size_z), F32),
            pltpu.VMEM((2, size_x, rows, size_z), F32),
            pltpu.VMEM((NSTEP, 2, comps, size_x, rows, size_z), F32),
        ],
        compiler_params=params,
        name="local",
    )(*shared)
    final, before, face, ratef, recv = lax.optimization_barrier((final, before, face, ratef, recv))
    recv_o = swap(recv)
    edges = [jax.ShapeDtypeStruct((comps, depth, size_y, size_z), F32) for depth in (NSTEP, NSTEP - 1)]
    whole = (final, before, face, ratef)
    near = pl.pallas_call(
        near_kernel,
        out_shape=tuple(edges),
        in_specs=[vmem] * 5,
        out_specs=(vmem, vmem),
        scratch_shapes=[face_scratch],
        compiler_params=params,
        name="near",
    )(*whole, recv)
    near, recv_o = lax.optimization_barrier((near, recv_o))
    return pl.pallas_call(
        far_kernel,
        out_shape=(
            jax.ShapeDtypeStruct(u_now.shape, F32),
            jax.ShapeDtypeStruct(u_now.shape, F32),
        ),
        in_specs=[vmem] * 7,
        out_specs=(pl.BlockSpec(memory_space=pl.ANY),) * 2,
        scratch_shapes=[
            face_scratch,
            pltpu.VMEM(edges[0].shape, F32),
            pltpu.VMEM(edges[1].shape, F32),
            pltpu.SemaphoreType.DMA((6,)),
        ],
        compiler_params=params,
        name="far",
    )(*whole, recv_o, *near)


def solution(mesh):
    in_specs = (
        P(None, "gx", "gy", "gz"),
        P(None, "gx", "gy", "gz"),
        P("gx", "gz", "gy", None, None),
        P("gx", "gz", None, None),
        P("gx", "gz", None),
        P(),
        P("gz"),
        P(),
        P("gx", "gy", "gz"),
    )
    out_specs = (P(None, "gx", "gy", "gz"), P(None, "gx", "gy", "gz"))
    return jax.shard_map(
        per_device, mesh=mesh, in_specs=in_specs, out_specs=out_specs, check_vma=False
    )
```

```python
import functools

import jax
import jax.numpy as jnp
import ml_dtypes
import numpy as np
from jax import lax
from jax.experimental import pallas as pl
from jax.experimental.pallas import tpu as pltpu
from jax.sharding import PartitionSpec as P

NSTEP = 4
HALO = 8
LANES = 128
PANELS = 16
TOP = 32000.0
F32 = jnp.float32
BF16 = jnp.bfloat16


def wave_table(count, per_step):
    half = count // 2
    freq = np.float32(2.0 * np.pi) * (np.arange(half, dtype=np.float32) + np.float32(0.5)) / np.float32(count)
    times = np.float32(37.0) + np.arange(NSTEP, dtype=np.float32)
    phase = freq[:, None] * times[None, :]
    table = np.concatenate([np.cos(phase), np.sin(phase)], axis=0) / np.sqrt(np.float32(half))
    wide = np.repeat(table.astype(ml_dtypes.bfloat16), per_step, axis=1)
    return np.pad(wide, ((0, 0), (0, -wide.shape[1] % 128)))


def shift_of(size):
    assert size & (size - 1) == 0
    return size.bit_length() - 1


def iota(shape, dim):
    return lax.broadcasted_iota(jnp.int32, shape, dim)


def spin(value, amount, axis):
    return pltpu.roll(value, amount % value.shape[axis], axis)


def across(z0, z1):
    lanes = z0.shape[-1]
    lane = iota(z0.shape, z0.ndim - 1)
    first, last = lane == 0, lane == lanes - 1
    ax = z0.ndim - 1
    down0, down1 = spin(z0, 1, ax), spin(z1, 1, ax)
    up0, up1 = spin(z0, -1, ax), spin(z1, -1, ax)
    sum0 = jnp.where(first, 0.0, down0) + jnp.where(last, up1, up0)
    sum1 = jnp.where(first, down0, down1) + jnp.where(last, 0.0, up1)
    return sum0, sum1


def inplane(z0, z1):
    ax = z0.ndim - 2
    sum0, sum1 = across(z0, z1)
    sum0 = sum0 + (spin(z0, 1, ax) + spin(z0, -1, ax)) - 6.0 * z0
    sum1 = sum1 + (spin(z1, 1, ax) + spin(z1, -1, ax)) - 6.0 * z1
    return sum0, sum1


def row_scales(exponents):
    return jnp.exp2(exponents) * (1.0 / TOP)


def quantize(load, groups, out_ref, spare=None):
    shape = (HALO, LANES)
    lane = iota(shape, 1)
    peak = jnp.zeros(shape, F32)
    for group in range(max(groups) + 1):
        members = [jnp.abs(load(t)) for t, of in enumerate(groups) if of == group]
        top = functools.reduce(jnp.maximum, members)
        peak = jnp.where(lane == group, jnp.max(top, axis=1, keepdims=True), peak)
    exponents = jnp.ceil(jnp.log2(jnp.maximum(peak, 1e-30)))
    factor = jnp.exp2(-exponents) * TOP
    zero = jnp.zeros(shape, jnp.int32)
    wide = [jnp.broadcast_to(factor[:, g:g + 1], shape) for g in range(max(groups) + 1)]
    parts = [jnp.round(load(t) * wide[of]).astype(jnp.int32) for t, of in enumerate(groups)]
    if spare is None:
        parts += [zero] * (len(groups) % 2) + [exponents.astype(jnp.int32), zero]
    else:
        moved = pltpu.roll(exponents, LANES // 2, 1).astype(jnp.int32)
        parts[spare] = jnp.where(lane < LANES // 2, parts[spare], moved)
    for i in range(out_ref.shape[0]):
        out_ref[i] = jnp.concatenate(parts[2 * i:2 * i + 2], axis=0).astype(jnp.int16)


def coded_shape(number):
    return ((number + 1) // 2 + 1, 2 * HALO, LANES)


def side_groups(comps, size_x, rest):
    near = [x // NSTEP for c in range(comps) for x in range(size_x)]
    return near + [max(near) + 1 + i for i in range(rest)]


def scales_of(coded):
    return row_scales(coded.astype(jnp.int32)[0:HALO].astype(F32))


def expand(load, store, scales, blocks):
    for at, one, two in blocks:
        pair = load(at).astype(jnp.int32).astype(F32)
        store(2 * at, pair[0:HALO] * scales[:, one:one + 1])
        store(2 * at + 1, pair[HALO:] * scales[:, two:two + 1])


def expand_all(ref, tiles_ref, groups):
    def store(t, value):
        tiles_ref[t] = value

    expand(lambda i: ref[i], store, scales_of(ref[ref.shape[0] - 1]), [
        (t // 2, groups[t], groups[t + 1]) for t in range(0, len(groups), 2)
    ])


def expand_sides(ref, tiles_ref, far_ref, first, groups, choose):
    last = len(groups) // 2
    forces = len(groups) - far_ref.shape[1]
    for half in range(2):
        z = first if half == 0 else 1 - first

        def store(t, value):
            tiles_ref[z, t] = value

        def store_far(t, value):
            far_ref[z, t] = value

        scales = pltpu.roll(scales_of(ref[half, last - 1]), LANES // 2, 1)
        for moved, blocks in choose(scales):
            expand(lambda i: ref[half, i], store, moved, blocks)
        if ref.shape[1] > last:
            scales = pltpu.roll(scales_of(ref[half, ref.shape[1] - 1]), LANES // 2, 1)
            expand(lambda i: ref[half, last + i], store_far, scales, [
                ((t - forces) // 2, groups[t], groups[t + 1]) for t in range(forces, len(groups), 2)
            ])


def position():
    return [lax.axis_index(axis) for axis in ("gx", "gy", "gz")] + [lax.axis_size("gx"), lax.axis_size("gy")]


def prepare_kernel(
    panels_hbm, coupling_hbm, table_hbm, depth_hbm, owner_hbm, block_hbm, speed_hbm,
    un_hbm, up_hbm, lat_hbm, out_ref, state_ref, theirs_ref, tiles_ref,
    panels_ref, coupling_ref, table_ref, depth_ref, owner_ref, block_ref, speed_ref, sems,
):
    scal_ref = position()
    comps = un_hbm.shape[0]
    un_ref, up_ref, lat_ref = state_ref.at[0:comps], state_ref.at[comps:2 * comps], state_ref.at[2 * comps]
    pairs = (
        (panels_hbm, panels_ref), (table_hbm, table_ref), (coupling_hbm, coupling_ref),
        (depth_hbm, depth_ref), (owner_hbm, owner_ref), (block_hbm, block_ref), (speed_hbm, speed_ref),
        (un_hbm, un_ref), (up_hbm, up_ref), (lat_hbm, lat_ref),
    )
    copies = [pltpu.make_async_copy(src, dst, sems.at[i]) for i, (src, dst) in enumerate(pairs)]
    for copy in copies:
        copy.start()
    for copy in copies[:7]:
        copy.wait()
    count, rows, spectral = panels_ref.shape
    block = rows // comps
    lanes = table_ref.shape[1]
    free = jnp.dot(
        panels_ref[...].reshape(count * rows, spectral), table_ref[...], preferred_element_type=F32
    )
    weights = coupling_ref[...].reshape(rows, block)
    stacked = jnp.concatenate([weights] * NSTEP + [jnp.zeros((lanes - NSTEP * rows, block), F32)], axis=0)
    pick = ((iota((rows, block), 0) & (block - 1)) == iota((rows, block), 1)).astype(F32)
    spread = lax.dot_general(
        pick, stacked, (((1,), (1,)), ((), ())), precision=lax.Precision.HIGHEST, preferred_element_type=F32
    )
    comp_row = iota((rows, lanes), 0) >> shift_of(block)
    comp_lane = iota((rows, lanes), 1) >> shift_of(block)
    same = comp_lane == comp_row
    for step in range(1, NSTEP):
        same = same | (comp_lane == comp_row + step * comps)
    spread = jnp.where(same, spread, 0.0)
    out_ref[0:count] = jnp.sum(free.reshape(count, rows, lanes) * spread[None], axis=1)
    out_ref[count:] = jnp.zeros((out_ref.shape[0] - count, lanes), F32)
    speed = jnp.zeros(depth_ref.shape, F32)
    for layer in range(speed_ref.shape[0]):
        speed = jnp.where(depth_ref[...] == layer, speed_ref[layer], speed)
    pieces = [speed]
    for ref in (owner_ref, block_ref):
        twice = jnp.concatenate([ref[...], ref[...]], axis=1)
        pieces += [twice[:, i:i + LANES] for i in range(0, twice.shape[1], LANES)]
    for i, piece in enumerate(pieces):
        row, at = count + i * LANES // lanes, i * LANES % lanes
        out_ref[row:row + 1, at:at + LANES] = piece.astype(F32)
    for copy in copies[7:]:
        copy.wait()
    code_side(state_ref, out_ref, 1 - lax.rem(scal_ref[1] + scal_ref[2], 2), tiles_ref, theirs_ref)


def mine_kernel(state_ref, force_ref, mine_ref, tiles_ref):
    scal_ref = position()
    code_side(state_ref, force_ref, lax.rem(scal_ref[1] + scal_ref[2], 2), tiles_ref, mine_ref)


def code_side(state_ref, force_ref, which, tiles_ref, coded_ref):
    un_ref, up_ref, lat_ref = fields(state_ref)
    comps, size_x, size_y, size_z = un_ref.shape
    count, lanes = PANELS, force_ref.shape[1]
    speed = listed(force_ref, LANES, 0)
    sub = iota((size_x, HALO, size_z), 1)

    def fill(side):
        base = 0 if side else size_y - HALO
        rate = lat_ref[:, base:base + HALO, :] * speed[None]
        for c in range(comps):
            now = un_ref[c, :, base:base + HALO, :]
            old = spin(up_ref[c, :, base:base + HALO, :], HALO // 2, 1)
            keep = sub < HALO // 2 if side else sub >= HALO // 2
            row = c if side else HALO - 1 - c
            tile = jnp.where(keep, now, old)
            tile = jnp.where(sub == (HALO - 1 if side else 0), rate[:, row:row + 1, :], tile)
            tiles_ref[c * size_x:(c + 1) * size_x] = tile

    for side in range(2):
        pl.when(which == side)(functools.partial(fill, side))
    for part in range(lanes // size_z):
        for piece in range(count // HALO):
            at = comps * size_x + part * (count // HALO) + piece
            tiles_ref[at] = force_ref[piece * HALO:(piece + 1) * HALO, part * size_z:(part + 1) * size_z]
    groups = side_groups(comps, size_x, tiles_ref.shape[0] - comps * size_x)
    quantize(lambda t: tiles_ref[t], groups, coded_ref, len(groups) - 2)


def listed(ref, panels, which):
    lanes = ref.shape[1]
    width = -(-2 * panels // LANES)
    first, number = ((0, 1), (1, width), (1 + width, width))[which]
    out = []
    for i in range(first, first + number):
        row, at = PANELS + i * LANES // lanes, i * LANES % lanes
        out.append(ref[row:row + 1, at:at + LANES])
    return jnp.concatenate(out, axis=1)


def place_forces(scal_ref, ints_ref, intso_ref, sets, all_ref):
    o, mine = scal_ref[1], scal_ref[2]
    side_ref, sideo_ref, far_ref, faro_ref = sets
    count, lanes = PANELS, ints_ref.shape[1]
    beside, opposite, mirror = o + 1 - 2 * lax.rem(o, 2), lax.rem(o + 2, 4), 3 - o
    size_z = side_ref.shape[-1]
    step = count // HALO
    here = mine == 0

    def spot(j):
        return pl.ds(pl.multiple_of(j * count, count), count)

    for ref, j in (
        (side_ref, jnp.where(here, beside, mirror)),
        (sideo_ref, jnp.where(here, mirror, beside)),
        (far_ref, jnp.where(here, opposite, mirror)),
        (faro_ref, jnp.where(here, mirror, opposite)),
    ):
        first = ref.shape[1] - lanes // size_z * step
        for z in range(2):
            for part in range(lanes // size_z):
                at = first + part * step
                all_ref[z, spot(j), part * size_z:(part + 1) * size_z] = ref[z, at:at + step].reshape(count, size_z)
    all_ref[mine, spot(o), :] = ints_ref[0:count]
    all_ref[1 - mine, spot(o), :] = intso_ref[0:count]
    return all_ref


def index_kernel(ints_ref, intso_ref, at_ref, hit_ref, *, sizes, block, panels):
    scal_ref = position()
    size_x, size_y, size_z = sizes
    rows = size_y + HALO
    for z, ints in ((scal_ref[2], ints_ref), (1 - scal_ref[2], intso_ref)):
        keys, depth = panel_keys(ints, scal_ref[1], panels, rows, size_x, size_y, size_z // block)
        at = (iota((size_z, depth.shape[1]), 0) >> shift_of(block)) == depth
        at_ref[z] = jnp.transpose(at.astype(F32))
        hit = iota((size_x * rows, keys.shape[1]), 0) == keys
        hit_ref[z] = hit.astype(F32).astype(BF16)


def panel_keys(ints_ref, o, panels, rows, size_x, size_y, zblocks):
    owner = listed(ints_ref, panels, 1).astype(jnp.int32)
    block = listed(ints_ref, panels, 2).astype(jnp.int32)
    depth = block & (zblocks - 1)
    y = (block >> shift_of(zblocks)) & (size_y - 1)
    x = block >> (shift_of(zblocks) + shift_of(size_y))
    key = x * rows
    reach = NSTEP - 1
    row = jnp.where(owner == o, y, -1)
    row = jnp.where((owner == o + 1) & (y < reach), y + size_y, row)
    row = jnp.where((owner == o - 1) & (y >= size_y - reach), y + rows - size_y, row)
    return jnp.where(row < 0, -1, key + row), depth


def spread_forces(force, at, block, steps):
    high = force.astype(BF16).astype(F32)
    both = jnp.concatenate([high, force - high], axis=0)
    rows, size_z = at.shape
    lane = iota((rows, size_z), 1) >> shift_of(block)
    base = (
        (iota((size_z, size_z), 0) & (block - 1)) == (iota((size_z, size_z), 1) & (block - 1))
    ).astype(BF16)
    per_tile = size_z // block
    out = []
    for q in range(steps * 3):
        part = both[:, (q // per_tile) * size_z:(q // per_tile + 1) * size_z]
        part = jnp.where(lane == q % per_tile, part, 0.0).astype(BF16)
        wide = jnp.dot(part, base, preferred_element_type=F32)
        out.append((wide * at).astype(BF16))
    return jnp.concatenate(out, axis=1)


def fields(state_ref):
    comps = state_ref.shape[0] // 2
    return state_ref.at[0:comps], state_ref.at[comps:2 * comps], state_ref.at[2 * comps]


def halo_tiles(high, low):
    sub = iota(high.shape, high.ndim - 2)
    upper = sub < HALO // 2
    now = jnp.where(upper, high, low)
    old = spin(jnp.where(upper, low, high), HALO // 2, high.ndim - 2)
    return now, old


def halo_rate(highs, lows):
    sub = iota(highs[0].shape, highs[0].ndim - 2)
    tile = jnp.zeros(highs[0].shape, F32)
    ends = slice(HALO - 1, HALO), slice(0, 1)
    for c in range(3):
        tile = jnp.where(sub == c, highs[c][..., ends[0], :], tile)
        tile = jnp.where(sub == HALO - 1 - c, lows[c][..., ends[1], :], tile)
    return tile


def sides(scal_ref, side_ref, sideo_ref, at):
    o, mine = scal_ref[1], scal_ref[2]
    high = lax.rem(o + mine, 2) == 0
    one, two = side_ref[at], sideo_ref[at]
    upper = jnp.where(o < scal_ref[4] - 1, jnp.where(high, one, two), 0.0)
    lower = jnp.where(o > 0, jnp.where(high, two, one), 0.0)
    return upper, lower


def forces_of(scal_ref, ints_ref, intso_ref, rest, all_ref, scratch):
    if rest:
        return rest[0]
    return place_forces(scal_ref, ints_ref, intso_ref, scratch, all_ref)


def face_kernel(
    state_ref, stateo_ref, ints_ref, intso_ref, at_ref, hit_ref, coded_ref, codedo_ref, *rest,
):
    scal_ref = position()
    *rest, out_ref, all_ref, side_ref, sideo_ref, far_ref, faro_ref, faces_ref = rest
    scratch = side_ref, sideo_ref, far_ref, faro_ref
    (un_ref, up_ref, lat_ref), (uno_ref, upo_ref, lato_ref) = fields(state_ref), fields(stateo_ref)
    comps, size_x, size_y, size_z = un_ref.shape
    rows = size_y + HALO
    tiles = comps * size_x
    a, o, mine = scal_ref[0], scal_ref[1], scal_ref[2]
    high = lax.rem(a + mine, 2) == 0
    skip = jnp.where(high, size_x - NSTEP, 0)

    groups = side_groups(comps, size_x, side_ref.shape[1] - tiles)

    def choose(scales):
        moved = pltpu.roll(scales, lax.rem(LANES - lax.div(skip, NSTEP), LANES), 1)
        near = [first + i for first in range(0, tiles, size_x) for i in range(0, NSTEP, 2)]
        rest = [(t // 2, groups[t], groups[t + 1]) for t in range(tiles, len(groups), 2)]
        return (moved, [(t // 2 + lax.div(skip, 2), groups[t], groups[t + 1]) for t in near]), (scales, rest)

    expand_sides(coded_ref, side_ref, far_ref, mine, groups, choose)
    expand_sides(codedo_ref, sideo_ref, faro_ref, 1 - mine, groups, choose)
    forces = forces_of(scal_ref, ints_ref, intso_ref, rest, all_ref, scratch)
    own = mine == 0
    now, old, rate, drive = {}, {}, {}, {}
    for z in range(2):
        wide = spread_forces(forces[z], at_ref[z], 16, NSTEP - 1)
        first = pl.multiple_of(jnp.where(high, size_x - NSTEP, 0) * rows, 2 * HALO)
        hit = hit_ref[z, pl.ds(first, NSTEP * rows)]
        got = jnp.dot(hit, wide, preferred_element_type=F32)
        got = got.reshape(NSTEP, rows, wide.shape[1])
        for d in range(1, NSTEP):
            for n in range(NSTEP - d):
                for c in range(comps):
                    q = (n * comps + c) * size_z
                    drive[z, n, d, c] = jnp.where(
                        high, got[NSTEP - d, :, q:q + size_z], got[d - 1, :, q:q + size_z]
                    )
        speed = jnp.where(
            own if z == 0 else jnp.logical_not(own),
            listed(ints_ref, LANES, 0),
            listed(intso_ref, LANES, 0),
        )
        near = own if z == 0 else jnp.logical_not(own)
        for d in range(1, NSTEP + 1):
            x = jnp.where(high, size_x - d, d - 1)
            ups, lows = [], []
            for c in range(comps):
                upper, lower = sides(scal_ref, side_ref, sideo_ref, (z, c * size_x + x))
                ups.append(upper)
                lows.append(lower)
                tile_now, tile_old = halo_tiles(upper, lower)
                centre = jnp.where(near, un_ref[c, x], uno_ref[c, x])
                now[z, d, c] = jnp.concatenate([centre, tile_now], axis=0)
                if d < NSTEP:
                    centre = jnp.where(near, up_ref[c, x], upo_ref[c, x])
                    old[z, d, c] = jnp.concatenate([centre, tile_old], axis=0)
            if d < NSTEP:
                centre = jnp.where(near, lat_ref[x], lato_ref[x]) * speed
                rate[z, d] = jnp.concatenate([centre, halo_rate(ups, lows)], axis=0)
    series = {(z, 0, c): now[z, 1, c] for z in range(2) for c in range(comps)}
    for n in range(1, NSTEP):
        later = {}
        for d in range(1, NSTEP - n + 1):
            for c in range(comps):
                sums = inplane(now[0, d, c], now[1, d, c])
                for z in range(2):
                    lap = sums[z] + now[z, d + 1, c]
                    if d > 1:
                        lap = lap + now[z, d - 1, c]
                    later[z, d, c] = (
                        2.0 * now[z, d, c] - old[z, d, c] + rate[z, d] * lap + drive[z, n - 1, d, c]
                    )
        old, now = now, later
        for z in range(2):
            for c in range(comps):
                series[z, n, c] = now[z, 1, c]
    sub = iota((HALO, size_z), 0)
    middle = (sub == HALO // 2 - 1) | (sub == HALO // 2)
    ends = (sub < 2) | (sub >= HALO - 2)
    for z in range(2):
        planes = [series[z, n, c] for n in range(NSTEP) for c in range(comps)] + [rate[z, 1], rate[z, 2]]
        rims = [plane[size_y:rows] for plane in planes]
        tails = [jnp.where(middle, spin(rims[2 * comps + c], HALO // 2, 0), rims[c]) for c in range(comps)]
        tails.append(jnp.where(ends, rims[comps], spin(rims[comps + 1], HALO // 2, 0)))
        tails.append(jnp.where(ends, rims[comps + 2], spin(rims[NSTEP * comps], HALO // 2, 0)))
        base = z * face_tiles(comps)
        for i, plane in enumerate(planes):
            for half in range(2):
                faces_ref[base + 2 * i + half] = plane[half * HALO:(half + 1) * HALO]
        for i, tail in enumerate(tails):
            faces_ref[base + 2 * len(planes) + i] = tail
    quantize(lambda t: faces_ref[t], face_groups(comps), out_ref)


def face_tiles(comps):
    return 2 * (NSTEP * comps + 2) + comps + 2


def face_groups(comps):
    groups = []
    for z in range(2):
        base = z * (NSTEP + 3)
        groups += [base + n for n in range(NSTEP) for _ in range(2 * comps)]
        groups += [base + NSTEP] * 4 + [base + NSTEP + 1] * comps + [base + NSTEP + 2] * 2
    return groups


def face_plane(tiles_ref, z, i, comps):
    count = NSTEP * comps + 2
    base = z * face_tiles(comps)
    tail = base + 2 * count
    parts = [tiles_ref[base + 2 * i], tiles_ref[base + 2 * i + 1]]
    turned = lambda at: spin(tiles_ref[at], HALO // 2, 0)
    if i < comps:
        parts.append(tiles_ref[tail + i])
    elif i < comps + 3:
        at, other = ((tail + comps, False), (tail + comps, True), (tail + comps + 1, False))[i - comps]
        parts.append(turned(at) if other else tiles_ref[at])
    elif 2 * comps <= i < 3 * comps:
        parts.append(turned(tail + i - 2 * comps))
    elif i == NSTEP * comps:
        parts.append(turned(tail + comps + 1))
    else:
        parts.append(jnp.zeros(parts[0].shape, F32))
    return jnp.concatenate(parts, axis=0)


def local_kernel(
    state_ref, stateo_ref, ints_ref, intso_ref, at_ref, hit_ref, coded_ref, codedo_ref, *rest,
):
    scal_ref = position()
    now_ref, old_ref, rate_ref, drive_ref = rest[-4:]
    all_ref, side_ref, sideo_ref, far_ref, faro_ref = rest[-9:-4]
    *rest, final_ref, before_ref, face_ref, ratef_ref = rest[:-9]
    scratch = side_ref, sideo_ref, far_ref, faro_ref
    (un_ref, up_ref, lat_ref), (uno_ref, upo_ref, lato_ref) = fields(state_ref), fields(stateo_ref)
    comps, size_x, size_y, size_z = un_ref.shape
    rows = size_y + HALO
    tiles = comps * size_x
    o, mine = scal_ref[1], scal_ref[2]
    groups = side_groups(comps, size_x, side_ref.shape[1] - comps * size_x)
    choose = lambda scales: (
        (scales, [(t // 2, groups[t], groups[t + 1]) for t in range(0, len(groups), 2)]),
    )
    expand_sides(coded_ref, side_ref, far_ref, mine, groups, choose)
    expand_sides(codedo_ref, sideo_ref, faro_ref, 1 - mine, groups, choose)
    forces = forces_of(scal_ref, ints_ref, intso_ref, rest, all_ref, scratch)
    own = mine == 0
    for z in range(2):
        wide = spread_forces(forces[z], at_ref[z], 16, NSTEP)
        hit = hit_ref[z]
        for n in range(NSTEP):
            span = comps * size_z
            got = jnp.dot(hit, wide[:, n * span:(n + 1) * span], preferred_element_type=F32)
            for c in range(comps):
                drive_ref[n, z, c] = got[:, c * size_z:(c + 1) * size_z].reshape(size_x, rows, size_z)
    edge = jnp.zeros((rows, size_z), F32)
    for z in range(2):
        for c in range(comps):
            for ref in (now_ref, old_ref):
                ref[z, c, 0] = edge
                ref[z, c, size_x + 1] = edge
    for z_at, un, up, lat, ints in (
        (mine, un_ref, up_ref, lat_ref, ints_ref),
        (1 - mine, uno_ref, upo_ref, lato_ref, intso_ref),
    ):
        speed = listed(ints, LANES, 0)
        ups, lows = [], []
        for c in range(comps):
            upper, lower = sides(scal_ref, side_ref, sideo_ref, (z_at, slice(c * size_x, (c + 1) * size_x)))
            ups.append(upper)
            lows.append(lower)
            tile_now, tile_old = halo_tiles(upper, lower)
            now_ref[z_at, c, 1:size_x + 1, 0:size_y] = un[c]
            now_ref[z_at, c, 1:size_x + 1, size_y:rows] = tile_now
            old_ref[z_at, c, 1:size_x + 1, 0:size_y] = up[c]
            old_ref[z_at, c, 1:size_x + 1, size_y:rows] = tile_old
        rate_ref[z_at, :, 0:size_y] = lat[...] * speed[None]
        rate_ref[z_at, :, size_y:rows] = halo_rate(ups, lows)
    for side in range(2):
        for z in range(2):
            for d in range(NSTEP):
                ratef_ref[side, z, d] = rate_ref[z, d if side else size_x - 1 - d]
    refs = [now_ref, old_ref]
    for n in range(NSTEP):
        now, old = refs[n % 2], refs[(n + 1) % 2]
        for side in range(2):
            for z in range(2):
                for c in range(comps):
                    face_ref[side, z, n * comps + c] = now[z, c, 1 if side else size_x]

        def step(x, carry, now=now, old=old, n=n, halves=(0, 1)):
            for c in range(comps):
                centre = now[0, c, x + 1], now[1, c, x + 1]
                sums = inplane(*centre)
                for z in halves:
                    lap = sums[z] + (now[z, c, x] + now[z, c, x + 2])
                    value = (
                        2.0 * centre[z] - old[z, c, x + 1] + rate_ref[z, x] * lap + drive_ref[n, z, c, x]
                    )
                    if len(halves) == 2:
                        old[z, c, x + 1] = value
                    else:
                        final_ref[c, x] = value[0:size_y]
                        before_ref[c, x] = centre[z][0:size_y]
            return carry

        if n < NSTEP - 1:
            lax.fori_loop(0, size_x, step, 0, unroll=size_x)
        else:
            for z in range(2):
                @pl.when(mine == z)
                def _(step=step, z=z):
                    lax.fori_loop(0, size_x, functools.partial(step, halves=(z,)), 0, unroll=size_x)


def corrected(scal_ref, final_in, before_in, face_ref, ratef_ref, coded_ref, recv_ref, high, edges):
    comps, size_x, size_y, size_z = final_in.shape
    a, mine = scal_ref[0], scal_ref[2]
    side = jnp.where(high, 0, 1)
    inside = jnp.where(high, a < scal_ref[3] - 1, a > 0)
    expand_all(coded_ref, recv_ref, face_groups(comps))

    def theirs(z, at):
        return jnp.where(inside, face_plane(recv_ref, z, at, comps), 0.0)

    def correct(own):
        rate = {}
        for z in range(2):
            for m in range(NSTEP):
                rate[z, -m] = ratef_ref[side, z, m]
            for m in (1, 2):
                rate[z, m] = theirs(z, NSTEP * comps + m - 1)
        for c in range(comps):
            last, now = {}, {}
            for n in range(NSTEP):
                later = {}
                for m in range(-n, min(n + 1, NSTEP - 1 - n) + 1):
                    centre = [now.get((z, m)) for z in range(2)]
                    sums = inplane(*centre) if centre[0] is not None else (None, None)
                    for z in range(2) if n < NSTEP - 1 else (own,):
                        terms = [sums[z], now.get((z, m - 1)), now.get((z, m + 1))]
                        if m == 0:
                            terms.append(theirs(z, n * comps + c))
                        if m == 1:
                            terms.append(face_ref[side, z, n * comps + c])
                        value = functools.reduce(lambda p, q: p + q, [t for t in terms if t is not None])
                        value = rate[z, m] * value
                        if centre[z] is not None:
                            value = value + 2.0 * centre[z]
                        if (z, m) in last:
                            value = value - last[z, m]
                        later[z, m] = value
                last, now = now, later
            for values, source, edge in zip((now, last), (final_in, before_in), edges):
                depth = edge.shape[1]
                for m in range(1 - depth, 1):
                    x, at = jnp.where(high, size_x - 1 + m, -m), jnp.where(high, depth - 1 + m, -m)
                    edge[c, at] = source[c, x] + values[own, m][0:size_y]

    for z in range(2):
        pl.when(mine == z)(functools.partial(correct, z))


def near_kernel(
    final_in, before_in, face_ref, ratef_ref, coded_ref, final_edge, before_edge, recv_ref
):
    scal_ref = position()
    high = lax.rem(scal_ref[0] + scal_ref[2], 2) == 0
    edges = final_edge, before_edge
    corrected(scal_ref, final_in, before_in, face_ref, ratef_ref, coded_ref, recv_ref, high, edges)


def far_kernel(
    final_in, before_in, face_ref, ratef_ref, coded_ref, final_near, before_near,
    final_ref, before_ref, recv_ref, final_edge, before_edge, sems,
):
    scal_ref = position()
    size_x = final_in.shape[1]
    high = lax.rem(scal_ref[0] + scal_ref[2], 2) == 1
    copies = []

    def begin(src, target, first, count):
        copies.append(pltpu.make_async_copy(src, target.at[:, pl.ds(first, count)], sems.at[len(copies)]))
        copies[-1].start()

    outputs = ((final_in, final_near, final_ref, final_edge), (before_in, before_near, before_ref, before_edge))
    for source, near, target, edge in outputs:
        depth = edge.shape[1]
        begin(near, target, jnp.where(high, 0, size_x - depth), depth)
        begin(source.at[:, pl.ds(depth, size_x - 2 * depth)], target, depth, size_x - 2 * depth)
    edges = final_edge, before_edge
    corrected(scal_ref, final_in, before_in, face_ref, ratef_ref, coded_ref, recv_ref, high, edges)
    for source, near, target, edge in outputs:
        depth = edge.shape[1]
        begin(edge, target, jnp.where(high, size_x - depth, 0), depth)
    for copy in copies:
        copy.wait()


def send(value, mesh_sizes, route):
    nx, ny, nz = mesh_sizes
    number = lambda i, j, k: (i * ny + j) * nz + k
    pairs = [
        (number(i, j, k), number(*route(i, j, k))) for i in range(nx) for j in range(ny) for k in range(nz)
    ]
    return lax.ppermute(value, ("gx", "gy", "gz"), pairs)


def partner(i, core, count):
    step = 1 if (i + core) % 2 == 0 else -1
    return (i + step) % count


def per_device(
    u_now, u_prev, panels, panel_owner, panel_block, coupling, layer_depth, layer_speed, lateral
):
    sizes = tuple(lax.axis_size(axis) for axis in ("gx", "gy", "gz"))
    nx, ny, nz = sizes
    assert nx % 2 == 0 and ny % 2 == 0 and nz == 2
    comps, size_x, size_y, size_z = u_now.shape
    rows = size_y + HALO
    per_dev, spectral = panels.shape[2], panels.shape[4]
    npanels = ny * per_dev

    def swap(value):
        return send(value, sizes, lambda i, j, k: (i, j, 1 - k))

    def route_x(i, j, k):
        return partner(i, k, nx), j, k

    def route_y(i, j, k):
        to = partner(j, k, ny)
        if abs(to - j) != 1 or (ny == 2 and k == 1):
            return i ^ 1, j, k
        return i, to, k

    assert per_dev == PANELS and size_z == LANES
    vmem = pl.BlockSpec(memory_space=pltpu.VMEM)
    params = pltpu.CompilerParams(vmem_limit_bytes=48 * 1024 * 1024)
    table = jnp.asarray(wave_table(spectral, panels.shape[3]))
    width = table.shape[1]
    extra_rows = -(-(LANES + 4 * npanels) // (8 * width)) * 8
    tiles = comps * size_x
    number = tiles + width // size_z * (per_dev // HALO)
    assert number - tiles == 4 and NSTEP * panels.shape[3] + LANES // 2 <= width
    half = jax.ShapeDtypeStruct((number // 2, 2 * HALO, LANES), jnp.int16)
    ints, fields_own, theirs = pl.pallas_call(
        prepare_kernel,
        out_shape=(
            jax.ShapeDtypeStruct((per_dev + extra_rows, width), F32),
            jax.ShapeDtypeStruct((2 * comps + 1,) + u_now.shape[1:], F32),
            half,
        ),
        in_specs=[pl.BlockSpec(memory_space=pl.ANY)] * 10,
        out_specs=(vmem,) * 3,
        scratch_shapes=[
            pltpu.VMEM((number, HALO, size_z), F32),
            pltpu.VMEM((per_dev,) + panels.shape[3:], BF16),
            pltpu.VMEM(coupling.shape, F32),
            pltpu.VMEM(table.shape, BF16),
            pltpu.VMEM((1, size_z), jnp.int32),
            pltpu.VMEM((1, npanels), jnp.int32),
            pltpu.VMEM((1, npanels), jnp.int32),
            pltpu.SMEM(layer_speed.shape, F32),
            pltpu.SemaphoreType.DMA((10,)),
        ],
        compiler_params=params,
        name="prepare",
    )(*(
        pltpu.with_memory_space_constraint(value, pltpu.HBM)
        for value in (
            panels.reshape((per_dev,) + panels.shape[3:]), coupling, table, layer_depth.reshape(1, -1),
            panel_owner.reshape(1, -1), panel_block.reshape(1, -1), layer_speed, u_now, u_prev, lateral,
        )
    ))
    mine = pl.pallas_call(
        mine_kernel,
        out_shape=half,
        in_specs=[vmem] * 2,
        out_specs=vmem,
        scratch_shapes=[pltpu.VMEM((number, HALO, size_z), F32)],
        compiler_params=params,
        name="mine",
    )(fields_own, ints)
    both = jnp.stack([mine, swap(theirs)])
    ints, fields_own, both = lax.optimization_barrier((ints, fields_own, both))
    side = send(both, sizes, route_y)
    ints_o, fields_o = swap(ints), swap(fields_own)
    index = pl.pallas_call(
        functools.partial(
            index_kernel, sizes=u_now.shape[1:], block=coupling.shape[1], panels=npanels
        ),
        out_shape=(
            jax.ShapeDtypeStruct((2, 2 * npanels, size_z), F32),
            jax.ShapeDtypeStruct((2, size_x * rows, 2 * npanels), BF16),
        ),
        in_specs=[vmem] * 2,
        out_specs=(vmem,) * 2,
        compiler_params=params,
        name="index",
    )(ints, ints_o)
    sets = ()
    if ny == 4:
        forces = both[:, tiles // 2:]
        far = send(forces, sizes, lambda i, j, k: (i, j ^ 2 if k == 0 else 3 - j, k))
        side = jnp.concatenate([side, far], axis=1)
    else:
        pair = jnp.stack([ints[0:per_dev], ints_o[0:per_dev]])
        pair = jnp.where(lax.axis_index("gz") == 0, pair, pair[::-1])
        sets = (jnp.moveaxis(lax.all_gather(pair, "gy"), 0, 1).reshape(2, npanels, -1),)
    side, index, ints_o, fields_o = lax.optimization_barrier((side, index, ints_o, fields_o))
    shared = (fields_own, fields_o, ints, ints_o, *index, side, swap(side)) + sets
    shared_specs = [vmem] * (8 + len(sets))
    tiles_scratch = pltpu.VMEM((2, number, HALO, size_z), F32)
    far_scratch = pltpu.VMEM((2, number - tiles, HALO, size_z), F32)
    all_scratch = pltpu.VMEM((2, npanels, width), F32)
    planes = NSTEP * comps
    face_scratch = pltpu.VMEM((2 * face_tiles(comps), HALO, size_z), F32)
    sent = pl.pallas_call(
        face_kernel,
        out_shape=jax.ShapeDtypeStruct(coded_shape(2 * face_tiles(comps)), jnp.int16),
        in_specs=shared_specs,
        out_specs=vmem,
        scratch_shapes=[all_scratch, tiles_scratch, tiles_scratch, far_scratch, far_scratch, face_scratch],
        compiler_params=params,
        name="face",
    )(*shared)
    recv = send(sent, sizes, route_x)
    final, before, face, ratef = pl.pallas_call(
        local_kernel,
        out_shape=(
            jax.ShapeDtypeStruct(u_now.shape, F32),
            jax.ShapeDtypeStruct(u_now.shape, F32),
            jax.ShapeDtypeStruct((2, 2, planes, rows, size_z), F32),
            jax.ShapeDtypeStruct((2, 2, NSTEP, rows, size_z), F32),
        ),
        in_specs=shared_specs,
        out_specs=(vmem,) * 4,
        scratch_shapes=[
            all_scratch,
            tiles_scratch,
            tiles_scratch,
            far_scratch,
            far_scratch,
            pltpu.VMEM((2, comps, size_x + 2, rows, size_z), F32),
            pltpu.VMEM((2, comps, size_x + 2, rows, size_z), F32),
            pltpu.VMEM((2, size_x, rows, size_z), F32),
            pltpu.VMEM((NSTEP, 2, comps, size_x, rows, size_z), F32),
        ],
        compiler_params=params,
        name="local",
    )(*shared)
    final, before, face, ratef, recv = lax.optimization_barrier((final, before, face, ratef, recv))
    recv_o = swap(recv)
    edges = [jax.ShapeDtypeStruct((comps, depth, size_y, size_z), F32) for depth in (NSTEP, NSTEP - 1)]
    whole = (final, before, face, ratef)
    near = pl.pallas_call(
        near_kernel,
        out_shape=tuple(edges),
        in_specs=[vmem] * 5,
        out_specs=(vmem, vmem),
        scratch_shapes=[face_scratch],
        compiler_params=params,
        name="near",
    )(*whole, recv)
    near, recv_o = lax.optimization_barrier((near, recv_o))
    return pl.pallas_call(
        far_kernel,
        out_shape=(
            jax.ShapeDtypeStruct(u_now.shape, F32),
            jax.ShapeDtypeStruct(u_now.shape, F32),
        ),
        in_specs=[vmem] * 7,
        out_specs=(pl.BlockSpec(memory_space=pl.ANY),) * 2,
        scratch_shapes=[
            face_scratch,
            pltpu.VMEM(edges[0].shape, F32),
            pltpu.VMEM(edges[1].shape, F32),
            pltpu.SemaphoreType.DMA((6,)),
        ],
        compiler_params=params,
        name="far",
    )(*whole, recv_o, *near)


def solution(mesh):
    in_specs = (
        P(None, "gx", "gy", "gz"),
        P(None, "gx", "gy", "gz"),
        P("gx", "gz", "gy", None, None),
        P("gx", "gz", None, None),
        P("gx", "gz", None),
        P(),
        P("gz"),
        P(),
        P("gx", "gy", "gz"),
    )
    out_specs = (P(None, "gx", "gy", "gz"), P(None, "gx", "gy", "gz"))
    return jax.shard_map(
        per_device, mesh=mesh, in_specs=in_specs, out_specs=out_specs, check_vma=False
    )
```
